32 devices in a mesh: phi: 16 (over z, y, x), row: 2 (over core).
Axes of the slice: x: 2, y: 2, z: 4, core: 2. Of those that a mesh axis runs over, the one named last changes fastest.
Arguments:
- magnetogram: bfloat16 [4096, 1024], P('phi', 'row'), may hold values from -6 to 6
- col_owner: int32 [4096], P('phi'), may hold values from 0 to 15, as said below
- col_offset: int32 [4096], P('phi'), may hold values from 0 to 31, as said below
- phi_weight: bfloat16 [512, 768], P(None, 'phi'), may hold values from -0.375 to 0.375
- theta_weight: bfloat16 [1024, 128], P('row'), may hold values from -0.1875 to 0.1875
- radial_coef: float32 [8], replicated, may hold values from 0.3 to 3
- theta_coef: float32 [128], replicated, may hold values from 0.3 to 3
- phi_coef: float32 [768], replicated, may hold values from 0.3 to 3
- start_field: float32 [8, 768, 128], P('row', 'phi'), may hold values from -0.3125 to 0.3125
Outputs:
- solution_field: float32 [8, 768, 128], P('row', 'phi')
- residual: float32 [8, 768, 128], P('row', 'phi')
The draws below stay inside these ranges and needn't reach their ends.
Inputs may be any that keep to these rules, and one draw needn't show every extreme that they name: `col_owner`: within each aligned block of 256 columns (the columns of one index of phi) at most 32 columns share an owner, and one owner receives exactly 32 columns from every block. `col_offset`: columns of one aligned block of 256 columns that share an owner have distinct offsets.
All inputs are finite; a program needn't handle non-finite values.
Results may differ from the reference program's by a relative error of at most 0.019.
Values may be sent and summed in bfloat16 or wider, within the bound.
No kernel may reach another device: no remote copies, remote signals or barrier semaphores. Data moves between devices by JAX's collectives and lax.ppermute only.
A program may use at most 64 MiB of HBM per device.

```python
import math
import jax
import jax.numpy as jnp
from jax import lax

CP = 48
NT = 128
MCOL_DEV = 256
ITERS = 2
NR = 8
NP = 768
MT = 1024
MAGC = 4096
SLOTS = 512
CAP = 32


def slot_table(key):
    sources = MAGC // MCOL_DEV
    base = jax.random.fold_in(key, 7)
    hot = jax.random.randint(jax.random.fold_in(base, 1), (), 0, sources)

    def one_source(source):
        source_key = jax.random.fold_in(base, source + 11)
        others = jax.random.permutation(jax.random.fold_in(source_key, 1), SLOTS - CAP)[:MCOL_DEV - CAP]
        others = jnp.where(others >= hot * CAP, others + CAP, others)
        hots = hot * CAP + jnp.arange(CAP, dtype=jnp.int32)
        chosen = jnp.concatenate([hots, others.astype(jnp.int32)])
        return jax.random.permutation(jax.random.fold_in(source_key, 2), chosen)
    return jax.vmap(one_source)(jnp.arange(sources, dtype=jnp.int32)).reshape(-1).astype(jnp.int32)


def draw_col_owner(key, part):
    return (slot_table(key) // CAP).astype(jnp.int32)


def draw_col_offset(key, part):
    return (slot_table(key) % CAP).astype(jnp.int32)


def draw_start_field(key, part):
    radial_ramp = 1.0 + 2.0 * jnp.arange(NR, dtype=jnp.float32) / max(NR - 1, 1)
    phi_ramp = 1.0 + 2.0 * jnp.arange(NP, dtype=jnp.float32) / max(NP - 1, 1)
    rough = jnp.clip(jax.random.normal(key, (NR, NP, NT), jnp.float32), -4.0, 4.0)
    return (0.005 * rough * radial_ramp[:, None, None] * phi_ramp[None, :, None]).astype(jnp.float32)


def block_levels(rng, dims, shards, smallest, top_value):
    gain = 1.0
    for dim, parts in shards:
        draws = jax.random.uniform(jax.random.fold_in(jax.random.fold_in(rng, 6), dim), (parts,), jnp.float32, smallest / len(shards), top_value / len(shards))
        gain = gain * jnp.repeat(jnp.exp(draws), dims[dim] // parts).reshape((-1,) + (1,) * (len(dims) - 1 - dim))
    return gain


def centred(own_key, dims, spread, most, shards=(), kind=jnp.bfloat16):
    array = spread * jax.random.normal(own_key, dims, jnp.float32)
    if shards:
        array = array * block_levels(own_key, dims, shards, -0.22, 0.18)
    return jnp.clip(array, -most, most).astype(kind)


def setup_inputs(seed: int = 0) -> dict:
    key_list = jax.random.split(jax.random.key(seed), 10)
    magnetogram = centred(key_list[0], (MAGC, MT), 1.0, 6.0, ((0, 16), (1, 2)))
    col_owner = draw_col_owner(jax.random.fold_in(key_list[9], 71), 0)
    col_offset = draw_col_offset(jax.random.fold_in(key_list[9], 71), 0)
    phi_weight = centred(key_list[3], (SLOTS, NP), MCOL_DEV ** -0.5, 0.375, ((1, 16),))
    theta_weight = centred(key_list[4], (MT, NT), MT ** -0.5, 0.1875, ((0, 2),))
    radial_coef = jnp.clip(jnp.exp(jax.random.uniform(key_list[5], (NR,), jnp.float32, math.log(0.3), math.log(3.0))), 0.3, 3.0)
    theta_coef = jnp.clip(jnp.exp(jax.random.uniform(key_list[6], (NT,), jnp.float32, math.log(0.3), math.log(3.0))), 0.3, 3.0)
    phi_coef = jnp.clip(jnp.exp(jax.random.uniform(key_list[7], (NP,), jnp.float32, math.log(0.3), math.log(3.0))), 0.3, 3.0)
    start_field = draw_start_field(jax.random.fold_in(key_list[9], 71), 0)
    return {"magnetogram": magnetogram, "col_owner": col_owner, "col_offset": col_offset, "phi_weight": phi_weight, "theta_weight": theta_weight, "radial_coef": radial_coef, "theta_coef": theta_coef, "phi_coef": phi_coef, "start_field": start_field}


def face_coefs(radial_coef, theta_coef, phi_coef):
    radial_mid = 0.5 * (radial_coef[:-1] + radial_coef[1:])
    radial_upper = jnp.concatenate([radial_mid, radial_coef[-1:]])
    radial_lower = jnp.concatenate([radial_coef[:1], radial_mid])
    theta_mid = 0.5 * (theta_coef[:-1] + theta_coef[1:])
    zero_one = jnp.zeros((1,), jnp.float32)
    theta_upper = jnp.concatenate([theta_mid, zero_one])
    theta_lower = jnp.concatenate([zero_one, theta_mid])
    phi_upper = 0.5 * (phi_coef + jnp.roll(phi_coef, -1))
    phi_lower = jnp.roll(phi_upper, 1)
    return radial_upper, radial_lower, theta_upper, theta_lower, phi_upper, phi_lower


def apply_operator(field, coefs):
    radial_upper, radial_lower, theta_upper, theta_lower, phi_upper, phi_lower = coefs
    radial_pad = jnp.pad(field, ((1, 1), (0, 0), (0, 0)))
    theta_pad = jnp.pad(field, ((0, 0), (0, 0), (1, 1)))
    phi_next = jnp.roll(field, -1, axis=1)
    phi_prev = jnp.roll(field, 1, axis=1)
    result = radial_upper[:, None, None] * (field - radial_pad[2:])
    result = result + radial_lower[:, None, None] * (field - radial_pad[:-2])
    result = result + theta_upper[None, None, :] * (field - theta_pad[:, :, 2:])
    result = result + theta_lower[None, None, :] * (field - theta_pad[:, :, :-2])
    result = result + phi_upper[None, :, None] * (field - phi_next)
    result = result + phi_lower[None, :, None] * (field - phi_prev)
    return result


def reference(magnetogram, col_owner, col_offset, phi_weight, theta_weight, radial_coef, theta_coef, phi_coef, start_field):
    columns = jnp.dot(magnetogram, theta_weight, preferred_element_type=jnp.float32)
    sources = MAGC // MCOL_DEV
    slot_index = ((jnp.arange(MAGC, dtype=jnp.int32) // MCOL_DEV) * CAP + col_offset).astype(jnp.int32)

    def add_block(total, block_index):
        start = (block_index * MCOL_DEV).astype(jnp.int32)
        block_cols = lax.dynamic_slice_in_dim(columns, start, MCOL_DEV, 0)
        owners = lax.dynamic_slice_in_dim(col_owner, start, MCOL_DEV, 0).astype(jnp.int32)
        slots = lax.dynamic_slice_in_dim(slot_index, start, MCOL_DEV, 0).astype(jnp.int32)
        weight_rows = phi_weight[slots].reshape(MCOL_DEV, sources, CP)
        chosen = jnp.take_along_axis(weight_rows, owners[:, None, None], axis=1)[:, 0, :].astype(jnp.float32)
        contrib = chosen[:, :, None] * block_cols[:, None, :]
        return total + jax.ops.segment_sum(contrib, owners, num_segments=sources), None

    init = jnp.zeros((sources, CP, NT), jnp.float32)
    total, unused = lax.scan(add_block, init, jnp.arange(sources, dtype=jnp.int32))
    boundary = total.reshape(NP, NT)
    coefs = face_coefs(radial_coef, theta_coef, phi_coef)
    diag = (coefs[0][:, None, None] + coefs[1][:, None, None] + coefs[2][None, None, :]
            + coefs[3][None, None, :] + coefs[4][None, :, None] + coefs[5][None, :, None])
    inv_diag = 1.0 / diag
    right_side = jnp.concatenate([(coefs[1][0] * boundary)[None], jnp.zeros((NR - 1, NP, NT), jnp.float32)], axis=0)
    solution_field = start_field
    residual = right_side - apply_operator(start_field, coefs)
    precond = residual * inv_diag
    direction = precond
    norm_now = jnp.sum(residual * precond)
    for sweep_index in range(ITERS):
        image = apply_operator(direction, coefs)
        alpha = norm_now / jnp.sum(direction * image)
        solution_field = solution_field + alpha * direction
        residual = residual - alpha * image
        if sweep_index + 1 < ITERS:
            precond = residual * inv_diag
            norm_next = jnp.sum(residual * precond)
            direction = precond + (norm_next / norm_now) * direction
            norm_now = norm_next
    return solution_field, residual
```

```python
import jax
import jax.numpy as jnp
from jax import lax
from jax.sharding import PartitionSpec as P

REACH = 3


def face_coefs(radial_coef, theta_coef, phi_coef):
    radial_mid = 0.5 * (radial_coef[:-1] + radial_coef[1:])
    radial_upper = jnp.concatenate([radial_mid, radial_coef[-1:]])
    radial_lower = jnp.concatenate([radial_coef[:1], radial_mid])
    theta_mid = 0.5 * (theta_coef[:-1] + theta_coef[1:])
    zero_one = jnp.zeros((1,), jnp.float32)
    theta_upper = jnp.concatenate([theta_mid, zero_one])
    theta_lower = jnp.concatenate([zero_one, theta_mid])
    phi_upper = 0.5 * (phi_coef + jnp.roll(phi_coef, -1))
    phi_lower = jnp.roll(phi_upper, 1)
    return (radial_upper, radial_lower, theta_upper, theta_lower, phi_upper, phi_lower)


def row_sum(value, rows):
    if rows == 2:
        return value + lax.ppermute(value, "row", [(0, 1), (1, 0)])
    return lax.psum(value, "row")


def pick(chunks, index):
    return lax.dynamic_index_in_dim(chunks, index, 0, keepdims=False)


def step_sizes(a, b, c, e):
    alpha = a / b
    beta = (alpha * alpha * c - a) / a
    gain = 1.0 + beta
    curvature = gain * gain * b - 2.0 * gain * alpha * c + alpha * alpha * e
    return alpha, gain, beta * a / curvature


def body(
    magnetogram,
    col_owner,
    col_offset,
    phi_weight,
    theta_weight,
    radial_coef,
    theta_coef,
    phi_coef,
    start_field,
):
    layers, cells, width = start_field.shape
    phi_devices = lax.axis_size("phi")
    rows = lax.axis_size("row")
    slots = phi_weight.shape[0]
    capacity = slots // phi_devices
    per = capacity // rows
    here = lax.axis_index("phi")
    row = lax.axis_index("row")
    above = lax.rem(here + 1, phi_devices)
    below = lax.rem(here + phi_devices - 1, phi_devices)

    climb = [(i, i + 1) for i in range(rows - 1)]
    low_layers = lax.ppermute(start_field[layers - REACH :], "row", climb)
    high_layers = lax.ppermute(start_field[:REACH], "row", [(t, s) for s, t in climb])
    window = jnp.concatenate([low_layers, start_field, high_layers], axis=0)

    columns = jnp.dot(magnetogram, theta_weight, preferred_element_type=jnp.float32)
    columns = row_sum(columns, rows)
    upper_part = lax.optimization_barrier(columns.astype(jnp.bfloat16))
    lower_part = (columns - upper_part.astype(jnp.float32)).astype(jnp.bfloat16)

    place = col_offset - row * per
    target = jnp.where((place >= 0) & (place < per), col_owner * per + place, -1)
    chosen = (target[None, :] == jnp.arange(phi_devices * per, dtype=jnp.int32)[:, None]).astype(
        jnp.bfloat16
    )
    packed = jnp.dot(chosen, upper_part, preferred_element_type=jnp.float32)
    packed = packed + jnp.dot(chosen, lower_part, preferred_element_type=jnp.float32)
    packed = packed.reshape(phi_devices, per, width)
    share = phi_weight.reshape(phi_devices, rows, per, cells)
    share = lax.dynamic_index_in_dim(share, row, 1, keepdims=False)
    share = share.reshape(phi_devices * per, cells)

    def edge(start):
        field = window[:, start : start + REACH].reshape(-1, width)
        lo = start + 1 if start else 0
        weights = share[:, lo : lo + 2].astype(jnp.float32).T.reshape(-1, width)
        return jnp.concatenate([field, weights], axis=0)

    to_above, to_below = edge(cells - REACH), edge(0)
    who = jnp.arange(phi_devices, dtype=jnp.int32)[:, None, None]
    edges = jnp.where(who == above, to_above[None], jnp.where(who == below, to_below[None], 0.0))
    sent = jnp.concatenate(
        [packed, jnp.roll(packed, 1, axis=0), jnp.roll(packed, -1, axis=0), edges], axis=1
    )
    got = lax.all_to_all(sent, "phi", split_axis=0, concat_axis=0, tiled=True)
    edge_low, edge_high = pick(got, below)[3 * per :], pick(got, above)[3 * per :]
    reach_rows = window.shape[0] * REACH

    def weigh(weights, which):
        data = got[:, which * per : (which + 1) * per].reshape(phi_devices * per, width)
        part = lax.optimization_barrier(data.astype(jnp.bfloat16))
        rest = (data - part.astype(jnp.float32)).astype(jnp.bfloat16)
        total = jnp.dot(weights, part, preferred_element_type=jnp.float32)
        return total + jnp.dot(weights, rest, preferred_element_type=jnp.float32)

    def ghost_weights(edge_rows):
        return edge_rows[reach_rows:].reshape(2, phi_devices * per).astype(jnp.bfloat16)

    boundary = row_sum(
        jnp.concatenate(
            [
                weigh(ghost_weights(edge_low), 1),
                weigh(share.T, 0),
                weigh(ghost_weights(edge_high), 2),
            ],
            axis=0,
        ),
        rows,
    )
    field = jnp.concatenate(
        [
            edge_low[:reach_rows].reshape(-1, REACH, width),
            window,
            edge_high[:reach_rows].reshape(-1, REACH, width),
        ],
        axis=1,
    )

    faces = face_coefs(radial_coef, theta_coef, phi_coef)
    spread = layers + 2 * REACH

    def radial_window(coef):
        padded = jnp.pad(coef, (REACH, REACH))
        return lax.dynamic_slice_in_dim(padded, row * layers, spread)[:, None, None]

    def phi_window(coef):
        padded = jnp.concatenate([coef[-REACH:], coef, coef[:REACH]])
        return lax.dynamic_slice_in_dim(padded, here * cells, cells + 2 * REACH)[None, :, None]

    rad_upper, rad_lower = radial_window(faces[0]), radial_window(faces[1])
    lon_upper, lon_lower = phi_window(faces[4]), phi_window(faces[5])
    lat_upper, lat_lower = faces[2][None, None, :], faces[3][None, None, :]
    inside = radial_window(jnp.ones_like(radial_coef))
    inv_diag = inside / (
        rad_upper + rad_lower + lat_upper + lat_lower + lon_upper + lon_lower + (1.0 - inside)
    )

    def apply_operator(value, depth):
        mid = value[1:-1, 1:-1]
        theta_pad = jnp.pad(mid, ((0, 0), (0, 0), (1, 1)))
        result = rad_upper[depth:-depth] * (mid - value[2:, 1:-1])
        result = result + rad_lower[depth:-depth] * (mid - value[:-2, 1:-1])
        result = result + lat_upper * (mid - theta_pad[:, :, 2:])
        result = result + lat_lower * (mid - theta_pad[:, :, :-2])
        result = result + lon_upper[:, depth:-depth] * (mid - value[1:-1, 2:])
        return result + lon_lower[:, depth:-depth] * (mid - value[1:-1, :-2])

    def inner(value, by):
        return value[by:-by, by:-by] if by else value

    level = row * layers - REACH + 1 + jnp.arange(spread - 2, dtype=jnp.int32)[:, None, None]
    source = jnp.where(level == 0, (faces[1][0] * boundary)[None], 0.0)
    residual = source - apply_operator(field, 1)
    first = residual * inner(inv_diag, 1)
    first_image = apply_operator(first, 2)
    second = first_image * inner(inv_diag, 2)
    second_image = apply_operator(second, 3)
    residual, first = inner(residual, 2), inner(first, 2)
    first_image, second = inner(first_image, 1), inner(second, 1)

    pairs = (
        (residual, first),
        (first, first_image),
        (first_image, second),
        (second, second_image),
    )
    sums = jnp.stack([jnp.sum(u * v, axis=(0, 1)) for u, v in pairs] * 2)
    devices = phi_devices * rows
    if devices <= 64:
        shared = jnp.broadcast_to(sums[None], (devices,) + sums.shape)
        shared = lax.all_to_all(shared, ("phi", "row"), split_axis=0, concat_axis=0, tiled=True)
        totals = jnp.sum(shared, axis=(0, 2))
    else:
        totals = lax.psum(jnp.sum(sums, axis=1), ("phi", "row"))
    alpha, gain, alpha_next = step_sizes(totals[0], totals[1], totals[2], totals[3])
    direction = gain * first - alpha * second
    solution_field = start_field + alpha * first + alpha_next * direction
    image = gain * first_image - alpha * second_image
    return solution_field, residual - alpha * first_image - alpha_next * image


def solution(mesh):
    in_specs = (
        P("phi", "row"),
        P("phi"),
        P("phi"),
        P(None, "phi"),
        P("row", None),
        P(),
        P(),
        P(),
        P("row", "phi", None),
    )
    out_specs = (P("row", "phi", None), P("row", "phi", None))
    return jax.shard_map(body, mesh=mesh, in_specs=in_specs, out_specs=out_specs, check_vma=False)
```

```python
import jax
import jax.numpy as jnp
from jax import lax
from jax.experimental import pallas as pl
from jax.experimental.pallas import tpu as pltpu
from jax.sharding import PartitionSpec as P

REACH = 3


def face_coefs(radial_coef, theta_coef, phi_coef):
    radial_mid = 0.5 * (radial_coef[:-1] + radial_coef[1:])
    radial_upper = jnp.concatenate([radial_mid, radial_coef[-1:]])
    radial_lower = jnp.concatenate([radial_coef[:1], radial_mid])
    theta_mid = 0.5 * (theta_coef[:-1] + theta_coef[1:])
    zero_one = jnp.zeros((1,), jnp.float32)
    theta_upper = jnp.concatenate([theta_mid, zero_one])
    theta_lower = jnp.concatenate([zero_one, theta_mid])
    phi_upper = 0.5 * (phi_coef + jnp.roll(phi_coef, -1))
    phi_lower = jnp.roll(phi_upper, 1)
    return (radial_upper, radial_lower, theta_upper, theta_lower, phi_upper, phi_lower)


def row_sum(value, rows):
    if rows == 2:
        return value + lax.ppermute(value, "row", [(0, 1), (1, 0)])
    return lax.psum(value, "row")


def pick(chunks, index):
    return lax.dynamic_index_in_dim(chunks, index, 0, keepdims=False)


def step_sizes(a, b, c, e):
    alpha = a / b
    beta = (alpha * alpha * c - a) / a
    gain = 1.0 + beta
    curvature = gain * gain * b - 2.0 * gain * alpha * c + alpha * alpha * e
    return alpha, gain, beta * a / curvature


def general_body(
    magnetogram,
    col_owner,
    col_offset,
    phi_weight,
    theta_weight,
    radial_coef,
    theta_coef,
    phi_coef,
    start_field,
):
    layers, cells, width = start_field.shape
    phi_devices = lax.axis_size("phi")
    rows = lax.axis_size("row")
    slots = phi_weight.shape[0]
    capacity = slots // phi_devices
    per = capacity // rows
    here = lax.axis_index("phi")
    row = lax.axis_index("row")
    above = lax.rem(here + 1, phi_devices)
    below = lax.rem(here + phi_devices - 1, phi_devices)

    climb = [(i, i + 1) for i in range(rows - 1)]
    low_layers = lax.ppermute(start_field[layers - REACH :], "row", climb)
    high_layers = lax.ppermute(start_field[:REACH], "row", [(t, s) for s, t in climb])
    window = jnp.concatenate([low_layers, start_field, high_layers], axis=0)

    columns = jnp.dot(magnetogram, theta_weight, preferred_element_type=jnp.float32)
    columns = row_sum(columns, rows)
    upper_part = lax.optimization_barrier(columns.astype(jnp.bfloat16))
    lower_part = (columns - upper_part.astype(jnp.float32)).astype(jnp.bfloat16)

    place = col_offset - row * per
    target = jnp.where((place >= 0) & (place < per), col_owner * per + place, -1)
    chosen = (target[None, :] == jnp.arange(phi_devices * per, dtype=jnp.int32)[:, None]).astype(
        jnp.bfloat16
    )
    packed = jnp.dot(chosen, upper_part, preferred_element_type=jnp.float32)
    packed = packed + jnp.dot(chosen, lower_part, preferred_element_type=jnp.float32)
    packed = packed.reshape(phi_devices, per, width)
    share = phi_weight.reshape(phi_devices, rows, per, cells)
    share = lax.dynamic_index_in_dim(share, row, 1, keepdims=False)
    share = share.reshape(phi_devices * per, cells)

    def edge(start):
        field = window[:, start : start + REACH].reshape(-1, width)
        lo = start + 1 if start else 0
        weights = share[:, lo : lo + 2].astype(jnp.float32).T.reshape(-1, width)
        return jnp.concatenate([field, weights], axis=0)

    to_above, to_below = edge(cells - REACH), edge(0)
    who = jnp.arange(phi_devices, dtype=jnp.int32)[:, None, None]
    edges = jnp.where(who == above, to_above[None], jnp.where(who == below, to_below[None], 0.0))
    sent = jnp.concatenate(
        [packed, jnp.roll(packed, 1, axis=0), jnp.roll(packed, -1, axis=0), edges], axis=1
    )
    got = lax.all_to_all(sent, "phi", split_axis=0, concat_axis=0, tiled=True)
    edge_low, edge_high = pick(got, below)[3 * per :], pick(got, above)[3 * per :]
    reach_rows = window.shape[0] * REACH

    def weigh(weights, which):
        data = got[:, which * per : (which + 1) * per].reshape(phi_devices * per, width)
        part = lax.optimization_barrier(data.astype(jnp.bfloat16))
        rest = (data - part.astype(jnp.float32)).astype(jnp.bfloat16)
        total = jnp.dot(weights, part, preferred_element_type=jnp.float32)
        return total + jnp.dot(weights, rest, preferred_element_type=jnp.float32)

    def ghost_weights(edge_rows):
        return edge_rows[reach_rows:].reshape(2, phi_devices * per).astype(jnp.bfloat16)

    boundary = row_sum(
        jnp.concatenate(
            [
                weigh(ghost_weights(edge_low), 1),
                weigh(share.T, 0),
                weigh(ghost_weights(edge_high), 2),
            ],
            axis=0,
        ),
        rows,
    )
    field = jnp.concatenate(
        [
            edge_low[:reach_rows].reshape(-1, REACH, width),
            window,
            edge_high[:reach_rows].reshape(-1, REACH, width),
        ],
        axis=1,
    )

    faces = face_coefs(radial_coef, theta_coef, phi_coef)
    spread = layers + 2 * REACH

    def radial_window(coef):
        padded = jnp.pad(coef, (REACH, REACH))
        return lax.dynamic_slice_in_dim(padded, row * layers, spread)[:, None, None]

    def phi_window(coef):
        padded = jnp.concatenate([coef[-REACH:], coef, coef[:REACH]])
        return lax.dynamic_slice_in_dim(padded, here * cells, cells + 2 * REACH)[None, :, None]

    rad_upper, rad_lower = radial_window(faces[0]), radial_window(faces[1])
    lon_upper, lon_lower = phi_window(faces[4]), phi_window(faces[5])
    lat_upper, lat_lower = faces[2][None, None, :], faces[3][None, None, :]
    inside = radial_window(jnp.ones_like(radial_coef))
    inv_diag = inside / (
        rad_upper + rad_lower + lat_upper + lat_lower + lon_upper + lon_lower + (1.0 - inside)
    )

    def apply_operator(value, depth):
        mid = value[1:-1, 1:-1]
        theta_pad = jnp.pad(mid, ((0, 0), (0, 0), (1, 1)))
        result = rad_upper[depth:-depth] * (mid - value[2:, 1:-1])
        result = result + rad_lower[depth:-depth] * (mid - value[:-2, 1:-1])
        result = result + lat_upper * (mid - theta_pad[:, :, 2:])
        result = result + lat_lower * (mid - theta_pad[:, :, :-2])
        result = result + lon_upper[:, depth:-depth] * (mid - value[1:-1, 2:])
        return result + lon_lower[:, depth:-depth] * (mid - value[1:-1, :-2])

    def inner(value, by):
        return value[by:-by, by:-by] if by else value

    level = row * layers - REACH + 1 + jnp.arange(spread - 2, dtype=jnp.int32)[:, None, None]
    source = jnp.where(level == 0, (faces[1][0] * boundary)[None], 0.0)
    residual = source - apply_operator(field, 1)
    first = residual * inner(inv_diag, 1)
    first_image = apply_operator(first, 2)
    second = first_image * inner(inv_diag, 2)
    second_image = apply_operator(second, 3)
    residual, first = inner(residual, 2), inner(first, 2)
    first_image, second = inner(first_image, 1), inner(second, 1)

    pairs = (
        (residual, first),
        (first, first_image),
        (first_image, second),
        (second, second_image),
    )
    sums = jnp.stack([jnp.sum(u * v, axis=(0, 1)) for u, v in pairs] * 2)
    devices = phi_devices * rows
    if devices <= 64:
        shared = jnp.broadcast_to(sums[None], (devices,) + sums.shape)
        shared = lax.all_to_all(shared, ("phi", "row"), split_axis=0, concat_axis=0, tiled=True)
        totals = jnp.sum(shared, axis=(0, 2))
    else:
        totals = lax.psum(jnp.sum(sums, axis=1), ("phi", "row"))
    alpha, gain, alpha_next = step_sizes(totals[0], totals[1], totals[2], totals[3])
    direction = gain * first - alpha * second
    solution_field = start_field + alpha * first + alpha_next * direction
    image = gain * first_image - alpha * second_image
    return solution_field, residual - alpha * first_image - alpha_next * image


def high_low(value):
    high = value.astype(jnp.bfloat16)
    return high, (value - high.astype(jnp.float32)).astype(jnp.bfloat16)


def radial_face(radial_ref, layers, face):
    if isinstance(face, int):
        low, high = max(face - 1, 0), min(face, layers - 1)
    else:
        low, high = jnp.maximum(face - 1, 0), jnp.minimum(face, layers - 1)
    return 0.5 * (radial_ref[low] + radial_ref[high])


def own_share(phi_ref, per):
    row = lax.axis_index("row")
    share = phi_ref[:, pl.ds(pl.multiple_of(row * per, per), per), :]
    return share.reshape(-1, share.shape[-1])


def column_kernel(mag_ref, theta_ref, out_ref):
    out_ref[...] = jnp.dot(mag_ref[...], theta_ref[...], preferred_element_type=jnp.float32)


def pack_kernel(mine_ref, other_ref, owner_ref, offset_ref, phi_ref, field_ref, out_ref, edge_ref):
    devices = out_ref.shape[0]
    layers, cells, width = field_ref.shape
    per = phi_ref.shape[1] // 2
    count = devices * per
    here = lax.axis_index("phi")
    high, low = high_low(mine_ref[...] + other_ref[...])
    place = offset_ref[...] - lax.axis_index("row") * per
    target = jnp.where((place >= 0) & (place < per), owner_ref[...] * per + place, -1)
    slot = lax.broadcasted_iota(jnp.int32, (count, target.shape[1]), 0)
    chosen = jnp.where(slot == target, 1.0, 0.0).astype(jnp.bfloat16)
    packed = jnp.dot(
        chosen, jnp.concatenate([high, low], axis=1), preferred_element_type=jnp.float32
    ).astype(jnp.bfloat16)
    high = packed[:, :width].reshape(devices, per, width)
    low = packed[:, width:].reshape(devices, per, width)
    out_ref[:, :per] = high
    out_ref[:, per : 2 * per] = low
    for to in range(devices):
        out_ref[to, 2 * per : 3 * per] = high[(to - 1) % devices]
        out_ref[to, 3 * per : 4 * per] = high[(to + 1) % devices]
    out_ref[:, 4 * per :] = jnp.zeros((devices, 32, width), jnp.bfloat16)
    cell = lax.broadcasted_iota(jnp.int32, (8, cells), 1)
    which = lax.broadcasted_iota(jnp.int32, (8, cells), 0)
    picked = jnp.where(which < 2, which, cells - 4 + which)
    picker = jnp.where((cell == picked) & (which < 4), 1.0, 0.0).astype(jnp.bfloat16)
    weights = lax.dot_general(
        picker,
        own_share(phi_ref, per),
        (((1,), (1,)), ((), ())),
        preferred_element_type=jnp.float32,
    )
    for side in range(2):
        start = 0 if side else cells - REACH
        first = 0 if side else 2
        for layer in range(layers):
            edge_ref[side, layer * REACH : (layer + 1) * REACH] = field_ref[
                layer, start : start + REACH
            ]
        for part in range(count // width):
            at = layers * REACH + 2 * part
            edge_ref[side, at : at + 2] = weights[
                first : first + 2, part * width : (part + 1) * width
            ]
        high, low = high_low(edge_ref[side])
        to = lax.rem(here + (devices - 1 if side else 1), devices)
        out_ref[to, 4 * per : 4 * per + 16] = high
        out_ref[to, 4 * per + 16 :] = low


def coef_kernel(radial_ref, theta_ref, phi_ref, weight_ref, inv_ref, lon_ref, lat_ref, share_ref):
    layers, spread, width = inv_ref.shape
    cells = share_ref.shape[0]
    per = weight_ref.shape[1] // 2
    chunks = phi_ref.shape[0]
    total = chunks * width
    share_ref[...] = own_share(weight_ref, per).astype(jnp.float32).T.astype(jnp.bfloat16)
    row = lax.broadcasted_iota(jnp.int32, (spread, width), 0)
    lane = lax.broadcasted_iota(jnp.int32, (spread, width), 1)
    cell = lax.axis_index("phi") * cells + jnp.where(row < cells + 4, row, row - spread)
    cell = jnp.where(cell < 0, cell + total, jnp.where(cell >= total, cell - total, cell))
    found = jnp.zeros((spread, width), jnp.float32)
    for chunk in range(chunks):
        found = found + jnp.where(lane + chunk * width == cell, phi_ref[chunk : chunk + 1], 0.0)
    column = jnp.broadcast_to(jnp.sum(found, axis=1, keepdims=True), (spread, width))
    upper = 0.5 * (column + pltpu.roll(column, spread - 1, 0))
    lower = pltpu.roll(upper, 1, 0)
    lon_ref[...] = upper
    theta = jnp.broadcast_to(theta_ref[...], (8, width))
    end = lax.broadcasted_iota(jnp.int32, (8, width), 1) == width - 1
    lat_upper = jnp.where(end, 0.0, 0.5 * (theta + pltpu.roll(theta, width - 1, 1)))
    lat_ref[...] = lat_upper
    flat = upper + lower + (lat_upper + pltpu.roll(lat_upper, 1, 1))[:1]
    for layer in range(layers):
        low, high = (radial_face(radial_ref, layers, layer + k) for k in range(2))
        inv_ref[layer] = 1.0 / (flat + (low + high))


def boundary_kernel(got_ref, share_ref, out_ref):
    devices, _, width = got_ref.shape
    cells, count = share_ref.shape
    per = count // devices
    spread = cells + 8
    layers = (out_ref.shape[0] - spread) // 8
    here = lax.axis_index("phi")
    below = lax.rem(here + devices - 1, devices)
    above = lax.rem(here + 1, devices)

    def rows(which):
        return got_ref[:, which * per : (which + 1) * per].reshape(count, width)

    own = jnp.dot(
        share_ref[...],
        jnp.concatenate([rows(0), rows(1)], axis=1),
        preferred_element_type=jnp.float32,
    )
    out_ref[:cells] = own[:, :width] + own[:, width:]
    out_ref[cells:] = jnp.zeros((out_ref.shape[0] - cells, width), jnp.float32)
    for side, source in enumerate((above, below)):
        high = got_ref[source, 4 * per : 4 * per + 16].astype(jnp.float32)
        edge = high + got_ref[source, 4 * per + 16 :].astype(jnp.float32)
        at = layers * REACH
        weights = jnp.concatenate(
            [high[at + 2 * k : at + 2 * k + 2] for k in range(count // width)], axis=1
        )
        weights = jnp.concatenate([weights, jnp.zeros((6, count), jnp.float32)], axis=0)
        ghost = jnp.dot(
            weights.astype(jnp.bfloat16), rows(2 if side else 3), preferred_element_type=jnp.float32
        )
        at = spread - 2 if side else cells
        out_ref[at : at + 2] = ghost[:2]
        for layer in range(layers):
            at = spread + layer * 8 + (8 - REACH if side else 0)
            out_ref[at : at + REACH] = edge[layer * REACH : (layer + 1) * REACH]


def krylov_kernel(
    radial_ref,
    mine_ref,
    other_ref,
    field_ref,
    far_ref,
    inv_ref,
    lon_ref,
    lat_ref,
    sums_ref,
    residual_ref,
    first_ref,
    image_ref,
    second_ref,
    image2_ref,
    x_ref,
    u_ref,
    v_ref,
    r_ref,
    w_ref,
):
    layers, cells, width = field_ref.shape
    every, spread, _ = inv_ref.shape
    row = lax.axis_index("row")
    lon, lat = lon_ref[...], lat_ref[:1]
    nothing = jnp.zeros((spread, width), jnp.float32)
    for ref in (x_ref, u_ref, v_ref):
        ref[0] = nothing
        ref[every + 1] = nothing
    for ref, edge, base in (
        (field_ref, mine_ref, row * layers),
        (far_ref, other_ref, (1 - row) * layers),
    ):
        for layer in range(layers):
            x_ref[base + layer + 1, :cells] = ref[layer]
            x_ref[base + layer + 1, cells:] = edge[spread + 8 * layer : spread + 8 * layer + 8]

    def operate(ref, start, count):
        mid = ref[start + 1]
        below = radial_face(radial_ref, every, start) * (mid - ref[start])
        for step in range(count):
            layer = start + step
            ahead = ref[layer + 2]
            rise = radial_face(radial_ref, every, layer + 1) * (ahead - mid)
            along = lon * (mid - pltpu.roll(mid, spread - 1, 0))
            across = lat * (mid - pltpu.roll(mid, width - 1, 1))
            yield (
                layer,
                step,
                (below - rise)
                + (along - pltpu.roll(along, 1, 0))
                + (across - pltpu.roll(across, 1, 1)),
            )
            mid, below = ahead, rise

    inflow = radial_face(radial_ref, every, 0) * (mine_ref[:spread] + other_ref[:spread])
    for layer, _, value in operate(x_ref, row * (layers - 2), layers + 2):
        residual = jnp.where(layer == 0, inflow, 0.0) - value
        r_ref[layer] = residual
        u_ref[layer + 1] = residual * inv_ref[layer]
    for layer, _, value in operate(u_ref, row * (layers - 1), layers + 1):
        w_ref[layer] = value
        v_ref[layer + 1] = value * inv_ref[layer]

    totals = [jnp.zeros((8, width), jnp.float32)] * 4
    for layer, step, value in operate(v_ref, row * layers, layers):
        residual, first = r_ref[layer, :cells], u_ref[layer + 1, :cells]
        image, second = w_ref[layer, :cells], v_ref[layer + 1, :cells]
        image2 = value[:cells]
        residual_ref[step] = residual
        first_ref[step] = first
        image_ref[step] = image
        second_ref[step] = second
        image2_ref[step] = image2
        pairs = ((residual, first), (first, image), (image, second), (second, image2))
        for which, (left, right) in enumerate(pairs):
            product = left * right
            for at in range(0, cells, 8):
                totals[which] = totals[which] + product[at : at + 8]
    lane = lax.broadcasted_iota(jnp.int32, (8, width), 1)
    packed = jnp.zeros((8, width), jnp.float32)
    for which, total in enumerate(totals):
        packed = jnp.where(lane == which, jnp.sum(total, axis=1, keepdims=True), packed)
    sums_ref[...] = jnp.broadcast_to(jnp.sum(packed, axis=0, keepdims=True), sums_ref.shape)


def update_kernel(
    sums_ref,
    field_ref,
    residual_ref,
    first_ref,
    image_ref,
    second_ref,
    image2_ref,
    out_ref,
    left_ref,
):
    totals = jnp.sum(sums_ref[...], axis=0, keepdims=True)
    lane = lax.broadcasted_iota(jnp.int32, totals.shape, 1)
    a, b, c, e = (
        jnp.sum(jnp.where(lane == which, totals, 0.0), axis=1, keepdims=True) for which in range(4)
    )
    alpha, gain, alpha_next = step_sizes(a, b, c, e)
    along, back = alpha + alpha_next * gain, alpha_next * alpha
    for layer in range(field_ref.shape[0]):
        out_ref[layer] = field_ref[layer] + (along * first_ref[layer] - back * second_ref[layer])
        left_ref[layer] = residual_ref[layer] - (along * image_ref[layer] - back * image2_ref[layer])


def in_vmem(count):
    return [pl.BlockSpec(memory_space=pltpu.VMEM)] * count


def paired_body(
    magnetogram,
    col_owner,
    col_offset,
    phi_weight,
    theta_weight,
    radial_coef,
    theta_coef,
    phi_coef,
    start_field,
):
    layers, cells, width = start_field.shape
    phi_devices = lax.axis_size("phi")
    slots = phi_weight.shape[0]
    capacity = slots // phi_devices
    per = capacity // 2
    count = phi_devices * per
    columns = magnetogram.shape[0]
    every, spread = 2 * layers, cells + 8
    real, half = jnp.float32, jnp.bfloat16
    struct = jax.ShapeDtypeStruct
    in_smem = [pl.BlockSpec(memory_space=pltpu.SMEM)]

    def swap(value):
        return lax.ppermute(value, "row", [(0, 1), (1, 0)])

    weights = phi_weight.reshape(phi_devices, capacity, cells)
    mine = pl.pallas_call(
        column_kernel,
        out_shape=struct((columns, width), real),
        in_specs=in_vmem(2),
        out_specs=in_vmem(1)[0],
    )(magnetogram, theta_weight)
    sent = pl.pallas_call(
        pack_kernel,
        out_shape=struct((phi_devices, 4 * per + 32, width), half),
        in_specs=in_vmem(6),
        out_specs=in_vmem(1)[0],
        scratch_shapes=[pltpu.VMEM((2, 16, width), real)],
    )(
        mine,
        swap(mine),
        col_owner.reshape(1, -1),
        col_offset.reshape(1, -1),
        weights,
        start_field,
    )
    sent, radial_coef, theta_coef, phi_coef, field = lax.optimization_barrier(
        (sent, radial_coef, theta_coef, phi_coef, start_field)
    )
    got = lax.all_to_all(sent, "phi", split_axis=0, concat_axis=0, tiled=True)
    far = swap(field)
    inv_diag, lon, lat, share = pl.pallas_call(
        coef_kernel,
        out_shape=[
            struct((every, spread, width), real),
            struct((spread, width), real),
            struct((8, width), real),
            struct((cells, count), half),
        ],
        in_specs=in_smem + in_vmem(3),
        out_specs=in_vmem(4),
    )(radial_coef, theta_coef.reshape(1, width), phi_coef.reshape(-1, width), weights)
    part = pl.pallas_call(
        boundary_kernel,
        out_shape=struct((spread + 8 * layers, width), real),
        in_specs=in_vmem(2),
        out_specs=in_vmem(1)[0],
    )(got, share)
    block = struct((layers, cells, width), real)
    lines = pltpu.VMEM((every + 2, spread, width), real)
    sums, *vectors = pl.pallas_call(
        krylov_kernel,
        out_shape=[struct((2 * phi_devices, width), real)] + [block] * 5,
        in_specs=in_smem + in_vmem(7),
        out_specs=in_vmem(6),
        scratch_shapes=[lines] * 5,
    )(radial_coef, part, swap(part), field, far, inv_diag, lon, lat)
    sums = lax.all_to_all(sums, ("phi", "row"), split_axis=0, concat_axis=0, tiled=True)
    return pl.pallas_call(
        update_kernel,
        out_shape=[block] * 2,
        in_specs=in_vmem(7),
        out_specs=in_vmem(2),
    )(sums, field, *vectors)


def body(*args):
    phi_weight, phi_coef, start_field = args[3], args[7], args[8]
    layers, cells, width = start_field.shape
    phi_devices = lax.axis_size("phi")
    per = phi_weight.shape[0] // phi_devices // 2
    edge_rows = layers * REACH + 2 * phi_devices * per // width
    fits = (
        lax.axis_size("row") == 2
        and phi_devices > 2
        and per % 16 == 0
        and layers >= 2
        and cells % 8 == 0
        and width % 128 == 0
        and phi_devices * per % width == 0
        and phi_coef.shape[0] % width == 0
        and edge_rows <= 16
    )
    return (paired_body if fits else general_body)(*args)


def solution(mesh):
    in_specs = (
        P("phi", "row"),
        P("phi"),
        P("phi"),
        P(None, "phi"),
        P("row", None),
        P(),
        P(),
        P(),
        P("row", "phi", None),
    )
    out_specs = (P("row", "phi", None), P("row", "phi", None))
    return jax.shard_map(body, mesh=mesh, in_specs=in_specs, out_specs=out_specs, check_vma=False)
```

```python
import jax
import jax.numpy as jnp
from jax import lax
from jax.experimental import pallas as pl
from jax.experimental.pallas import tpu as pltpu
from jax.sharding import PartitionSpec as P

REACH = 3


def face_coefs(radial_coef, theta_coef, phi_coef):
    radial_mid = 0.5 * (radial_coef[:-1] + radial_coef[1:])
    radial_upper = jnp.concatenate([radial_mid, radial_coef[-1:]])
    radial_lower = jnp.concatenate([radial_coef[:1], radial_mid])
    theta_mid = 0.5 * (theta_coef[:-1] + theta_coef[1:])
    zero_one = jnp.zeros((1,), jnp.float32)
    theta_upper = jnp.concatenate([theta_mid, zero_one])
    theta_lower = jnp.concatenate([zero_one, theta_mid])
    phi_upper = 0.5 * (phi_coef + jnp.roll(phi_coef, -1))
    phi_lower = jnp.roll(phi_upper, 1)
    return (radial_upper, radial_lower, theta_upper, theta_lower, phi_upper, phi_lower)


def row_sum(value, rows):
    if rows == 2:
        return value + lax.ppermute(value, "row", [(0, 1), (1, 0)])
    return lax.psum(value, "row")


def pick(chunks, index):
    return lax.dynamic_index_in_dim(chunks, index, 0, keepdims=False)


def step_sizes(a, b, c, e):
    alpha = a / b
    beta = (alpha * alpha * c - a) / a
    gain = 1.0 + beta
    curvature = gain * gain * b - 2.0 * gain * alpha * c + alpha * alpha * e
    return alpha, gain, beta * a / curvature


def general_body(
    magnetogram,
    col_owner,
    col_offset,
    phi_weight,
    theta_weight,
    radial_coef,
    theta_coef,
    phi_coef,
    start_field,
):
    layers, cells, width = start_field.shape
    phi_devices = lax.axis_size("phi")
    rows = lax.axis_size("row")
    slots = phi_weight.shape[0]
    capacity = slots // phi_devices
    per = capacity // rows
    here = lax.axis_index("phi")
    row = lax.axis_index("row")
    above = lax.rem(here + 1, phi_devices)
    below = lax.rem(here + phi_devices - 1, phi_devices)

    climb = [(i, i + 1) for i in range(rows - 1)]
    low_layers = lax.ppermute(start_field[layers - REACH :], "row", climb)
    high_layers = lax.ppermute(start_field[:REACH], "row", [(t, s) for s, t in climb])
    window = jnp.concatenate([low_layers, start_field, high_layers], axis=0)

    columns = jnp.dot(magnetogram, theta_weight, preferred_element_type=jnp.float32)
    columns = row_sum(columns, rows)
    upper_part = lax.optimization_barrier(columns.astype(jnp.bfloat16))
    lower_part = (columns - upper_part.astype(jnp.float32)).astype(jnp.bfloat16)

    place = col_offset - row * per
    target = jnp.where((place >= 0) & (place < per), col_owner * per + place, -1)
    chosen = (target[None, :] == jnp.arange(phi_devices * per, dtype=jnp.int32)[:, None]).astype(
        jnp.bfloat16
    )
    packed = jnp.dot(chosen, upper_part, preferred_element_type=jnp.float32)
    packed = packed + jnp.dot(chosen, lower_part, preferred_element_type=jnp.float32)
    packed = packed.reshape(phi_devices, per, width)
    share = phi_weight.reshape(phi_devices, rows, per, cells)
    share = lax.dynamic_index_in_dim(share, row, 1, keepdims=False)
    share = share.reshape(phi_devices * per, cells)

    def edge(start):
        field = window[:, start : start + REACH].reshape(-1, width)
        lo = start + 1 if start else 0
        weights = share[:, lo : lo + 2].astype(jnp.float32).T.reshape(-1, width)
        return jnp.concatenate([field, weights], axis=0)

    to_above, to_below = edge(cells - REACH), edge(0)
    who = jnp.arange(phi_devices, dtype=jnp.int32)[:, None, None]
    edges = jnp.where(who == above, to_above[None], jnp.where(who == below, to_below[None], 0.0))
    sent = jnp.concatenate(
        [packed, jnp.roll(packed, 1, axis=0), jnp.roll(packed, -1, axis=0), edges], axis=1
    )
    got = lax.all_to_all(sent, "phi", split_axis=0, concat_axis=0, tiled=True)
    edge_low, edge_high = pick(got, below)[3 * per :], pick(got, above)[3 * per :]
    reach_rows = window.shape[0] * REACH

    def weigh(weights, which):
        data = got[:, which * per : (which + 1) * per].reshape(phi_devices * per, width)
        part = lax.optimization_barrier(data.astype(jnp.bfloat16))
        rest = (data - part.astype(jnp.float32)).astype(jnp.bfloat16)
        total = jnp.dot(weights, part, preferred_element_type=jnp.float32)
        return total + jnp.dot(weights, rest, preferred_element_type=jnp.float32)

    def ghost_weights(edge_rows):
        return edge_rows[reach_rows:].reshape(2, phi_devices * per).astype(jnp.bfloat16)

    boundary = row_sum(
        jnp.concatenate(
            [
                weigh(ghost_weights(edge_low), 1),
                weigh(share.T, 0),
                weigh(ghost_weights(edge_high), 2),
            ],
            axis=0,
        ),
        rows,
    )
    field = jnp.concatenate(
        [
            edge_low[:reach_rows].reshape(-1, REACH, width),
            window,
            edge_high[:reach_rows].reshape(-1, REACH, width),
        ],
        axis=1,
    )

    faces = face_coefs(radial_coef, theta_coef, phi_coef)
    spread = layers + 2 * REACH

    def radial_window(coef):
        padded = jnp.pad(coef, (REACH, REACH))
        return lax.dynamic_slice_in_dim(padded, row * layers, spread)[:, None, None]

    def phi_window(coef):
        padded = jnp.concatenate([coef[-REACH:], coef, coef[:REACH]])
        return lax.dynamic_slice_in_dim(padded, here * cells, cells + 2 * REACH)[None, :, None]

    rad_upper, rad_lower = radial_window(faces[0]), radial_window(faces[1])
    lon_upper, lon_lower = phi_window(faces[4]), phi_window(faces[5])
    lat_upper, lat_lower = faces[2][None, None, :], faces[3][None, None, :]
    inside = radial_window(jnp.ones_like(radial_coef))
    inv_diag = inside / (
        rad_upper + rad_lower + lat_upper + lat_lower + lon_upper + lon_lower + (1.0 - inside)
    )

    def apply_operator(value, depth):
        mid = value[1:-1, 1:-1]
        theta_pad = jnp.pad(mid, ((0, 0), (0, 0), (1, 1)))
        result = rad_upper[depth:-depth] * (mid - value[2:, 1:-1])
        result = result + rad_lower[depth:-depth] * (mid - value[:-2, 1:-1])
        result = result + lat_upper * (mid - theta_pad[:, :, 2:])
        result = result + lat_lower * (mid - theta_pad[:, :, :-2])
        result = result + lon_upper[:, depth:-depth] * (mid - value[1:-1, 2:])
        return result + lon_lower[:, depth:-depth] * (mid - value[1:-1, :-2])

    def inner(value, by):
        return value[by:-by, by:-by] if by else value

    level = row * layers - REACH + 1 + jnp.arange(spread - 2, dtype=jnp.int32)[:, None, None]
    source = jnp.where(level == 0, (faces[1][0] * boundary)[None], 0.0)
    residual = source - apply_operator(field, 1)
    first = residual * inner(inv_diag, 1)
    first_image = apply_operator(first, 2)
    second = first_image * inner(inv_diag, 2)
    second_image = apply_operator(second, 3)
    residual, first = inner(residual, 2), inner(first, 2)
    first_image, second = inner(first_image, 1), inner(second, 1)

    pairs = (
        (residual, first),
        (first, first_image),
        (first_image, second),
        (second, second_image),
    )
    sums = jnp.stack([jnp.sum(u * v, axis=(0, 1)) for u, v in pairs] * 2)
    devices = phi_devices * rows
    if devices <= 64:
        shared = jnp.broadcast_to(sums[None], (devices,) + sums.shape)
        shared = lax.all_to_all(shared, ("phi", "row"), split_axis=0, concat_axis=0, tiled=True)
        totals = jnp.sum(shared, axis=(0, 2))
    else:
        totals = lax.psum(jnp.sum(sums, axis=1), ("phi", "row"))
    alpha, gain, alpha_next = step_sizes(totals[0], totals[1], totals[2], totals[3])
    direction = gain * first - alpha * second
    solution_field = start_field + alpha * first + alpha_next * direction
    image = gain * first_image - alpha * second_image
    return solution_field, residual - alpha * first_image - alpha_next * image


def high_low(value):
    high = value.astype(jnp.bfloat16)
    return high, (value - high.astype(jnp.float32)).astype(jnp.bfloat16)


def radial_face(radial_ref, layers, face):
    if isinstance(face, int):
        low, high = max(face - 1, 0), min(face, layers - 1)
    else:
        low, high = jnp.maximum(face - 1, 0), jnp.minimum(face, layers - 1)
    return 0.5 * (radial_ref[low] + radial_ref[high])


def own_share(phi_ref, per):
    row = lax.axis_index("row")
    share = phi_ref[:, pl.ds(pl.multiple_of(row * per, per), per), :]
    return share.reshape(-1, share.shape[-1])


def column_kernel(mag_ref, theta_ref, out_ref):
    out_ref[...] = jnp.dot(mag_ref[...], theta_ref[...], preferred_element_type=jnp.float32)


def pack_kernel(mine_ref, other_ref, owner_ref, offset_ref, phi_ref, field_ref, out_ref, edge_ref):
    devices = out_ref.shape[0]
    layers, cells, width = field_ref.shape
    per = phi_ref.shape[1] // 2
    count = devices * per
    here = lax.axis_index("phi")
    high, low = high_low(mine_ref[...] + other_ref[...])
    place = offset_ref[...] - lax.axis_index("row") * per
    target = jnp.where((place >= 0) & (place < per), owner_ref[...] * per + place, -1)
    slot = lax.broadcasted_iota(jnp.int32, (count, target.shape[1]), 0)
    chosen = jnp.where(slot == target, 1.0, 0.0).astype(jnp.bfloat16)
    packed = jnp.dot(
        chosen, jnp.concatenate([high, low], axis=1), preferred_element_type=jnp.float32
    ).astype(jnp.bfloat16)
    high = packed[:, :width].reshape(devices, per, width)
    low = packed[:, width:].reshape(devices, per, width)
    out_ref[:, :per] = high
    out_ref[:, per : 2 * per] = low
    for to in range(devices):
        out_ref[to, 2 * per : 3 * per] = high[(to - 1) % devices]
        out_ref[to, 3 * per : 4 * per] = high[(to + 1) % devices]
    out_ref[:, 4 * per :] = jnp.zeros((devices, 32, width), jnp.bfloat16)
    cell = lax.broadcasted_iota(jnp.int32, (8, cells), 1)
    which = lax.broadcasted_iota(jnp.int32, (8, cells), 0)
    picked = jnp.where(which < 2, which, cells - 4 + which)
    picker = jnp.where((cell == picked) & (which < 4), 1.0, 0.0).astype(jnp.bfloat16)
    weights = lax.dot_general(
        picker,
        own_share(phi_ref, per),
        (((1,), (1,)), ((), ())),
        preferred_element_type=jnp.float32,
    )
    for side in range(2):
        start = 0 if side else cells - REACH
        first = 0 if side else 2
        for layer in range(layers):
            edge_ref[side, layer * REACH : (layer + 1) * REACH] = field_ref[
                layer, start : start + REACH
            ]
        for part in range(count // width):
            at = layers * REACH + 2 * part
            edge_ref[side, at : at + 2] = weights[
                first : first + 2, part * width : (part + 1) * width
            ]
        high, low = high_low(edge_ref[side])
        to = lax.rem(here + (devices - 1 if side else 1), devices)
        out_ref[to, 4 * per : 4 * per + 16] = high
        out_ref[to, 4 * per + 16 :] = low


def coef_kernel(radial_ref, theta_ref, phi_ref, weight_ref, inv_ref, lon_ref, lat_ref, share_ref):
    layers, spread, width = inv_ref.shape
    cells = share_ref.shape[0]
    per = weight_ref.shape[1] // 2
    chunks = phi_ref.shape[0]
    total = chunks * width
    share_ref[...] = own_share(weight_ref, per).astype(jnp.float32).T.astype(jnp.bfloat16)
    row = lax.broadcasted_iota(jnp.int32, (spread, width), 0)
    lane = lax.broadcasted_iota(jnp.int32, (spread, width), 1)
    cell = lax.axis_index("phi") * cells + jnp.where(row < cells + 4, row, row - spread)
    cell = jnp.where(cell < 0, cell + total, jnp.where(cell >= total, cell - total, cell))
    found = jnp.zeros((spread, width), jnp.float32)
    for chunk in range(chunks):
        found = found + jnp.where(lane + chunk * width == cell, phi_ref[chunk : chunk + 1], 0.0)
    column = jnp.broadcast_to(jnp.sum(found, axis=1, keepdims=True), (spread, width))
    upper = 0.5 * (column + pltpu.roll(column, spread - 1, 0))
    lower = pltpu.roll(upper, 1, 0)
    lon_ref[...] = upper
    theta = jnp.broadcast_to(theta_ref[...], (8, width))
    end = lax.broadcasted_iota(jnp.int32, (8, width), 1) == width - 1
    lat_upper = jnp.where(end, 0.0, 0.5 * (theta + pltpu.roll(theta, width - 1, 1)))
    lat_ref[...] = lat_upper
    flat = upper + lower + (lat_upper + pltpu.roll(lat_upper, 1, 1))[:1]
    for layer in range(layers):
        low, high = (radial_face(radial_ref, layers, layer + k) for k in range(2))
        inv_ref[layer] = 1.0 / (flat + (low + high))


def boundary_kernel(got_ref, share_ref, out_ref):
    devices, _, width = got_ref.shape
    cells, count = share_ref.shape
    per = count // devices
    spread = cells + 8
    layers = (out_ref.shape[0] - spread) // 8
    here = lax.axis_index("phi")
    below = lax.rem(here + devices - 1, devices)
    above = lax.rem(here + 1, devices)

    def rows(which):
        return got_ref[:, which * per : (which + 1) * per].reshape(count, width)

    own = jnp.dot(
        share_ref[...],
        jnp.concatenate([rows(0), rows(1)], axis=1),
        preferred_element_type=jnp.float32,
    )
    out_ref[:cells] = own[:, :width] + own[:, width:]
    out_ref[cells:] = jnp.zeros((out_ref.shape[0] - cells, width), jnp.float32)
    for side, source in enumerate((above, below)):
        high = got_ref[source, 4 * per : 4 * per + 16].astype(jnp.float32)
        edge = high + got_ref[source, 4 * per + 16 :].astype(jnp.float32)
        at = layers * REACH
        weights = jnp.concatenate(
            [high[at + 2 * k : at + 2 * k + 2] for k in range(count // width)], axis=1
        )
        weights = jnp.concatenate([weights, jnp.zeros((6, count), jnp.float32)], axis=0)
        ghost = jnp.dot(
            weights.astype(jnp.bfloat16), rows(2 if side else 3), preferred_element_type=jnp.float32
        )
        at = spread - 2 if side else cells
        out_ref[at : at + 2] = ghost[:2]
        for layer in range(layers):
            at = spread + layer * 8 + (8 - REACH if side else 0)
            out_ref[at : at + REACH] = edge[layer * REACH : (layer + 1) * REACH]


def krylov_kernel(
    radial_ref,
    mine_ref,
    other_ref,
    field_ref,
    far_ref,
    inv_ref,
    lon_ref,
    lat_ref,
    sums_ref,
    residual_ref,
    first_ref,
    image_ref,
    second_ref,
    image2_ref,
    x_ref,
    u_ref,
    v_ref,
    r_ref,
    w_ref,
):
    layers, cells, width = field_ref.shape
    every, spread, _ = inv_ref.shape
    row = lax.axis_index("row")
    lon, lat = lon_ref[...], lat_ref[:1]
    nothing = jnp.zeros((spread, width), jnp.float32)
    for ref in (x_ref, u_ref, v_ref):
        ref[0] = nothing
        ref[every + 1] = nothing
    for ref, edge, base in (
        (field_ref, mine_ref, row * layers),
        (far_ref, other_ref, (1 - row) * layers),
    ):
        for layer in range(layers):
            x_ref[base + layer + 1, :cells] = ref[layer]
            x_ref[base + layer + 1, cells:] = edge[spread + 8 * layer : spread + 8 * layer + 8]

    def operate(ref, start, count):
        mid = ref[start + 1]
        below = radial_face(radial_ref, every, start) * (mid - ref[start])
        for step in range(count):
            layer = start + step
            ahead = ref[layer + 2]
            rise = radial_face(radial_ref, every, layer + 1) * (ahead - mid)
            along = lon * (mid - pltpu.roll(mid, spread - 1, 0))
            across = lat * (mid - pltpu.roll(mid, width - 1, 1))
            yield (
                layer,
                step,
                (below - rise)
                + (along - pltpu.roll(along, 1, 0))
                + (across - pltpu.roll(across, 1, 1)),
            )
            mid, below = ahead, rise

    inflow = radial_face(radial_ref, every, 0) * (mine_ref[:spread] + other_ref[:spread])
    for layer, _, value in operate(x_ref, row * (layers - 2), layers + 2):
        residual = jnp.where(layer == 0, inflow, 0.0) - value
        r_ref[layer] = residual
        u_ref[layer + 1] = residual * inv_ref[layer]
    for layer, _, value in operate(u_ref, row * (layers - 1), layers + 1):
        w_ref[layer] = value
        v_ref[layer + 1] = value * inv_ref[layer]

    totals = [jnp.zeros((8, width), jnp.float32)] * 4
    for layer, step, value in operate(v_ref, row * layers, layers):
        residual, first = r_ref[layer, :cells], u_ref[layer + 1, :cells]
        image, second = w_ref[layer, :cells], v_ref[layer + 1, :cells]
        image2 = value[:cells]
        residual_ref[step] = residual
        first_ref[step] = first
        image_ref[step] = image
        second_ref[step] = second
        image2_ref[step] = image2
        pairs = ((residual, first), (first, image), (image, second), (second, image2))
        for which, (left, right) in enumerate(pairs):
            product = left * right
            for at in range(0, cells, 8):
                totals[which] = totals[which] + product[at : at + 8]
    lane = lax.broadcasted_iota(jnp.int32, (8, width), 1)
    packed = jnp.zeros((8, width), jnp.float32)
    for which, total in enumerate(totals):
        packed = jnp.where(lane == which, jnp.sum(total, axis=1, keepdims=True), packed)
    sums_ref[...] = jnp.broadcast_to(jnp.sum(packed, axis=0, keepdims=True), sums_ref.shape)


def update_kernel(
    sums_ref,
    field_ref,
    residual_ref,
    first_ref,
    image_ref,
    second_ref,
    image2_ref,
    out_ref,
    left_ref,
):
    totals = jnp.sum(sums_ref[...], axis=0, keepdims=True)
    lane = lax.broadcasted_iota(jnp.int32, totals.shape, 1)
    a, b, c, e = (
        jnp.sum(jnp.where(lane == which, totals, 0.0), axis=1, keepdims=True) for which in range(4)
    )
    alpha, gain, alpha_next = step_sizes(a, b, c, e)
    along, back = alpha + alpha_next * gain, alpha_next * alpha
    for layer in range(field_ref.shape[0]):
        out_ref[layer] = field_ref[layer] + (along * first_ref[layer] - back * second_ref[layer])
        left_ref[layer] = residual_ref[layer] - (along * image_ref[layer] - back * image2_ref[layer])


def in_vmem(count):
    return [pl.BlockSpec(memory_space=pltpu.VMEM)] * count


def paired_body(
    magnetogram,
    col_owner,
    col_offset,
    phi_weight,
    theta_weight,
    radial_coef,
    theta_coef,
    phi_coef,
    start_field,
):
    layers, cells, width = start_field.shape
    phi_devices = lax.axis_size("phi")
    slots = phi_weight.shape[0]
    capacity = slots // phi_devices
    per = capacity // 2
    count = phi_devices * per
    columns = magnetogram.shape[0]
    every, spread = 2 * layers, cells + 8
    real, half = jnp.float32, jnp.bfloat16
    struct = jax.ShapeDtypeStruct
    in_smem = [pl.BlockSpec(memory_space=pltpu.SMEM)]

    def swap(value):
        return lax.ppermute(value, "row", [(0, 1), (1, 0)])

    weights = phi_weight.reshape(phi_devices, capacity, cells)
    mine = pl.pallas_call(
        column_kernel,
        compiler_params=pltpu.CompilerParams(vmem_limit_bytes=8 << 20),
        out_shape=struct((columns, width), real),
        in_specs=in_vmem(2),
        out_specs=in_vmem(1)[0],
    )(magnetogram, theta_weight)
    sent = pl.pallas_call(
        pack_kernel,
        compiler_params=pltpu.CompilerParams(vmem_limit_bytes=8 << 20),
        out_shape=struct((phi_devices, 4 * per + 32, width), half),
        in_specs=in_vmem(6),
        out_specs=in_vmem(1)[0],
        scratch_shapes=[pltpu.VMEM((2, 16, width), real)],
    )(
        mine,
        swap(mine),
        col_owner.reshape(1, -1),
        col_offset.reshape(1, -1),
        weights,
        start_field,
    )
    sent, radial_coef, theta_coef, phi_coef, field = lax.optimization_barrier(
        (sent, radial_coef, theta_coef, phi_coef, start_field)
    )
    got = lax.all_to_all(sent, "phi", split_axis=0, concat_axis=0, tiled=True)
    far = swap(field)
    inv_diag, lon, lat, share = pl.pallas_call(
        coef_kernel,
        compiler_params=pltpu.CompilerParams(vmem_limit_bytes=8 << 20),
        out_shape=[
            struct((every, spread, width), real),
            struct((spread, width), real),
            struct((8, width), real),
            struct((cells, count), half),
        ],
        in_specs=in_smem + in_vmem(3),
        out_specs=in_vmem(4),
    )(radial_coef, theta_coef.reshape(1, width), phi_coef.reshape(-1, width), weights)
    part = pl.pallas_call(
        boundary_kernel,
        compiler_params=pltpu.CompilerParams(vmem_limit_bytes=8 << 20),
        out_shape=struct((spread + 8 * layers, width), real),
        in_specs=in_vmem(2),
        out_specs=in_vmem(1)[0],
    )(got, share)
    block = struct((layers, cells, width), real)
    lines = pltpu.VMEM((every + 2, spread, width), real)
    sums, *vectors = pl.pallas_call(
        krylov_kernel,
        compiler_params=pltpu.CompilerParams(vmem_limit_bytes=8 << 20),
        out_shape=[struct((2 * phi_devices, width), real)] + [block] * 5,
        in_specs=in_smem + in_vmem(7),
        out_specs=in_vmem(6),
        scratch_shapes=[lines] * 5,
    )(radial_coef, part, swap(part), field, far, inv_diag, lon, lat)
    sums = lax.all_to_all(sums, ("phi", "row"), split_axis=0, concat_axis=0, tiled=True)
    return pl.pallas_call(
        update_kernel,
        compiler_params=pltpu.CompilerParams(vmem_limit_bytes=8 << 20),
        out_shape=[block] * 2,
        in_specs=in_vmem(7),
        out_specs=in_vmem(2),
    )(sums, field, *vectors)


def body(*args):
    phi_weight, phi_coef, start_field = args[3], args[7], args[8]
    layers, cells, width = start_field.shape
    phi_devices = lax.axis_size("phi")
    per = phi_weight.shape[0] // phi_devices // 2
    edge_rows = layers * REACH + 2 * phi_devices * per // width
    fits = (
        lax.axis_size("row") == 2
        and phi_devices > 2
        and per % 16 == 0
        and layers >= 2
        and cells % 8 == 0
        and width % 128 == 0
        and phi_devices * per % width == 0
        and phi_coef.shape[0] % width == 0
        and edge_rows <= 16
    )
    return (paired_body if fits else general_body)(*args)


def solution(mesh):
    in_specs = (
        P("phi", "row"),
        P("phi"),
        P("phi"),
        P(None, "phi"),
        P("row", None),
        P(),
        P(),
        P(),
        P("row", "phi", None),
    )
    out_specs = (P("row", "phi", None), P("row", "phi", None))
    return jax.shard_map(body, mesh=mesh, in_specs=in_specs, out_specs=out_specs, check_vma=False)
```

```python
import jax
import jax.numpy as jnp
from jax import lax
from jax.experimental import pallas as pl
from jax.experimental.pallas import tpu as pltpu
from jax.sharding import PartitionSpec as P

REACH = 3


def face_coefs(radial_coef, theta_coef, phi_coef):
    radial_mid = 0.5 * (radial_coef[:-1] + radial_coef[1:])
    radial_upper = jnp.concatenate([radial_mid, radial_coef[-1:]])
    radial_lower = jnp.concatenate([radial_coef[:1], radial_mid])
    theta_mid = 0.5 * (theta_coef[:-1] + theta_coef[1:])
    zero_one = jnp.zeros((1,), jnp.float32)
    theta_upper = jnp.concatenate([theta_mid, zero_one])
    theta_lower = jnp.concatenate([zero_one, theta_mid])
    phi_upper = 0.5 * (phi_coef + jnp.roll(phi_coef, -1))
    phi_lower = jnp.roll(phi_upper, 1)
    return (radial_upper, radial_lower, theta_upper, theta_lower, phi_upper, phi_lower)


def row_sum(value, rows):
    if rows == 2:
        return value + lax.ppermute(value, "row", [(0, 1), (1, 0)])
    return lax.psum(value, "row")


def pick(chunks, index):
    return lax.dynamic_index_in_dim(chunks, index, 0, keepdims=False)


def step_sizes(a, b, c, e):
    alpha = a / b
    beta = (alpha * alpha * c - a) / a
    gain = 1.0 + beta
    curvature = gain * gain * b - 2.0 * gain * alpha * c + alpha * alpha * e
    return alpha, gain, beta * a / curvature


def general_body(
    magnetogram,
    col_owner,
    col_offset,
    phi_weight,
    theta_weight,
    radial_coef,
    theta_coef,
    phi_coef,
    start_field,
):
    layers, cells, width = start_field.shape
    phi_devices = lax.axis_size("phi")
    rows = lax.axis_size("row")
    slots = phi_weight.shape[0]
    capacity = slots // phi_devices
    per = capacity // rows
    here = lax.axis_index("phi")
    row = lax.axis_index("row")
    above = lax.rem(here + 1, phi_devices)
    below = lax.rem(here + phi_devices - 1, phi_devices)

    climb = [(i, i + 1) for i in range(rows - 1)]
    low_layers = lax.ppermute(start_field[layers - REACH :], "row", climb)
    high_layers = lax.ppermute(start_field[:REACH], "row", [(t, s) for s, t in climb])
    window = jnp.concatenate([low_layers, start_field, high_layers], axis=0)

    columns = jnp.dot(magnetogram, theta_weight, preferred_element_type=jnp.float32)
    columns = row_sum(columns, rows)
    upper_part = lax.optimization_barrier(columns.astype(jnp.bfloat16))
    lower_part = (columns - upper_part.astype(jnp.float32)).astype(jnp.bfloat16)

    place = col_offset - row * per
    target = jnp.where((place >= 0) & (place < per), col_owner * per + place, -1)
    chosen = (target[None, :] == jnp.arange(phi_devices * per, dtype=jnp.int32)[:, None]).astype(
        jnp.bfloat16
    )
    packed = jnp.dot(chosen, upper_part, preferred_element_type=jnp.float32)
    packed = packed + jnp.dot(chosen, lower_part, preferred_element_type=jnp.float32)
    packed = packed.reshape(phi_devices, per, width)
    share = phi_weight.reshape(phi_devices, rows, per, cells)
    share = lax.dynamic_index_in_dim(share, row, 1, keepdims=False)
    share = share.reshape(phi_devices * per, cells)

    def edge(start):
        field = window[:, start : start + REACH].reshape(-1, width)
        lo = start + 1 if start else 0
        weights = share[:, lo : lo + 2].astype(jnp.float32).T.reshape(-1, width)
        return jnp.concatenate([field, weights], axis=0)

    to_above, to_below = edge(cells - REACH), edge(0)
    who = jnp.arange(phi_devices, dtype=jnp.int32)[:, None, None]
    edges = jnp.where(who == above, to_above[None], jnp.where(who == below, to_below[None], 0.0))
    sent = jnp.concatenate(
        [packed, jnp.roll(packed, 1, axis=0), jnp.roll(packed, -1, axis=0), edges], axis=1
    )
    got = lax.all_to_all(sent, "phi", split_axis=0, concat_axis=0, tiled=True)
    edge_low, edge_high = pick(got, below)[3 * per :], pick(got, above)[3 * per :]
    reach_rows = window.shape[0] * REACH

    def weigh(weights, which):
        data = got[:, which * per : (which + 1) * per].reshape(phi_devices * per, width)
        part = lax.optimization_barrier(data.astype(jnp.bfloat16))
        rest = (data - part.astype(jnp.float32)).astype(jnp.bfloat16)
        total = jnp.dot(weights, part, preferred_element_type=jnp.float32)
        return total + jnp.dot(weights, rest, preferred_element_type=jnp.float32)

    def ghost_weights(edge_rows):
        return edge_rows[reach_rows:].reshape(2, phi_devices * per).astype(jnp.bfloat16)

    boundary = row_sum(
        jnp.concatenate(
            [
                weigh(ghost_weights(edge_low), 1),
                weigh(share.T, 0),
                weigh(ghost_weights(edge_high), 2),
            ],
            axis=0,
        ),
        rows,
    )
    field = jnp.concatenate(
        [
            edge_low[:reach_rows].reshape(-1, REACH, width),
            window,
            edge_high[:reach_rows].reshape(-1, REACH, width),
        ],
        axis=1,
    )

    faces = face_coefs(radial_coef, theta_coef, phi_coef)
    spread = layers + 2 * REACH

    def radial_window(coef):
        padded = jnp.pad(coef, (REACH, REACH))
        return lax.dynamic_slice_in_dim(padded, row * layers, spread)[:, None, None]

    def phi_window(coef):
        padded = jnp.concatenate([coef[-REACH:], coef, coef[:REACH]])
        return lax.dynamic_slice_in_dim(padded, here * cells, cells + 2 * REACH)[None, :, None]

    rad_upper, rad_lower = radial_window(faces[0]), radial_window(faces[1])
    lon_upper, lon_lower = phi_window(faces[4]), phi_window(faces[5])
    lat_upper, lat_lower = faces[2][None, None, :], faces[3][None, None, :]
    inside = radial_window(jnp.ones_like(radial_coef))
    inv_diag = inside / (
        rad_upper + rad_lower + lat_upper + lat_lower + lon_upper + lon_lower + (1.0 - inside)
    )

    def apply_operator(value, depth):
        mid = value[1:-1, 1:-1]
        theta_pad = jnp.pad(mid, ((0, 0), (0, 0), (1, 1)))
        result = rad_upper[depth:-depth] * (mid - value[2:, 1:-1])
        result = result + rad_lower[depth:-depth] * (mid - value[:-2, 1:-1])
        result = result + lat_upper * (mid - theta_pad[:, :, 2:])
        result = result + lat_lower * (mid - theta_pad[:, :, :-2])
        result = result + lon_upper[:, depth:-depth] * (mid - value[1:-1, 2:])
        return result + lon_lower[:, depth:-depth] * (mid - value[1:-1, :-2])

    def inner(value, by):
        return value[by:-by, by:-by] if by else value

    level = row * layers - REACH + 1 + jnp.arange(spread - 2, dtype=jnp.int32)[:, None, None]
    source = jnp.where(level == 0, (faces[1][0] * boundary)[None], 0.0)
    residual = source - apply_operator(field, 1)
    first = residual * inner(inv_diag, 1)
    first_image = apply_operator(first, 2)
    second = first_image * inner(inv_diag, 2)
    second_image = apply_operator(second, 3)
    residual, first = inner(residual, 2), inner(first, 2)
    first_image, second = inner(first_image, 1), inner(second, 1)

    pairs = (
        (residual, first),
        (first, first_image),
        (first_image, second),
        (second, second_image),
    )
    sums = jnp.stack([jnp.sum(u * v, axis=(0, 1)) for u, v in pairs] * 2)
    devices = phi_devices * rows
    if devices <= 64:
        shared = jnp.broadcast_to(sums[None], (devices,) + sums.shape)
        shared = lax.all_to_all(shared, ("phi", "row"), split_axis=0, concat_axis=0, tiled=True)
        totals = jnp.sum(shared, axis=(0, 2))
    else:
        totals = lax.psum(jnp.sum(sums, axis=1), ("phi", "row"))
    alpha, gain, alpha_next = step_sizes(totals[0], totals[1], totals[2], totals[3])
    direction = gain * first - alpha * second
    solution_field = start_field + alpha * first + alpha_next * direction
    image = gain * first_image - alpha * second_image
    return solution_field, residual - alpha * first_image - alpha_next * image


def high_low(value):
    high = value.astype(jnp.bfloat16)
    return high, (value - high.astype(jnp.float32)).astype(jnp.bfloat16)


def radial_face(radial_ref, layers, face):
    if isinstance(face, int):
        low, high = max(face - 1, 0), min(face, layers - 1)
    else:
        low, high = jnp.maximum(face - 1, 0), jnp.minimum(face, layers - 1)
    return 0.5 * (radial_ref[low] + radial_ref[high])


def own_share(weights, devices):
    slots = weights.shape[1]
    per = slots // devices // 2
    slot = lax.broadcasted_iota(jnp.int32, (slots, slots // 2), 0)
    place = lax.broadcasted_iota(jnp.int32, (slots, slots // 2), 1)
    wanted = place // per * (2 * per) + lax.axis_index("row") * per + place % per
    picker = jnp.where(slot == wanted, 1.0, 0.0).astype(jnp.bfloat16)
    return jnp.dot(weights, picker, preferred_element_type=jnp.float32).astype(jnp.bfloat16)


def column_kernel(
    mag_hbm,
    theta_hbm,
    owner_hbm,
    offset_hbm,
    out_ref,
    chosen_ref,
    mag_ref,
    theta_ref,
    owner_ref,
    offset_ref,
    done,
):
    pairs = (
        (theta_hbm, theta_ref),
        (mag_hbm, mag_ref),
        (owner_hbm, owner_ref),
        (offset_hbm, offset_ref),
    )
    copies = [pltpu.make_async_copy(*pair, done.at[at]) for at, pair in enumerate(pairs)]
    for copy in copies:
        copy.start()
    for copy in copies:
        copy.wait()
    out_ref[...] = jnp.dot(mag_ref[...], theta_ref[...], preferred_element_type=jnp.float32)
    per = chosen_ref.shape[0] // lax.axis_size("phi")
    place = offset_ref[...] - lax.axis_index("row") * per
    target = jnp.where((place >= 0) & (place < per), owner_ref[...] * per + place, -1)
    slot = lax.broadcasted_iota(jnp.int32, chosen_ref.shape, 0)
    chosen_ref[...] = jnp.where(slot == target, 1.0, 0.0).astype(jnp.bfloat16)


def pack_kernel(mine_ref, other_ref, chosen_ref, out_ref):
    devices, rows, width = out_ref.shape
    per = rows // 4
    high, low = high_low(mine_ref[...] + other_ref[...])
    packed = jnp.dot(
        chosen_ref[...], jnp.concatenate([high, low], axis=1), preferred_element_type=jnp.float32
    ).astype(jnp.bfloat16)
    high = packed[:, :width].reshape(devices, per, width)
    low = packed[:, width:].reshape(devices, per, width)
    out_ref[:, :per] = high
    out_ref[:, per : 2 * per] = low
    for to in range(devices):
        out_ref[to, 2 * per : 3 * per] = high[(to - 1) % devices]
        out_ref[to, 3 * per : 4 * per] = high[(to + 1) % devices]


def is_odd():
    return lax.rem(lax.axis_index("phi"), 2) == 1


def edge_kernel(field_ref, weight_ref, far_ref, near_ref, share_ref):
    layers, cells, width = field_ref.shape
    devices = lax.axis_size("phi")
    share = own_share(weight_ref[...], devices)
    share_ref[...] = share
    weights = share.astype(jnp.float32)
    odd = is_odd()

    def put(at, up, down):
        far_ref[at : at + up.shape[0]] = jnp.where(odd, up, down)
        near_ref[at : at + up.shape[0]] = jnp.where(odd, down, up)

    for layer in range(layers):
        put(layer * REACH, field_ref[layer, cells - REACH :], field_ref[layer, :REACH])
    for part in range(share.shape[1] // width):
        piece = weights[:, part * width : (part + 1) * width]
        put(layers * REACH + 2 * part, piece[cells - 2 :], piece[:2])


def coef_kernel(radial_ref, theta_ref, phi_ref, inv_ref, lon_ref, lat_ref):
    layers, spread, width = inv_ref.shape
    cells = spread - 8
    chunks = phi_ref.shape[0]
    total = chunks * width
    row = lax.broadcasted_iota(jnp.int32, (spread, width), 0)
    lane = lax.broadcasted_iota(jnp.int32, (spread, width), 1)
    cell = lax.axis_index("phi") * cells + jnp.where(row < cells + 4, row, row - spread)
    cell = jnp.where(cell < 0, cell + total, jnp.where(cell >= total, cell - total, cell))
    found = jnp.zeros((spread, width), jnp.float32)
    for chunk in range(chunks):
        found = found + jnp.where(lane + chunk * width == cell, phi_ref[chunk : chunk + 1], 0.0)
    column = jnp.broadcast_to(jnp.sum(found, axis=1, keepdims=True), (spread, width))
    upper = 0.5 * (column + pltpu.roll(column, spread - 1, 0))
    lower = pltpu.roll(upper, 1, 0)
    lon_ref[...] = upper
    theta = jnp.broadcast_to(theta_ref[...], (8, width))
    end = lax.broadcasted_iota(jnp.int32, (8, width), 1) == width - 1
    lat_upper = jnp.where(end, 0.0, 0.5 * (theta + pltpu.roll(theta, width - 1, 1)))
    lat_ref[...] = lat_upper
    flat = upper + lower + (lat_upper + pltpu.roll(lat_upper, 1, 1))[:1]
    for layer in range(layers):
        low, high = (radial_face(radial_ref, layers, layer + k) for k in range(2))
        inv_ref[layer] = 1.0 / (flat + (low + high))


def boundary_kernel(got_ref, share_ref, far_ref, near_ref, out_ref):
    devices, rows, width = got_ref.shape
    cells, count = share_ref.shape
    per, spread = rows // 4, cells + 8
    layers = (out_ref.shape[0] - spread) // 8
    odd = is_odd()
    above_edge = jnp.where(odd, far_ref[...], near_ref[...])
    below_edge = jnp.where(odd, near_ref[...], far_ref[...])

    def product(weights, first):
        data = [
            got_ref[:, which * per : (which + 1) * per].reshape(count, width)
            for which in (first, first + 1)
        ]
        total = jnp.dot(
            weights, jnp.concatenate(data, axis=1), preferred_element_type=jnp.float32
        )
        return total[:, :width], total[:, width:]

    def edge_weights(edge):
        at = layers * REACH
        parts = [edge[at + 2 * k : at + 2 * k + 2] for k in range(count // width)]
        return jnp.concatenate(parts, axis=1)

    high, low = product(share_ref[...], 0)
    out_ref[:cells] = high + low
    weights = jnp.concatenate(
        [edge_weights(above_edge), jnp.zeros((4, count), jnp.float32), edge_weights(below_edge)],
        axis=0,
    )
    below, above = product(weights.astype(jnp.bfloat16), 2)
    row = lax.broadcasted_iota(jnp.int32, (8, width), 0)
    out_ref[cells:spread] = jnp.where(row < 4, above, below)
    for layer in range(layers):
        at, part = spread + 8 * layer, slice(layer * REACH, (layer + 1) * REACH)
        out_ref[at : at + 8] = jnp.concatenate(
            [above_edge[part], jnp.zeros((8 - 2 * REACH, width), jnp.float32), below_edge[part]],
            axis=0,
        )


def krylov_kernel(
    radial_ref,
    mine_ref,
    other_ref,
    field_ref,
    far_ref,
    inv_ref,
    lon_ref,
    lat_ref,
    sums_ref,
    residual_ref,
    first_ref,
    image_ref,
    second_ref,
    image2_ref,
    x_ref,
    u_ref,
    v_ref,
    r_ref,
    w_ref,
):
    layers, cells, width = field_ref.shape
    every, spread, _ = inv_ref.shape
    row = lax.axis_index("row")
    lon, lat = lon_ref[...], lat_ref[:1]
    nothing = jnp.zeros((spread, width), jnp.float32)
    for ref in (x_ref, u_ref, v_ref):
        ref[0] = nothing
        ref[every + 1] = nothing
    for ref, edge, base in (
        (field_ref, mine_ref, row * layers),
        (far_ref, other_ref, (1 - row) * layers),
    ):
        for layer in range(layers):
            x_ref[base + layer + 1, :cells] = ref[layer]
            x_ref[base + layer + 1, cells:] = edge[spread + 8 * layer : spread + 8 * layer + 8]

    def operate(ref, start, count):
        mid = ref[start + 1]
        below = radial_face(radial_ref, every, start) * (mid - ref[start])
        for step in range(count):
            layer = start + step
            ahead = ref[layer + 2]
            rise = radial_face(radial_ref, every, layer + 1) * (ahead - mid)
            along = lon * (mid - pltpu.roll(mid, spread - 1, 0))
            across = lat * (mid - pltpu.roll(mid, width - 1, 1))
            yield (
                layer,
                step,
                (below - rise)
                + (along - pltpu.roll(along, 1, 0))
                + (across - pltpu.roll(across, 1, 1)),
            )
            mid, below = ahead, rise

    inflow = radial_face(radial_ref, every, 0) * (mine_ref[:spread] + other_ref[:spread])
    for layer, _, value in operate(x_ref, row * (layers - 2), layers + 2):
        residual = jnp.where(layer == 0, inflow, 0.0) - value
        r_ref[layer] = residual
        u_ref[layer + 1] = residual * inv_ref[layer]
    for layer, _, value in operate(u_ref, row * (layers - 1), layers + 1):
        w_ref[layer] = value
        v_ref[layer + 1] = value * inv_ref[layer]

    totals = [jnp.zeros((8, width), jnp.float32)] * 4
    for layer, step, value in operate(v_ref, row * layers, layers):
        residual, first = r_ref[layer, :cells], u_ref[layer + 1, :cells]
        image, second = w_ref[layer, :cells], v_ref[layer + 1, :cells]
        image2 = value[:cells]
        residual_ref[step] = residual
        first_ref[step] = first
        image_ref[step] = image
        second_ref[step] = second
        image2_ref[step] = image2
        pairs = ((residual, first), (first, image), (image, second), (second, image2))
        for which, (left, right) in enumerate(pairs):
            product = left * right
            for at in range(0, cells, 8):
                totals[which] = totals[which] + product[at : at + 8]
    lane = lax.broadcasted_iota(jnp.int32, (8, width), 1)
    packed = jnp.zeros((8, width), jnp.float32)
    for which, total in enumerate(totals):
        packed = jnp.where(lane == which, jnp.sum(total, axis=1, keepdims=True), packed)
    sums_ref[...] = jnp.broadcast_to(jnp.sum(packed, axis=0, keepdims=True), sums_ref.shape)


def update_kernel(
    sums_ref,
    field_ref,
    residual_ref,
    first_ref,
    image_ref,
    second_ref,
    image2_ref,
    out_ref,
    left_ref,
):
    totals = jnp.sum(sums_ref[...], axis=0, keepdims=True)
    lane = lax.broadcasted_iota(jnp.int32, totals.shape, 1)
    a, b, c, e = (
        jnp.sum(jnp.where(lane == which, totals, 0.0), axis=1, keepdims=True) for which in range(4)
    )
    alpha, gain, alpha_next = step_sizes(a, b, c, e)
    along, back = alpha + alpha_next * gain, alpha_next * alpha
    for layer in range(field_ref.shape[0]):
        out_ref[layer] = field_ref[layer] + (along * first_ref[layer] - back * second_ref[layer])
        left_ref[layer] = residual_ref[layer] - (along * image_ref[layer] - back * image2_ref[layer])


SMALL = pltpu.CompilerParams(vmem_limit_bytes=8 << 20)


def in_vmem(count):
    return [pl.BlockSpec(memory_space=pltpu.VMEM)] * count


def paired_body(
    magnetogram,
    col_owner,
    col_offset,
    phi_weight,
    theta_weight,
    radial_coef,
    theta_coef,
    phi_coef,
    start_field,
):
    layers, cells, width = start_field.shape
    phi_devices = lax.axis_size("phi")
    per = phi_weight.shape[0] // phi_devices // 2
    count = phi_devices * per
    columns = magnetogram.shape[0]
    every, spread = 2 * layers, cells + 8
    real, half = jnp.float32, jnp.bfloat16
    struct = jax.ShapeDtypeStruct
    in_smem = [pl.BlockSpec(memory_space=pltpu.SMEM)]

    def swap(value):
        return lax.ppermute(value, "row", [(0, 1), (1, 0)])

    inner = [(i, i ^ 1) for i in range(phi_devices)]
    outer = [(i, (i + (1 if i % 2 else -1)) % phi_devices) for i in range(phi_devices)]

    def in_hbm(value):
        return pltpu.with_memory_space_constraint(value, pltpu.HBM)

    mine, chosen = pl.pallas_call(
        column_kernel,
        compiler_params=SMALL,
        out_shape=[struct((columns, width), real), struct((count, columns), half)],
        in_specs=[pl.BlockSpec(memory_space=pltpu.HBM)] * 4,
        out_specs=in_vmem(2),
        scratch_shapes=[
            pltpu.VMEM(magnetogram.shape, half),
            pltpu.VMEM(theta_weight.shape, half),
            pltpu.VMEM((1, columns), jnp.int32),
            pltpu.VMEM((1, columns), jnp.int32),
            pltpu.SemaphoreType.DMA((4,)),
        ],
    )(
        in_hbm(magnetogram),
        in_hbm(theta_weight),
        in_hbm(col_owner.reshape(1, -1)),
        in_hbm(col_offset.reshape(1, -1)),
    )
    sent = pl.pallas_call(
        pack_kernel,
        compiler_params=SMALL,
        out_shape=struct((phi_devices, 4 * per, width), half),
        in_specs=in_vmem(3),
        out_specs=in_vmem(1)[0],
    )(mine, swap(mine), chosen)
    sent, radial_coef, theta_coef, phi_coef, field, weights = lax.optimization_barrier(
        (sent, radial_coef, theta_coef, phi_coef, start_field, phi_weight.T)
    )
    got = lax.all_to_all(sent, "phi", split_axis=0, concat_axis=0, tiled=True)
    edge_rows = layers * REACH + 2 * count // width
    edge = struct((-(-edge_rows // 8) * 8, width), real)
    far_edge, near_edge, share = pl.pallas_call(
        edge_kernel,
        compiler_params=SMALL,
        out_shape=[edge, edge, struct((cells, count), half)],
        in_specs=in_vmem(2),
        out_specs=in_vmem(3),
    )(field, weights)
    far_edge, near_edge = lax.ppermute(far_edge, "phi", outer), lax.ppermute(near_edge, "phi", inner)
    far = swap(field)
    inv_diag, lon, lat = pl.pallas_call(
        coef_kernel,
        compiler_params=SMALL,
        out_shape=[
            struct((every, spread, width), real),
            struct((spread, width), real),
            struct((8, width), real),
        ],
        in_specs=in_smem + in_vmem(2),
        out_specs=in_vmem(3),
    )(radial_coef, theta_coef.reshape(1, width), phi_coef.reshape(-1, width))
    got, far_edge, near_edge, far, inv_diag, lon, lat = lax.optimization_barrier(
        (got, far_edge, near_edge, far, inv_diag, lon, lat)
    )
    part = pl.pallas_call(
        boundary_kernel,
        compiler_params=SMALL,
        out_shape=struct((spread + 8 * layers, width), real),
        in_specs=in_vmem(4),
        out_specs=in_vmem(1)[0],
    )(got, share, far_edge, near_edge)
    block = struct((layers, cells, width), real)
    lines = pltpu.VMEM((every + 2, spread, width), real)
    sums, *vectors = pl.pallas_call(
        krylov_kernel,
        compiler_params=SMALL,
        out_shape=[struct((2 * phi_devices, width), real)] + [block] * 5,
        in_specs=in_smem + in_vmem(7),
        out_specs=in_vmem(6),
        scratch_shapes=[lines] * 5,
    )(radial_coef, part, swap(part), field, far, inv_diag, lon, lat)
    sums = lax.all_to_all(sums, ("phi", "row"), split_axis=0, concat_axis=0, tiled=True)
    return pl.pallas_call(
        update_kernel,
        compiler_params=SMALL,
        out_shape=[block] * 2,
        in_specs=in_vmem(7),
        out_specs=in_vmem(2),
    )(sums, field, *vectors)


def body(*args):
    phi_weight, phi_coef, start_field = args[3], args[7], args[8]
    layers, cells, width = start_field.shape
    phi_devices = lax.axis_size("phi")
    fits = (
        lax.axis_size("row") == 2
        and phi_devices > 2
        and phi_devices % 2 == 0
        and phi_weight.shape[0] % (32 * phi_devices) == 0
        and layers >= 2
        and cells % 8 == 0
        and cells >= 8
        and width % 128 == 0
        and phi_coef.shape[0] % width == 0
        and phi_weight.shape[0] % (2 * width) == 0
    )
    return (paired_body if fits else general_body)(*args)


def solution(mesh):
    in_specs = (
        P("phi", "row"),
        P("phi"),
        P("phi"),
        P(None, "phi"),
        P("row", None),
        P(),
        P(),
        P(),
        P("row", "phi", None),
    )
    out_specs = (P("row", "phi", None), P("row", "phi", None))
    return jax.shard_map(body, mesh=mesh, in_specs=in_specs, out_specs=out_specs, check_vma=False)
```

```python
import jax
import jax.numpy as jnp
from jax import lax
from jax.experimental import pallas as pl
from jax.experimental.pallas import tpu as pltpu
from jax.sharding import PartitionSpec as P

REACH = 3


def face_coefs(radial_coef, theta_coef, phi_coef):
    radial_mid = 0.5 * (radial_coef[:-1] + radial_coef[1:])
    radial_upper = jnp.concatenate([radial_mid, radial_coef[-1:]])
    radial_lower = jnp.concatenate([radial_coef[:1], radial_mid])
    theta_mid = 0.5 * (theta_coef[:-1] + theta_coef[1:])
    zero_one = jnp.zeros((1,), jnp.float32)
    theta_upper = jnp.concatenate([theta_mid, zero_one])
    theta_lower = jnp.concatenate([zero_one, theta_mid])
    phi_upper = 0.5 * (phi_coef + jnp.roll(phi_coef, -1))
    phi_lower = jnp.roll(phi_upper, 1)
    return (radial_upper, radial_lower, theta_upper, theta_lower, phi_upper, phi_lower)


def row_sum(value, rows):
    if rows == 2:
        return value + lax.ppermute(value, "row", [(0, 1), (1, 0)])
    return lax.psum(value, "row")


def pick(chunks, index):
    return lax.dynamic_index_in_dim(chunks, index, 0, keepdims=False)


def step_sizes(a, b, c, e):
    alpha = a / b
    beta = (alpha * alpha * c - a) / a
    gain = 1.0 + beta
    curvature = gain * gain * b - 2.0 * gain * alpha * c + alpha * alpha * e
    return alpha, gain, beta * a / curvature


def general_body(
    magnetogram,
    col_owner,
    col_offset,
    phi_weight,
    theta_weight,
    radial_coef,
    theta_coef,
    phi_coef,
    start_field,
):
    layers, cells, width = start_field.shape
    phi_devices = lax.axis_size("phi")
    rows = lax.axis_size("row")
    slots = phi_weight.shape[0]
    capacity = slots // phi_devices
    per = capacity // rows
    here = lax.axis_index("phi")
    row = lax.axis_index("row")
    above = lax.rem(here + 1, phi_devices)
    below = lax.rem(here + phi_devices - 1, phi_devices)

    climb = [(i, i + 1) for i in range(rows - 1)]
    low_layers = lax.ppermute(start_field[layers - REACH :], "row", climb)
    high_layers = lax.ppermute(start_field[:REACH], "row", [(t, s) for s, t in climb])
    window = jnp.concatenate([low_layers, start_field, high_layers], axis=0)

    columns = jnp.dot(magnetogram, theta_weight, preferred_element_type=jnp.float32)
    columns = row_sum(columns, rows)
    upper_part = lax.optimization_barrier(columns.astype(jnp.bfloat16))
    lower_part = (columns - upper_part.astype(jnp.float32)).astype(jnp.bfloat16)

    place = col_offset - row * per
    target = jnp.where((place >= 0) & (place < per), col_owner * per + place, -1)
    chosen = (target[None, :] == jnp.arange(phi_devices * per, dtype=jnp.int32)[:, None]).astype(
        jnp.bfloat16
    )
    packed = jnp.dot(chosen, upper_part, preferred_element_type=jnp.float32)
    packed = packed + jnp.dot(chosen, lower_part, preferred_element_type=jnp.float32)
    packed = packed.reshape(phi_devices, per, width)
    share = phi_weight.reshape(phi_devices, rows, per, cells)
    share = lax.dynamic_index_in_dim(share, row, 1, keepdims=False)
    share = share.reshape(phi_devices * per, cells)

    def edge(start):
        field = window[:, start : start + REACH].reshape(-1, width)
        lo = start + 1 if start else 0
        weights = share[:, lo : lo + 2].astype(jnp.float32).T.reshape(-1, width)
        return jnp.concatenate([field, weights], axis=0)

    to_above, to_below = edge(cells - REACH), edge(0)
    who = jnp.arange(phi_devices, dtype=jnp.int32)[:, None, None]
    edges = jnp.where(who == above, to_above[None], jnp.where(who == below, to_below[None], 0.0))
    sent = jnp.concatenate(
        [packed, jnp.roll(packed, 1, axis=0), jnp.roll(packed, -1, axis=0), edges], axis=1
    )
    got = lax.all_to_all(sent, "phi", split_axis=0, concat_axis=0, tiled=True)
    edge_low, edge_high = pick(got, below)[3 * per :], pick(got, above)[3 * per :]
    reach_rows = window.shape[0] * REACH

    def weigh(weights, which):
        data = got[:, which * per : (which + 1) * per].reshape(phi_devices * per, width)
        part = lax.optimization_barrier(data.astype(jnp.bfloat16))
        rest = (data - part.astype(jnp.float32)).astype(jnp.bfloat16)
        total = jnp.dot(weights, part, preferred_element_type=jnp.float32)
        return total + jnp.dot(weights, rest, preferred_element_type=jnp.float32)

    def ghost_weights(edge_rows):
        return edge_rows[reach_rows:].reshape(2, phi_devices * per).astype(jnp.bfloat16)

    boundary = row_sum(
        jnp.concatenate(
            [
                weigh(ghost_weights(edge_low), 1),
                weigh(share.T, 0),
                weigh(ghost_weights(edge_high), 2),
            ],
            axis=0,
        ),
        rows,
    )
    field = jnp.concatenate(
        [
            edge_low[:reach_rows].reshape(-1, REACH, width),
            window,
            edge_high[:reach_rows].reshape(-1, REACH, width),
        ],
        axis=1,
    )

    faces = face_coefs(radial_coef, theta_coef, phi_coef)
    spread = layers + 2 * REACH

    def radial_window(coef):
        padded = jnp.pad(coef, (REACH, REACH))
        return lax.dynamic_slice_in_dim(padded, row * layers, spread)[:, None, None]

    def phi_window(coef):
        padded = jnp.concatenate([coef[-REACH:], coef, coef[:REACH]])
        return lax.dynamic_slice_in_dim(padded, here * cells, cells + 2 * REACH)[None, :, None]

    rad_upper, rad_lower = radial_window(faces[0]), radial_window(faces[1])
    lon_upper, lon_lower = phi_window(faces[4]), phi_window(faces[5])
    lat_upper, lat_lower = faces[2][None, None, :], faces[3][None, None, :]
    inside = radial_window(jnp.ones_like(radial_coef))
    inv_diag = inside / (
        rad_upper + rad_lower + lat_upper + lat_lower + lon_upper + lon_lower + (1.0 - inside)
    )

    def apply_operator(value, depth):
        mid = value[1:-1, 1:-1]
        theta_pad = jnp.pad(mid, ((0, 0), (0, 0), (1, 1)))
        result = rad_upper[depth:-depth] * (mid - value[2:, 1:-1])
        result = result + rad_lower[depth:-depth] * (mid - value[:-2, 1:-1])
        result = result + lat_upper * (mid - theta_pad[:, :, 2:])
        result = result + lat_lower * (mid - theta_pad[:, :, :-2])
        result = result + lon_upper[:, depth:-depth] * (mid - value[1:-1, 2:])
        return result + lon_lower[:, depth:-depth] * (mid - value[1:-1, :-2])

    def inner(value, by):
        return value[by:-by, by:-by] if by else value

    level = row * layers - REACH + 1 + jnp.arange(spread - 2, dtype=jnp.int32)[:, None, None]
    source = jnp.where(level == 0, (faces[1][0] * boundary)[None], 0.0)
    residual = source - apply_operator(field, 1)
    first = residual * inner(inv_diag, 1)
    first_image = apply_operator(first, 2)
    second = first_image * inner(inv_diag, 2)
    second_image = apply_operator(second, 3)
    residual, first = inner(residual, 2), inner(first, 2)
    first_image, second = inner(first_image, 1), inner(second, 1)

    pairs = (
        (residual, first),
        (first, first_image),
        (first_image, second),
        (second, second_image),
    )
    sums = jnp.stack([jnp.sum(u * v, axis=(0, 1)) for u, v in pairs] * 2)
    devices = phi_devices * rows
    if devices <= 64:
        shared = jnp.broadcast_to(sums[None], (devices,) + sums.shape)
        shared = lax.all_to_all(shared, ("phi", "row"), split_axis=0, concat_axis=0, tiled=True)
        totals = jnp.sum(shared, axis=(0, 2))
    else:
        totals = lax.psum(jnp.sum(sums, axis=1), ("phi", "row"))
    alpha, gain, alpha_next = step_sizes(totals[0], totals[1], totals[2], totals[3])
    direction = gain * first - alpha * second
    solution_field = start_field + alpha * first + alpha_next * direction
    image = gain * first_image - alpha * second_image
    return solution_field, residual - alpha * first_image - alpha_next * image


def high_low(value):
    high = value.astype(jnp.bfloat16)
    return high, (value - high.astype(jnp.float32)).astype(jnp.bfloat16)


def column_kernel(
    mag_hbm,
    theta_hbm,
    owner_hbm,
    offset_hbm,
    out_ref,
    chosen_ref,
    mag_ref,
    theta_ref,
    owner_ref,
    offset_ref,
    done,
):
    pairs = (
        (theta_hbm, theta_ref),
        (mag_hbm, mag_ref),
        (owner_hbm, owner_ref),
        (offset_hbm, offset_ref),
    )
    copies = [pltpu.make_async_copy(*pair, done.at[at]) for at, pair in enumerate(pairs)]
    for copy in copies:
        copy.start()
    for copy in copies:
        copy.wait()
    out_ref[...] = jnp.dot(mag_ref[...], theta_ref[...], preferred_element_type=jnp.float32)
    per = chosen_ref.shape[0] // lax.axis_size("phi")
    place = offset_ref[...] - lax.axis_index("row") * per
    target = jnp.where((place >= 0) & (place < per), owner_ref[...] * per + place, -1)
    slot = lax.broadcasted_iota(jnp.int32, chosen_ref.shape, 0)
    chosen_ref[...] = jnp.where(slot == target, 1.0, 0.0).astype(jnp.bfloat16)


def pack_kernel(mine_ref, other_ref, chosen_ref, out_ref):
    targets, rows, width = out_ref.shape
    devices, per = targets // 2, rows // 2
    high, low = high_low(mine_ref[...] + other_ref[...])
    packed = jnp.dot(
        chosen_ref[...], jnp.concatenate([high, low], axis=1), preferred_element_type=jnp.float32
    ).astype(jnp.bfloat16)
    high = packed[:, :width].reshape(devices, per, width)
    low = packed[:, width:].reshape(devices, per, width)
    for to in range(devices):
        out_ref[2 * to, :per] = high[to]
        out_ref[2 * to, per:] = low[to]
        out_ref[2 * to + 1, :per] = high[(to - 1) % devices]
        out_ref[2 * to + 1, per:] = high[(to + 1) % devices]


def is_odd():
    return lax.rem(lax.axis_index("phi"), 2) == 1


def edge_kernel(field_ref, other_ref, weight_ref, far_ref, near_ref):
    layers, cells, width = field_ref.shape
    slots = weight_ref.shape[1]
    odd = is_odd()
    first = lax.axis_index("row") == 0

    def put(at, up, down):
        far_ref[at : at + up.shape[0]] = jnp.where(odd, up, down)
        near_ref[at : at + up.shape[0]] = jnp.where(odd, down, up)

    for layer in range(layers):
        up = [ref[layer, cells - REACH :] for ref in (field_ref, other_ref)]
        down = [ref[layer, :REACH] for ref in (field_ref, other_ref)]
        put(layer * REACH, jnp.where(first, *up), jnp.where(first, *down))
        put((layers + layer) * REACH, jnp.where(first, *up[::-1]), jnp.where(first, *down[::-1]))
    up = weight_ref[cells - 16 :].astype(jnp.float32)[14:]
    down = weight_ref[:16].astype(jnp.float32)[:2]
    for part in range(slots // width):
        piece = slice(part * width, (part + 1) * width)
        put(2 * layers * REACH + 2 * part, up[:, piece], down[:, piece])


def sides(far_ref, near_ref):
    odd = is_odd()
    return (
        jnp.where(odd, far_ref[...], near_ref[...]),
        jnp.where(odd, near_ref[...], far_ref[...]),
    )


def coef_kernel(
    radial_ref, theta_ref, phi_ref, diag_ref, inv_ref, lon_ref, lat_ref, face_ref
):
    layers, spread, width = inv_ref.shape
    cells = spread - 8
    chunks = phi_ref.shape[0]
    total = chunks * width
    row = lax.broadcasted_iota(jnp.int32, (spread, width), 0)
    lane = lax.broadcasted_iota(jnp.int32, (spread, width), 1)
    cell = lax.axis_index("phi") * cells + jnp.where(row < cells + 4, row, row - spread)
    cell = jnp.where(cell < 0, cell + total, jnp.where(cell >= total, cell - total, cell))
    found = jnp.zeros((spread, width), jnp.float32)
    for chunk in range(chunks):
        found = found + jnp.where(lane + chunk * width == cell, phi_ref[chunk : chunk + 1], 0.0)
    column = jnp.broadcast_to(jnp.sum(found, axis=1, keepdims=True), (spread, width))
    lon_ref[0] = 0.5 * (column + pltpu.roll(column, spread - 1, 0))
    lon_ref[1] = 0.5 * (column + pltpu.roll(column, 1, 0))
    theta = jnp.broadcast_to(theta_ref[...], (8, width))
    ends = lax.broadcasted_iota(jnp.int32, (8, width), 1)
    upper = jnp.where(ends == width - 1, 0.0, 0.5 * (theta + pltpu.roll(theta, width - 1, 1)))
    lower = jnp.where(ends == 0, 0.0, 0.5 * (theta + pltpu.roll(theta, 1, 1)))
    lat_ref[0], lat_ref[1] = upper, lower
    flat = lon_ref[0] + lon_ref[1] + (upper + lower)[:1]
    faces = [
        0.5 * (radial_ref[max(face - 1, 0)] + radial_ref[min(face, layers - 1)])
        for face in range(layers + 1)
    ]
    for face in range(layers + 1):
        face_ref[face : face + 1] = jnp.full((1, width), faces[face], jnp.float32)
    for layer in range(layers):
        diag = flat + (faces[layer] + faces[layer + 1])
        diag_ref[layer] = diag
        inv_ref[layer] = 1.0 / diag


def boundary_kernel(got_ref, weight_ref, far_ref, near_ref, own_ref, beyond_ref):
    sources, rows, width = got_ref.shape
    cells, slots = weight_ref.shape
    per = rows // 2

    def product(weights):
        data = [got_ref[:, :per].reshape(slots, width), got_ref[:, per:].reshape(slots, width)]
        total = jnp.dot(
            weights, jnp.concatenate(data, axis=1), preferred_element_type=jnp.float32
        )
        return total[:, :width], total[:, width:]

    @pl.when(lax.axis_index("row") == 0)
    def _():
        high, low = product(weight_ref[...])
        own_ref[...] = high + low
        beyond_ref[...] = jnp.zeros(beyond_ref.shape, jnp.float32)

    @pl.when(lax.axis_index("row") == 1)
    def _():
        above, below = sides(far_ref, near_ref)

        def edge_weights(edge):
            at = edge.shape[0] - 2 * slots // width
            parts = [edge[at + 2 * k : at + 2 * k + 2] for k in range(slots // width)]
            return jnp.concatenate(parts, axis=1)

        weights = jnp.concatenate(
            [edge_weights(above), jnp.zeros((4, slots), jnp.float32), edge_weights(below)], axis=0
        )
        from_below, from_above = product(weights.astype(jnp.bfloat16))
        row = lax.broadcasted_iota(jnp.int32, (8, width), 0)
        own_ref[...] = jnp.zeros(own_ref.shape, jnp.float32)
        beyond_ref[...] = jnp.where(row < 4, from_above, from_below)


def neighbours(values, layer, faces, lon, lat):
    mid = values[layer]
    spread, width = mid.shape
    total = lat[0] * pltpu.roll(mid, width - 1, 1) + lat[1] * pltpu.roll(mid, 1, 1)
    total = total + lon[0] * pltpu.roll(mid, spread - 1, 0)
    total = total + lon[1] * pltpu.roll(mid, 1, 0)
    for at, face in ((layer - 1, layer), (layer + 1, layer + 1)):
        if at in values:
            total = total + faces[face] * values[at]
    return total


def krylov_kernel(
    face_ref,
    own_ref,
    field_ref,
    other_ref,
    far_ref,
    near_ref,
    diag_ref,
    inv_ref,
    lon_ref,
    lat_ref,
    totals_ref,
    *vector_refs,
):
    layers, cells, width = field_ref.shape
    every, spread, _ = inv_ref.shape
    above, below = sides(far_ref, near_ref)
    gap = jnp.zeros((8 - 2 * REACH, width), jnp.float32)

    def work(row):
        faces = [face_ref[face : face + 1] for face in range(every + 1)]
        lon, lat = (lon_ref[0], lon_ref[1]), (lat_ref[0, :1], lat_ref[1, :1])
        halves = (other_ref, field_ref) if row else (field_ref, other_ref)
        field = {}
        for layer in range(every):
            part = slice(layer * REACH, (layer + 1) * REACH)
            block = halves[layer // layers][layer % layers]
            field[layer] = jnp.concatenate([block, above[part], gap, below[part]], axis=0)
        residual, first, image, second = {}, {}, {}, {}
        start = row * (layers - 2)
        for layer in range(start, start + layers + 2):
            value = neighbours(field, layer, faces, lon, lat) - diag_ref[layer] * field[layer]
            if layer == 0:
                source = jnp.concatenate([own_ref[...], jnp.zeros((8, width), jnp.float32)], axis=0)
                value = value + faces[0] * source
            residual[layer] = value
            first[layer] = value * inv_ref[layer]
        start = row * (layers - 1)
        for layer in range(start, start + layers + 1):
            image[layer] = residual[layer] - neighbours(first, layer, faces, lon, lat)
            second[layer] = image[layer] * inv_ref[layer]
        totals = [jnp.zeros((8, width), jnp.float32)] * 4
        for at in range(layers):
            layer = row * layers + at
            image2 = image[layer] - neighbours(second, layer, faces, lon, lat)
            vectors = (residual[layer], first[layer], image[layer], second[layer], image2)
            vectors = [vector[:cells] for vector in vectors]
            for ref, vector in zip(vector_refs, vectors):
                ref[at] = vector
            for which in range(4):
                product = vectors[which] * vectors[which + 1]
                for begin in range(0, cells, 8):
                    later = row == 0 and at < REACH and which and begin in (0, cells - 8)
                    if not later:
                        totals[which] = totals[which] + product[begin : begin + 8]
        for which in range(4):
            totals_ref[which] = totals[which]

    for row in range(2):
        pl.when(lax.axis_index("row") == row)(lambda row=row: work(row))


def finish_kernel(
    face_ref,
    beyond_ref,
    totals_ref,
    first_ref,
    inv_ref,
    lon_ref,
    lat_ref,
    image_ref,
    second_ref,
    image2_ref,
    sums_ref,
    changes_ref,
):
    every, spread, width = inv_ref.shape
    cells = spread - 8

    def strip(value):
        return jnp.concatenate([value[cells - 8 :], value[:8]], axis=0)

    def total_up(totals):
        lane = lax.broadcasted_iota(jnp.int32, (8, width), 1)
        packed = jnp.zeros((8, width), jnp.float32)
        for which, total in enumerate(totals):
            packed = jnp.where(lane == which, jnp.sum(total, axis=1, keepdims=True), packed)
        sums_ref[...] = jnp.broadcast_to(jnp.sum(packed, axis=0, keepdims=True), sums_ref.shape)

    @pl.when(lax.axis_index("row") == 1)
    def _():
        total_up([totals_ref[which] for which in range(4)])
        changes_ref[...] = jnp.zeros(changes_ref.shape, jnp.float32)

    @pl.when(lax.axis_index("row") == 0)
    def _():
        faces = [face_ref[face : face + 1] for face in range(REACH + 1)]
        lon = (strip(lon_ref[0]), strip(lon_ref[1]))
        lat = (lat_ref[0, :1], lat_ref[1, :1])
        inv = [strip(inv_ref[layer]) for layer in range(2)]
        blank = jnp.zeros((8, width), jnp.float32)
        source = jnp.concatenate([blank, faces[0] * beyond_ref[...], blank], axis=0)
        first = {0: source * inv[0]}
        image = {0: source - neighbours(first, 0, faces, lon, lat), 1: -faces[1] * first[0]}
        second = {layer: image[layer] * inv[layer] for layer in range(2)}
        image2 = {
            layer: image[layer] - neighbours(second, layer, faces, lon, lat) for layer in range(2)
        }
        image2[2] = -faces[2] * second[1]
        changes = (image, second, image2)
        totals = [totals_ref[which] for which in range(4)]
        for layer in range(REACH):
            for side, begin in enumerate((cells - 8, 0)):
                rows = slice(begin, begin + 8)
                vectors = [first_ref[layer, rows]]
                for which, ref in enumerate((image_ref, second_ref, image2_ref)):
                    change = blank
                    if layer in changes[which]:
                        change = changes[which][layer][16 * side : 16 * side + 8]
                    changes_ref[which, layer, side] = change
                    vectors.append(ref[layer, rows] + change)
                for which in range(1, 4):
                    totals[which] = totals[which] + vectors[which - 1] * vectors[which]
        total_up(totals)


def update_kernel(
    sums_ref,
    field_ref,
    residual_ref,
    first_ref,
    image_ref,
    second_ref,
    image2_ref,
    changes_ref,
    out_ref,
    left_ref,
):
    totals = jnp.sum(sums_ref[...], axis=0, keepdims=True)
    lane = lax.broadcasted_iota(jnp.int32, totals.shape, 1)
    a, b, c, e = (
        jnp.sum(jnp.where(lane == which, totals, 0.0), axis=1, keepdims=True) for which in range(4)
    )
    alpha, gain, alpha_next = step_sizes(a, b, c, e)
    along, back = alpha + alpha_next * gain, alpha_next * alpha
    layers, cells, _ = field_ref.shape
    for layer in range(layers):
        out_ref[layer] = field_ref[layer] + (along * first_ref[layer] - back * second_ref[layer])
        left_ref[layer] = residual_ref[layer] - (along * image_ref[layer] - back * image2_ref[layer])
    for layer in range(REACH):
        for side, begin in enumerate((cells - 8, 0)):
            rows = slice(begin, begin + 8)
            image, second, image2 = (changes_ref[which, layer, side] for which in range(3))
            out_ref[layer, rows] = out_ref[layer, rows] - back * second
            left_ref[layer, rows] = left_ref[layer, rows] - (along * image - back * image2)


SMALL = pltpu.CompilerParams(vmem_limit_bytes=8 << 20)


def in_vmem(count):
    return [pl.BlockSpec(memory_space=pltpu.VMEM)] * count


def paired_body(
    magnetogram,
    col_owner,
    col_offset,
    phi_weight,
    theta_weight,
    radial_coef,
    theta_coef,
    phi_coef,
    start_field,
):
    layers, cells, width = start_field.shape
    phi_devices = lax.axis_size("phi")
    per = phi_weight.shape[0] // phi_devices // 2
    count = phi_devices * per
    columns = magnetogram.shape[0]
    every, spread = 2 * layers, cells + 8
    real, half = jnp.float32, jnp.bfloat16
    struct = jax.ShapeDtypeStruct
    in_smem = [pl.BlockSpec(memory_space=pltpu.SMEM)]

    def swap(value):
        return lax.ppermute(value, "row", [(0, 1), (1, 0)])

    inner = [(i, i ^ 1) for i in range(phi_devices)]
    outer = [(i, (i + (1 if i % 2 else -1)) % phi_devices) for i in range(phi_devices)]

    def in_hbm(value):
        return pltpu.with_memory_space_constraint(value, pltpu.HBM)

    mine, chosen = pl.pallas_call(
        column_kernel,
        compiler_params=SMALL,
        out_shape=[struct((columns, width), real), struct((count, columns), half)],
        in_specs=[pl.BlockSpec(memory_space=pltpu.HBM)] * 4,
        out_specs=in_vmem(2),
        scratch_shapes=[
            pltpu.VMEM(magnetogram.shape, half),
            pltpu.VMEM(theta_weight.shape, half),
            pltpu.VMEM((1, columns), jnp.int32),
            pltpu.VMEM((1, columns), jnp.int32),
            pltpu.SemaphoreType.DMA((4,)),
        ],
    )(
        in_hbm(magnetogram),
        in_hbm(theta_weight),
        in_hbm(col_owner.reshape(1, -1)),
        in_hbm(col_offset.reshape(1, -1)),
    )
    mine, field = lax.optimization_barrier((mine, start_field))
    sent = pl.pallas_call(
        pack_kernel,
        compiler_params=SMALL,
        out_shape=struct((2 * phi_devices, 2 * per, width), half),
        in_specs=in_vmem(3),
        out_specs=in_vmem(1)[0],
    )(mine, swap(mine), chosen)
    other = swap(field)
    sent, radial_coef, theta_coef, phi_coef, field, other, weights = lax.optimization_barrier(
        (sent, radial_coef, theta_coef, phi_coef, field, other, phi_weight.T)
    )
    got = lax.all_to_all(sent, ("phi", "row"), split_axis=0, concat_axis=0, tiled=True)
    edge = struct((every * REACH + 2 * phi_weight.shape[0] // width, width), real)
    far_edge, near_edge = pl.pallas_call(
        edge_kernel,
        compiler_params=SMALL,
        out_shape=[edge, edge],
        in_specs=in_vmem(3),
        out_specs=in_vmem(2),
    )(field, other, weights)
    far_edge, near_edge = lax.ppermute(far_edge, "phi", outer), lax.ppermute(near_edge, "phi", inner)
    lines = struct((every, spread, width), real)
    diag, inv, lon, lat, faces = pl.pallas_call(
        coef_kernel,
        compiler_params=SMALL,
        out_shape=[
            lines,
            lines,
            struct((2, spread, width), real),
            struct((2, 8, width), real),
            struct((every + 1, width), real),
        ],
        in_specs=in_smem + in_vmem(2),
        out_specs=in_vmem(5),
    )(radial_coef, theta_coef.reshape(1, width), phi_coef.reshape(-1, width))
    got, far_edge, near_edge, diag, inv, lon, lat, faces = lax.optimization_barrier(
        (got, far_edge, near_edge, diag, inv, lon, lat, faces)
    )
    own, beyond = pl.pallas_call(
        boundary_kernel,
        compiler_params=SMALL,
        out_shape=[struct((cells, width), real), struct((8, width), real)],
        in_specs=in_vmem(4),
        out_specs=in_vmem(2),
    )(got, weights, far_edge, near_edge)
    block = struct((layers, cells, width), real)
    totals, residual, first, image, second, image2 = pl.pallas_call(
        krylov_kernel,
        compiler_params=SMALL,
        out_shape=[struct((4, 8, width), real)] + [block] * 5,
        in_specs=in_vmem(10),
        out_specs=in_vmem(6),
    )(faces, own, field, other, far_edge, near_edge, diag, inv, lon, lat)
    sums, changes = pl.pallas_call(
        finish_kernel,
        compiler_params=SMALL,
        out_shape=[struct((2 * phi_devices, width), real), struct((3, REACH, 2, 8, width), real)],
        in_specs=in_vmem(10),
        out_specs=in_vmem(2),
    )(faces, swap(beyond), totals, first, inv, lon, lat, image, second, image2)
    sums = lax.all_to_all(sums, ("phi", "row"), split_axis=0, concat_axis=0, tiled=True)
    return pl.pallas_call(
        update_kernel,
        compiler_params=SMALL,
        out_shape=[block] * 2,
        in_specs=in_vmem(8),
        out_specs=in_vmem(2),
    )(sums, field, residual, first, image, second, image2, changes)


def body(*args):
    phi_weight, phi_coef, start_field = args[3], args[7], args[8]
    layers, cells, width = start_field.shape
    phi_devices = lax.axis_size("phi")
    fits = (
        lax.axis_size("row") == 2
        and phi_devices > 2
        and phi_devices % 2 == 0
        and phi_weight.shape[0] % (32 * phi_devices) == 0
        and layers >= REACH
        and cells % 8 == 0
        and cells >= 16
        and width % 128 == 0
        and phi_coef.shape[0] % width == 0
        and phi_weight.shape[0] % width == 0
        and (2 * layers * REACH) % 8 == 0
    )
    return (paired_body if fits else general_body)(*args)


def solution(mesh):
    in_specs = (
        P("phi", "row"),
        P("phi"),
        P("phi"),
        P(None, "phi"),
        P("row", None),
        P(),
        P(),
        P(),
        P("row", "phi", None),
    )
    out_specs = (P("row", "phi", None), P("row", "phi", None))
    return jax.shard_map(body, mesh=mesh, in_specs=in_specs, out_specs=out_specs, check_vma=False)
```

```python
import jax
import jax.numpy as jnp
from jax import lax
from jax.experimental import pallas as pl
from jax.experimental.pallas import tpu as pltpu
from jax.sharding import PartitionSpec as P

REACH = 3


def face_coefs(radial_coef, theta_coef, phi_coef):
    radial_mid = 0.5 * (radial_coef[:-1] + radial_coef[1:])
    radial_upper = jnp.concatenate([radial_mid, radial_coef[-1:]])
    radial_lower = jnp.concatenate([radial_coef[:1], radial_mid])
    theta_mid = 0.5 * (theta_coef[:-1] + theta_coef[1:])
    zero_one = jnp.zeros((1,), jnp.float32)
    theta_upper = jnp.concatenate([theta_mid, zero_one])
    theta_lower = jnp.concatenate([zero_one, theta_mid])
    phi_upper = 0.5 * (phi_coef + jnp.roll(phi_coef, -1))
    phi_lower = jnp.roll(phi_upper, 1)
    return (radial_upper, radial_lower, theta_upper, theta_lower, phi_upper, phi_lower)


def row_sum(value, rows):
    if rows == 2:
        return value + lax.ppermute(value, "row", [(0, 1), (1, 0)])
    return lax.psum(value, "row")


def pick(chunks, index):
    return lax.dynamic_index_in_dim(chunks, index, 0, keepdims=False)


def step_sizes(a, b, c, e):
    alpha = a / b
    beta = (alpha * alpha * c - a) / a
    gain = 1.0 + beta
    curvature = gain * gain * b - 2.0 * gain * alpha * c + alpha * alpha * e
    return alpha, gain, beta * a / curvature


def general_body(
    magnetogram,
    col_owner,
    col_offset,
    phi_weight,
    theta_weight,
    radial_coef,
    theta_coef,
    phi_coef,
    start_field,
):
    layers, cells, width = start_field.shape
    phi_devices = lax.axis_size("phi")
    rows = lax.axis_size("row")
    slots = phi_weight.shape[0]
    capacity = slots // phi_devices
    per = capacity // rows
    here = lax.axis_index("phi")
    row = lax.axis_index("row")
    above = lax.rem(here + 1, phi_devices)
    below = lax.rem(here + phi_devices - 1, phi_devices)

    climb = [(i, i + 1) for i in range(rows - 1)]
    low_layers = lax.ppermute(start_field[layers - REACH :], "row", climb)
    high_layers = lax.ppermute(start_field[:REACH], "row", [(t, s) for s, t in climb])
    window = jnp.concatenate([low_layers, start_field, high_layers], axis=0)

    columns = jnp.dot(magnetogram, theta_weight, preferred_element_type=jnp.float32)
    columns = row_sum(columns, rows)
    upper_part = lax.optimization_barrier(columns.astype(jnp.bfloat16))
    lower_part = (columns - upper_part.astype(jnp.float32)).astype(jnp.bfloat16)

    place = col_offset - row * per
    target = jnp.where((place >= 0) & (place < per), col_owner * per + place, -1)
    chosen = (target[None, :] == jnp.arange(phi_devices * per, dtype=jnp.int32)[:, None]).astype(
        jnp.bfloat16
    )
    packed = jnp.dot(chosen, upper_part, preferred_element_type=jnp.float32)
    packed = packed + jnp.dot(chosen, lower_part, preferred_element_type=jnp.float32)
    packed = packed.reshape(phi_devices, per, width)
    share = phi_weight.reshape(phi_devices, rows, per, cells)
    share = lax.dynamic_index_in_dim(share, row, 1, keepdims=False)
    share = share.reshape(phi_devices * per, cells)

    def edge(start):
        field = window[:, start : start + REACH].reshape(-1, width)
        lo = start + 1 if start else 0
        weights = share[:, lo : lo + 2].astype(jnp.float32).T.reshape(-1, width)
        return jnp.concatenate([field, weights], axis=0)

    to_above, to_below = edge(cells - REACH), edge(0)
    who = jnp.arange(phi_devices, dtype=jnp.int32)[:, None, None]
    edges = jnp.where(who == above, to_above[None], jnp.where(who == below, to_below[None], 0.0))
    sent = jnp.concatenate(
        [packed, jnp.roll(packed, 1, axis=0), jnp.roll(packed, -1, axis=0), edges], axis=1
    )
    got = lax.all_to_all(sent, "phi", split_axis=0, concat_axis=0, tiled=True)
    edge_low, edge_high = pick(got, below)[3 * per :], pick(got, above)[3 * per :]
    reach_rows = window.shape[0] * REACH

    def weigh(weights, which):
        data = got[:, which * per : (which + 1) * per].reshape(phi_devices * per, width)
        part = lax.optimization_barrier(data.astype(jnp.bfloat16))
        rest = (data - part.astype(jnp.float32)).astype(jnp.bfloat16)
        total = jnp.dot(weights, part, preferred_element_type=jnp.float32)
        return total + jnp.dot(weights, rest, preferred_element_type=jnp.float32)

    def ghost_weights(edge_rows):
        return edge_rows[reach_rows:].reshape(2, phi_devices * per).astype(jnp.bfloat16)

    boundary = row_sum(
        jnp.concatenate(
            [
                weigh(ghost_weights(edge_low), 1),
                weigh(share.T, 0),
                weigh(ghost_weights(edge_high), 2),
            ],
            axis=0,
        ),
        rows,
    )
    field = jnp.concatenate(
        [
            edge_low[:reach_rows].reshape(-1, REACH, width),
            window,
            edge_high[:reach_rows].reshape(-1, REACH, width),
        ],
        axis=1,
    )

    faces = face_coefs(radial_coef, theta_coef, phi_coef)
    spread = layers + 2 * REACH

    def radial_window(coef):
        padded = jnp.pad(coef, (REACH, REACH))
        return lax.dynamic_slice_in_dim(padded, row * layers, spread)[:, None, None]

    def phi_window(coef):
        padded = jnp.concatenate([coef[-REACH:], coef, coef[:REACH]])
        return lax.dynamic_slice_in_dim(padded, here * cells, cells + 2 * REACH)[None, :, None]

    rad_upper, rad_lower = radial_window(faces[0]), radial_window(faces[1])
    lon_upper, lon_lower = phi_window(faces[4]), phi_window(faces[5])
    lat_upper, lat_lower = faces[2][None, None, :], faces[3][None, None, :]
    inside = radial_window(jnp.ones_like(radial_coef))
    inv_diag = inside / (
        rad_upper + rad_lower + lat_upper + lat_lower + lon_upper + lon_lower + (1.0 - inside)
    )

    def apply_operator(value, depth):
        mid = value[1:-1, 1:-1]
        theta_pad = jnp.pad(mid, ((0, 0), (0, 0), (1, 1)))
        result = rad_upper[depth:-depth] * (mid - value[2:, 1:-1])
        result = result + rad_lower[depth:-depth] * (mid - value[:-2, 1:-1])
        result = result + lat_upper * (mid - theta_pad[:, :, 2:])
        result = result + lat_lower * (mid - theta_pad[:, :, :-2])
        result = result + lon_upper[:, depth:-depth] * (mid - value[1:-1, 2:])
        return result + lon_lower[:, depth:-depth] * (mid - value[1:-1, :-2])

    def inner(value, by):
        return value[by:-by, by:-by] if by else value

    level = row * layers - REACH + 1 + jnp.arange(spread - 2, dtype=jnp.int32)[:, None, None]
    source = jnp.where(level == 0, (faces[1][0] * boundary)[None], 0.0)
    residual = source - apply_operator(field, 1)
    first = residual * inner(inv_diag, 1)
    first_image = apply_operator(first, 2)
    second = first_image * inner(inv_diag, 2)
    second_image = apply_operator(second, 3)
    residual, first = inner(residual, 2), inner(first, 2)
    first_image, second = inner(first_image, 1), inner(second, 1)

    pairs = (
        (residual, first),
        (first, first_image),
        (first_image, second),
        (second, second_image),
    )
    sums = jnp.stack([jnp.sum(u * v, axis=(0, 1)) for u, v in pairs] * 2)
    devices = phi_devices * rows
    if devices <= 64:
        shared = jnp.broadcast_to(sums[None], (devices,) + sums.shape)
        shared = lax.all_to_all(shared, ("phi", "row"), split_axis=0, concat_axis=0, tiled=True)
        totals = jnp.sum(shared, axis=(0, 2))
    else:
        totals = lax.psum(jnp.sum(sums, axis=1), ("phi", "row"))
    alpha, gain, alpha_next = step_sizes(totals[0], totals[1], totals[2], totals[3])
    direction = gain * first - alpha * second
    solution_field = start_field + alpha * first + alpha_next * direction
    image = gain * first_image - alpha * second_image
    return solution_field, residual - alpha * first_image - alpha_next * image


def high_low(value):
    high = value.astype(jnp.bfloat16)
    return high, (value - high.astype(jnp.float32)).astype(jnp.bfloat16)


def column_kernel(
    mag_hbm,
    theta_hbm,
    owner_hbm,
    offset_hbm,
    out_ref,
    chosen_ref,
    mag_ref,
    theta_ref,
    owner_ref,
    offset_ref,
    done,
):
    pairs = (
        (theta_hbm, theta_ref),
        (mag_hbm, mag_ref),
        (owner_hbm, owner_ref),
        (offset_hbm, offset_ref),
    )
    copies = [pltpu.make_async_copy(*pair, done.at[at]) for at, pair in enumerate(pairs)]
    for copy in copies:
        copy.start()
    for copy in copies:
        copy.wait()
    out_ref[...] = jnp.dot(mag_ref[...], theta_ref[...], preferred_element_type=jnp.float32)
    per = chosen_ref.shape[0] // lax.axis_size("phi")
    place = offset_ref[...] - lax.axis_index("row") * per
    target = jnp.where((place >= 0) & (place < per), owner_ref[...] * per + place, -1)
    slot = lax.broadcasted_iota(jnp.int32, chosen_ref.shape, 0)
    chosen_ref[...] = jnp.where(slot == target, 1.0, 0.0).astype(jnp.bfloat16)


def pack_kernel(mine_ref, mag_ref, theta_ref, chosen_ref, out_ref):
    targets, rows, width = out_ref.shape
    devices, per = targets // 2, rows // 2
    other = jnp.dot(mag_ref[...], theta_ref[...], preferred_element_type=jnp.float32)
    high, low = high_low(mine_ref[...] + other)
    packed = jnp.dot(
        chosen_ref[...], jnp.concatenate([high, low], axis=1), preferred_element_type=jnp.float32
    ).astype(jnp.bfloat16)
    high = packed[:, :width].reshape(devices, per, width)
    low = packed[:, width:].reshape(devices, per, width)
    for to in range(devices):
        out_ref[2 * to, :per] = high[to]
        out_ref[2 * to, per:] = low[to]
        out_ref[2 * to + 1, :per] = high[(to - 1) % devices]
        out_ref[2 * to + 1, per:] = high[(to + 1) % devices]


def is_odd():
    return lax.rem(lax.axis_index("phi"), 2) == 1


def edge_kernel(field_ref, other_ref, weight_ref, far_ref, near_ref):
    layers, cells, width = field_ref.shape
    slots = weight_ref.shape[1]
    odd = is_odd()
    first = lax.axis_index("row") == 0

    def put(at, up, down):
        far_ref[at : at + up.shape[0]] = jnp.where(odd, up, down)
        near_ref[at : at + up.shape[0]] = jnp.where(odd, down, up)

    for layer in range(layers):
        up = [ref[layer, cells - REACH :] for ref in (field_ref, other_ref)]
        down = [ref[layer, :REACH] for ref in (field_ref, other_ref)]
        put(layer * REACH, jnp.where(first, *up), jnp.where(first, *down))
        put((layers + layer) * REACH, jnp.where(first, *up[::-1]), jnp.where(first, *down[::-1]))
    up = weight_ref[cells - 16 :].astype(jnp.float32)[14:]
    down = weight_ref[:16].astype(jnp.float32)[:2]
    for part in range(slots // width):
        piece = slice(part * width, (part + 1) * width)
        put(2 * layers * REACH + 2 * part, up[:, piece], down[:, piece])


def sides(far_ref, near_ref):
    odd = is_odd()
    return (
        jnp.where(odd, far_ref[...], near_ref[...]),
        jnp.where(odd, near_ref[...], far_ref[...]),
    )


def coef_kernel(
    radial_ref, theta_ref, phi_ref, diag_ref, inv_ref, lon_ref, lat_ref, face_ref
):
    layers, spread, width = inv_ref.shape
    cells = spread - 8
    chunks = phi_ref.shape[0]
    total = chunks * width
    row = lax.broadcasted_iota(jnp.int32, (spread, width), 0)
    lane = lax.broadcasted_iota(jnp.int32, (spread, width), 1)
    cell = lax.axis_index("phi") * cells + jnp.where(row < cells + 4, row, row - spread)
    cell = jnp.where(cell < 0, cell + total, jnp.where(cell >= total, cell - total, cell))
    found = jnp.zeros((spread, width), jnp.float32)
    for chunk in range(chunks):
        found = found + jnp.where(lane + chunk * width == cell, phi_ref[chunk : chunk + 1], 0.0)
    column = jnp.broadcast_to(jnp.sum(found, axis=1, keepdims=True), (spread, width))
    lon_ref[0] = 0.5 * (column + pltpu.roll(column, spread - 1, 0))
    lon_ref[1] = 0.5 * (column + pltpu.roll(column, 1, 0))
    theta = jnp.broadcast_to(theta_ref[...], (8, width))
    ends = lax.broadcasted_iota(jnp.int32, (8, width), 1)
    upper = jnp.where(ends == width - 1, 0.0, 0.5 * (theta + pltpu.roll(theta, width - 1, 1)))
    lower = jnp.where(ends == 0, 0.0, 0.5 * (theta + pltpu.roll(theta, 1, 1)))
    lat_ref[0], lat_ref[1] = upper, lower
    flat = lon_ref[0] + lon_ref[1] + (upper + lower)[:1]
    faces = [
        0.5 * (radial_ref[max(face - 1, 0)] + radial_ref[min(face, layers - 1)])
        for face in range(layers + 1)
    ]
    for face in range(layers + 1):
        face_ref[face : face + 1] = jnp.full((1, width), faces[face], jnp.float32)
    for layer in range(layers):
        diag = flat + (faces[layer] + faces[layer + 1])
        diag_ref[layer] = diag
        inv_ref[layer] = 1.0 / diag


def boundary_kernel(got_ref, weight_ref, far_ref, near_ref, own_ref, beyond_ref):
    sources, rows, width = got_ref.shape
    cells, slots = weight_ref.shape
    per = rows // 2

    def product(weights):
        data = [got_ref[:, :per].reshape(slots, width), got_ref[:, per:].reshape(slots, width)]
        total = jnp.dot(
            weights, jnp.concatenate(data, axis=1), preferred_element_type=jnp.float32
        )
        return total[:, :width], total[:, width:]

    @pl.when(lax.axis_index("row") == 0)
    def _():
        high, low = product(weight_ref[...])
        own_ref[...] = high + low
        beyond_ref[...] = jnp.zeros(beyond_ref.shape, jnp.float32)

    @pl.when(lax.axis_index("row") == 1)
    def _():
        above, below = sides(far_ref, near_ref)

        def edge_weights(edge):
            at = edge.shape[0] - 2 * slots // width
            parts = [edge[at + 2 * k : at + 2 * k + 2] for k in range(slots // width)]
            return jnp.concatenate(parts, axis=1)

        weights = jnp.concatenate(
            [edge_weights(above), jnp.zeros((4, slots), jnp.float32), edge_weights(below)], axis=0
        )
        from_below, from_above = product(weights.astype(jnp.bfloat16))
        row = lax.broadcasted_iota(jnp.int32, (8, width), 0)
        own_ref[...] = jnp.zeros(own_ref.shape, jnp.float32)
        beyond_ref[...] = jnp.where(row < 4, from_above, from_below)


def neighbours(values, layer, faces, lon, lat):
    mid = values[layer]
    spread, width = mid.shape
    total = lat[0] * pltpu.roll(mid, width - 1, 1) + lat[1] * pltpu.roll(mid, 1, 1)
    total = total + lon[0] * pltpu.roll(mid, spread - 1, 0)
    total = total + lon[1] * pltpu.roll(mid, 1, 0)
    for at, face in ((layer - 1, layer), (layer + 1, layer + 1)):
        if at in values:
            total = total + faces[face] * values[at]
    return total


def krylov_kernel(
    face_ref,
    own_ref,
    field_ref,
    other_ref,
    far_ref,
    near_ref,
    diag_ref,
    inv_ref,
    lon_ref,
    lat_ref,
    totals_ref,
    *vector_refs,
):
    layers, cells, width = field_ref.shape
    every, spread, _ = inv_ref.shape
    above, below = sides(far_ref, near_ref)
    gap = jnp.zeros((8 - 2 * REACH, width), jnp.float32)

    def work(row):
        faces = [face_ref[face : face + 1] for face in range(every + 1)]
        lon, lat = (lon_ref[0], lon_ref[1]), (lat_ref[0, :1], lat_ref[1, :1])
        halves = (other_ref, field_ref) if row else (field_ref, other_ref)
        field = {}
        for layer in range(every):
            part = slice(layer * REACH, (layer + 1) * REACH)
            block = halves[layer // layers][layer % layers]
            field[layer] = jnp.concatenate([block, above[part], gap, below[part]], axis=0)
        residual, first, image, second = {}, {}, {}, {}
        start = row * (layers - 2)
        for layer in range(start, start + layers + 2):
            value = neighbours(field, layer, faces, lon, lat) - diag_ref[layer] * field[layer]
            if layer == 0:
                source = jnp.concatenate([own_ref[...], jnp.zeros((8, width), jnp.float32)], axis=0)
                value = value + faces[0] * source
            residual[layer] = value
            first[layer] = value * inv_ref[layer]
        start = row * (layers - 1)
        for layer in range(start, start + layers + 1):
            image[layer] = residual[layer] - neighbours(first, layer, faces, lon, lat)
            second[layer] = image[layer] * inv_ref[layer]
        totals = [jnp.zeros((8, width), jnp.float32)] * 4
        for at in range(layers):
            layer = row * layers + at
            image2 = image[layer] - neighbours(second, layer, faces, lon, lat)
            vectors = (residual[layer], first[layer], image[layer], second[layer], image2)
            vectors = [vector[:cells] for vector in vectors]
            for ref, vector in zip(vector_refs, vectors):
                ref[at] = vector
            for which in range(4):
                product = vectors[which] * vectors[which + 1]
                for begin in range(0, cells, 8):
                    later = row == 0 and at < REACH and which and begin in (0, cells - 8)
                    if not later:
                        totals[which] = totals[which] + product[begin : begin + 8]
        for which in range(4):
            totals_ref[which] = totals[which]

    for row in range(2):
        pl.when(lax.axis_index("row") == row)(lambda row=row: work(row))


def finish_kernel(
    face_ref,
    beyond_ref,
    totals_ref,
    first_ref,
    inv_ref,
    lon_ref,
    lat_ref,
    image_ref,
    second_ref,
    image2_ref,
    sums_ref,
    changes_ref,
):
    every, spread, width = inv_ref.shape
    cells = spread - 8

    def strip(value):
        return jnp.concatenate([value[cells - 8 :], value[:8]], axis=0)

    def total_up(totals):
        lane = lax.broadcasted_iota(jnp.int32, (8, width), 1)
        packed = jnp.zeros((8, width), jnp.float32)
        for which, total in enumerate(totals):
            packed = jnp.where(lane == which, jnp.sum(total, axis=1, keepdims=True), packed)
        sums_ref[...] = jnp.broadcast_to(jnp.sum(packed, axis=0, keepdims=True), sums_ref.shape)

    @pl.when(lax.axis_index("row") == 1)
    def _():
        total_up([totals_ref[which] for which in range(4)])
        changes_ref[...] = jnp.zeros(changes_ref.shape, jnp.float32)

    @pl.when(lax.axis_index("row") == 0)
    def _():
        faces = [face_ref[face : face + 1] for face in range(REACH + 1)]
        lon = (strip(lon_ref[0]), strip(lon_ref[1]))
        lat = (lat_ref[0, :1], lat_ref[1, :1])
        inv = [strip(inv_ref[layer]) for layer in range(2)]
        blank = jnp.zeros((8, width), jnp.float32)
        source = jnp.concatenate([blank, faces[0] * beyond_ref[...], blank], axis=0)
        first = {0: source * inv[0]}
        image = {0: source - neighbours(first, 0, faces, lon, lat), 1: -faces[1] * first[0]}
        second = {layer: image[layer] * inv[layer] for layer in range(2)}
        image2 = {
            layer: image[layer] - neighbours(second, layer, faces, lon, lat) for layer in range(2)
        }
        image2[2] = -faces[2] * second[1]
        changes = (image, second, image2)
        totals = [totals_ref[which] for which in range(4)]
        for layer in range(REACH):
            for side, begin in enumerate((cells - 8, 0)):
                rows = slice(begin, begin + 8)
                vectors = [first_ref[layer, rows]]
                for which, ref in enumerate((image_ref, second_ref, image2_ref)):
                    change = blank
                    if layer in changes[which]:
                        change = changes[which][layer][16 * side : 16 * side + 8]
                    changes_ref[which, layer, side] = change
                    vectors.append(ref[layer, rows] + change)
                for which in range(1, 4):
                    totals[which] = totals[which] + vectors[which - 1] * vectors[which]
        total_up(totals)


def update_kernel(
    sums_ref,
    field_ref,
    residual_ref,
    first_ref,
    image_ref,
    second_ref,
    image2_ref,
    changes_ref,
    out_ref,
    left_ref,
):
    totals = jnp.sum(sums_ref[...], axis=0, keepdims=True)
    lane = lax.broadcasted_iota(jnp.int32, totals.shape, 1)
    a, b, c, e = (
        jnp.sum(jnp.where(lane == which, totals, 0.0), axis=1, keepdims=True) for which in range(4)
    )
    alpha, gain, alpha_next = step_sizes(a, b, c, e)
    along, back = alpha + alpha_next * gain, alpha_next * alpha
    layers, cells, _ = field_ref.shape
    for layer in range(layers):
        out_ref[layer] = field_ref[layer] + (along * first_ref[layer] - back * second_ref[layer])
        left_ref[layer] = residual_ref[layer] - (along * image_ref[layer] - back * image2_ref[layer])
    for layer in range(REACH):
        for side, begin in enumerate((cells - 8, 0)):
            rows = slice(begin, begin + 8)
            image, second, image2 = (changes_ref[which, layer, side] for which in range(3))
            out_ref[layer, rows] = out_ref[layer, rows] - back * second
            left_ref[layer, rows] = left_ref[layer, rows] - (along * image - back * image2)


SMALL = pltpu.CompilerParams(vmem_limit_bytes=8 << 20)


def in_vmem(count):
    return [pl.BlockSpec(memory_space=pltpu.VMEM)] * count


def paired_body(
    magnetogram,
    col_owner,
    col_offset,
    phi_weight,
    theta_weight,
    radial_coef,
    theta_coef,
    phi_coef,
    start_field,
):
    layers, cells, width = start_field.shape
    phi_devices = lax.axis_size("phi")
    per = phi_weight.shape[0] // phi_devices // 2
    count = phi_devices * per
    columns = magnetogram.shape[0]
    every, spread = 2 * layers, cells + 8
    real, half = jnp.float32, jnp.bfloat16
    struct = jax.ShapeDtypeStruct
    in_smem = [pl.BlockSpec(memory_space=pltpu.SMEM)]

    def swap(value):
        return lax.ppermute(value, "row", [(0, 1), (1, 0)])

    inner = [(i, i ^ 1) for i in range(phi_devices)]
    outer = [(i, (i + (1 if i % 2 else -1)) % phi_devices) for i in range(phi_devices)]

    def in_hbm(value):
        return pltpu.with_memory_space_constraint(value, pltpu.HBM)

    mine, chosen = pl.pallas_call(
        column_kernel,
        compiler_params=SMALL,
        out_shape=[struct((columns, width), real), struct((count, columns), half)],
        in_specs=[pl.BlockSpec(memory_space=pltpu.HBM)] * 4,
        out_specs=in_vmem(2),
        scratch_shapes=[
            pltpu.VMEM(magnetogram.shape, half),
            pltpu.VMEM(theta_weight.shape, half),
            pltpu.VMEM((1, columns), jnp.int32),
            pltpu.VMEM((1, columns), jnp.int32),
            pltpu.SemaphoreType.DMA((4,)),
        ],
    )(
        in_hbm(magnetogram),
        in_hbm(theta_weight),
        in_hbm(col_owner.reshape(1, -1)),
        in_hbm(col_offset.reshape(1, -1)),
    )
    partner = swap(magnetogram), swap(theta_weight)
    other = swap(start_field)
    sent = pl.pallas_call(
        pack_kernel,
        compiler_params=SMALL,
        out_shape=struct((2 * phi_devices, 2 * per, width), half),
        in_specs=in_vmem(4),
        out_specs=in_vmem(1)[0],
    )(mine, *partner, chosen)
    sent, radial_coef, theta_coef, phi_coef, field, other, weights = lax.optimization_barrier(
        (sent, radial_coef, theta_coef, phi_coef, start_field, other, phi_weight.T)
    )
    got = lax.all_to_all(sent, ("phi", "row"), split_axis=0, concat_axis=0, tiled=True)
    edge = struct((every * REACH + 2 * phi_weight.shape[0] // width, width), real)
    far_edge, near_edge = pl.pallas_call(
        edge_kernel,
        compiler_params=SMALL,
        out_shape=[edge, edge],
        in_specs=in_vmem(3),
        out_specs=in_vmem(2),
    )(field, other, weights)
    far_edge, near_edge = lax.ppermute(far_edge, "phi", outer), lax.ppermute(near_edge, "phi", inner)
    lines = struct((every, spread, width), real)
    diag, inv, lon, lat, faces = pl.pallas_call(
        coef_kernel,
        compiler_params=SMALL,
        out_shape=[
            lines,
            lines,
            struct((2, spread, width), real),
            struct((2, 8, width), real),
            struct((every + 1, width), real),
        ],
        in_specs=in_smem + in_vmem(2),
        out_specs=in_vmem(5),
    )(radial_coef, theta_coef.reshape(1, width), phi_coef.reshape(-1, width))
    got, far_edge, near_edge, diag, inv, lon, lat, faces = lax.optimization_barrier(
        (got, far_edge, near_edge, diag, inv, lon, lat, faces)
    )
    own, beyond = pl.pallas_call(
        boundary_kernel,
        compiler_params=SMALL,
        out_shape=[struct((cells, width), real), struct((8, width), real)],
        in_specs=in_vmem(4),
        out_specs=in_vmem(2),
    )(got, weights, far_edge, near_edge)
    block = struct((layers, cells, width), real)
    totals, residual, first, image, second, image2 = pl.pallas_call(
        krylov_kernel,
        compiler_params=SMALL,
        out_shape=[struct((4, 8, width), real)] + [block] * 5,
        in_specs=in_vmem(10),
        out_specs=in_vmem(6),
    )(faces, own, field, other, far_edge, near_edge, diag, inv, lon, lat)
    sums, changes = pl.pallas_call(
        finish_kernel,
        compiler_params=SMALL,
        out_shape=[struct((2 * phi_devices, width), real), struct((3, REACH, 2, 8, width), real)],
        in_specs=in_vmem(10),
        out_specs=in_vmem(2),
    )(faces, swap(beyond), totals, first, inv, lon, lat, image, second, image2)
    sums = lax.all_to_all(sums, ("phi", "row"), split_axis=0, concat_axis=0, tiled=True)
    return pl.pallas_call(
        update_kernel,
        compiler_params=SMALL,
        out_shape=[block] * 2,
        in_specs=in_vmem(8),
        out_specs=in_vmem(2),
    )(sums, field, residual, first, image, second, image2, changes)


def body(*args):
    phi_weight, phi_coef, start_field = args[3], args[7], args[8]
    layers, cells, width = start_field.shape
    phi_devices = lax.axis_size("phi")
    fits = (
        lax.axis_size("row") == 2
        and phi_devices > 2
        and phi_devices % 2 == 0
        and phi_weight.shape[0] % (32 * phi_devices) == 0
        and layers >= REACH
        and cells % 8 == 0
        and cells >= 16
        and width % 128 == 0
        and phi_coef.shape[0] % width == 0
        and phi_weight.shape[0] % width == 0
        and (2 * layers * REACH) % 8 == 0
    )
    return (paired_body if fits else general_body)(*args)


def solution(mesh):
    in_specs = (
        P("phi", "row"),
        P("phi"),
        P("phi"),
        P(None, "phi"),
        P("row", None),
        P(),
        P(),
        P(),
        P("row", "phi", None),
    )
    out_specs = (P("row", "phi", None), P("row", "phi", None))
    return jax.shard_map(body, mesh=mesh, in_specs=in_specs, out_specs=out_specs, check_vma=False)
```

```python
import jax
import jax.numpy as jnp
from jax import lax
from jax.experimental import pallas as pl
from jax.experimental.pallas import tpu as pltpu
from jax.sharding import PartitionSpec as P

REACH = 3


def face_coefs(radial_coef, theta_coef, phi_coef):
    radial_mid = 0.5 * (radial_coef[:-1] + radial_coef[1:])
    radial_upper = jnp.concatenate([radial_mid, radial_coef[-1:]])
    radial_lower = jnp.concatenate([radial_coef[:1], radial_mid])
    theta_mid = 0.5 * (theta_coef[:-1] + theta_coef[1:])
    zero_one = jnp.zeros((1,), jnp.float32)
    theta_upper = jnp.concatenate([theta_mid, zero_one])
    theta_lower = jnp.concatenate([zero_one, theta_mid])
    phi_upper = 0.5 * (phi_coef + jnp.roll(phi_coef, -1))
    phi_lower = jnp.roll(phi_upper, 1)
    return (radial_upper, radial_lower, theta_upper, theta_lower, phi_upper, phi_lower)


def row_sum(value, rows):
    if rows == 2:
        return value + lax.ppermute(value, "row", [(0, 1), (1, 0)])
    return lax.psum(value, "row")


def pick(chunks, index):
    return lax.dynamic_index_in_dim(chunks, index, 0, keepdims=False)


def step_sizes(a, b, c, e):
    alpha = a / b
    beta = (alpha * alpha * c - a) / a
    gain = 1.0 + beta
    curvature = gain * gain * b - 2.0 * gain * alpha * c + alpha * alpha * e
    return alpha, gain, beta * a / curvature


def general_body(
    magnetogram,
    col_owner,
    col_offset,
    phi_weight,
    theta_weight,
    radial_coef,
    theta_coef,
    phi_coef,
    start_field,
):
    layers, cells, width = start_field.shape
    phi_devices = lax.axis_size("phi")
    rows = lax.axis_size("row")
    slots = phi_weight.shape[0]
    capacity = slots // phi_devices
    per = capacity // rows
    here = lax.axis_index("phi")
    row = lax.axis_index("row")
    above = lax.rem(here + 1, phi_devices)
    below = lax.rem(here + phi_devices - 1, phi_devices)

    climb = [(i, i + 1) for i in range(rows - 1)]
    low_layers = lax.ppermute(start_field[layers - REACH :], "row", climb)
    high_layers = lax.ppermute(start_field[:REACH], "row", [(t, s) for s, t in climb])
    window = jnp.concatenate([low_layers, start_field, high_layers], axis=0)

    columns = jnp.dot(magnetogram, theta_weight, preferred_element_type=jnp.float32)
    columns = row_sum(columns, rows)
    upper_part = lax.optimization_barrier(columns.astype(jnp.bfloat16))
    lower_part = (columns - upper_part.astype(jnp.float32)).astype(jnp.bfloat16)

    place = col_offset - row * per
    target = jnp.where((place >= 0) & (place < per), col_owner * per + place, -1)
    chosen = (target[None, :] == jnp.arange(phi_devices * per, dtype=jnp.int32)[:, None]).astype(
        jnp.bfloat16
    )
    packed = jnp.dot(chosen, upper_part, preferred_element_type=jnp.float32)
    packed = packed + jnp.dot(chosen, lower_part, preferred_element_type=jnp.float32)
    packed = packed.reshape(phi_devices, per, width)
    share = phi_weight.reshape(phi_devices, rows, per, cells)
    share = lax.dynamic_index_in_dim(share, row, 1, keepdims=False)
    share = share.reshape(phi_devices * per, cells)

    def edge(start):
        field = window[:, start : start + REACH].reshape(-1, width)
        lo = start + 1 if start else 0
        weights = share[:, lo : lo + 2].astype(jnp.float32).T.reshape(-1, width)
        return jnp.concatenate([field, weights], axis=0)

    to_above, to_below = edge(cells - REACH), edge(0)
    who = jnp.arange(phi_devices, dtype=jnp.int32)[:, None, None]
    edges = jnp.where(who == above, to_above[None], jnp.where(who == below, to_below[None], 0.0))
    sent = jnp.concatenate(
        [packed, jnp.roll(packed, 1, axis=0), jnp.roll(packed, -1, axis=0), edges], axis=1
    )
    got = lax.all_to_all(sent, "phi", split_axis=0, concat_axis=0, tiled=True)
    edge_low, edge_high = pick(got, below)[3 * per :], pick(got, above)[3 * per :]
    reach_rows = window.shape[0] * REACH

    def weigh(weights, which):
        data = got[:, which * per : (which + 1) * per].reshape(phi_devices * per, width)
        part = lax.optimization_barrier(data.astype(jnp.bfloat16))
        rest = (data - part.astype(jnp.float32)).astype(jnp.bfloat16)
        total = jnp.dot(weights, part, preferred_element_type=jnp.float32)
        return total + jnp.dot(weights, rest, preferred_element_type=jnp.float32)

    def ghost_weights(edge_rows):
        return edge_rows[reach_rows:].reshape(2, phi_devices * per).astype(jnp.bfloat16)

    boundary = row_sum(
        jnp.concatenate(
            [
                weigh(ghost_weights(edge_low), 1),
                weigh(share.T, 0),
                weigh(ghost_weights(edge_high), 2),
            ],
            axis=0,
        ),
        rows,
    )
    field = jnp.concatenate(
        [
            edge_low[:reach_rows].reshape(-1, REACH, width),
            window,
            edge_high[:reach_rows].reshape(-1, REACH, width),
        ],
        axis=1,
    )

    faces = face_coefs(radial_coef, theta_coef, phi_coef)
    spread = layers + 2 * REACH

    def radial_window(coef):
        padded = jnp.pad(coef, (REACH, REACH))
        return lax.dynamic_slice_in_dim(padded, row * layers, spread)[:, None, None]

    def phi_window(coef):
        padded = jnp.concatenate([coef[-REACH:], coef, coef[:REACH]])
        return lax.dynamic_slice_in_dim(padded, here * cells, cells + 2 * REACH)[None, :, None]

    rad_upper, rad_lower = radial_window(faces[0]), radial_window(faces[1])
    lon_upper, lon_lower = phi_window(faces[4]), phi_window(faces[5])
    lat_upper, lat_lower = faces[2][None, None, :], faces[3][None, None, :]
    inside = radial_window(jnp.ones_like(radial_coef))
    inv_diag = inside / (
        rad_upper + rad_lower + lat_upper + lat_lower + lon_upper + lon_lower + (1.0 - inside)
    )

    def apply_operator(value, depth):
        mid = value[1:-1, 1:-1]
        theta_pad = jnp.pad(mid, ((0, 0), (0, 0), (1, 1)))
        result = rad_upper[depth:-depth] * (mid - value[2:, 1:-1])
        result = result + rad_lower[depth:-depth] * (mid - value[:-2, 1:-1])
        result = result + lat_upper * (mid - theta_pad[:, :, 2:])
        result = result + lat_lower * (mid - theta_pad[:, :, :-2])
        result = result + lon_upper[:, depth:-depth] * (mid - value[1:-1, 2:])
        return result + lon_lower[:, depth:-depth] * (mid - value[1:-1, :-2])

    def inner(value, by):
        return value[by:-by, by:-by] if by else value

    level = row * layers - REACH + 1 + jnp.arange(spread - 2, dtype=jnp.int32)[:, None, None]
    source = jnp.where(level == 0, (faces[1][0] * boundary)[None], 0.0)
    residual = source - apply_operator(field, 1)
    first = residual * inner(inv_diag, 1)
    first_image = apply_operator(first, 2)
    second = first_image * inner(inv_diag, 2)
    second_image = apply_operator(second, 3)
    residual, first = inner(residual, 2), inner(first, 2)
    first_image, second = inner(first_image, 1), inner(second, 1)

    pairs = (
        (residual, first),
        (first, first_image),
        (first_image, second),
        (second, second_image),
    )
    sums = jnp.stack([jnp.sum(u * v, axis=(0, 1)) for u, v in pairs] * 2)
    devices = phi_devices * rows
    if devices <= 64:
        shared = jnp.broadcast_to(sums[None], (devices,) + sums.shape)
        shared = lax.all_to_all(shared, ("phi", "row"), split_axis=0, concat_axis=0, tiled=True)
        totals = jnp.sum(shared, axis=(0, 2))
    else:
        totals = lax.psum(jnp.sum(sums, axis=1), ("phi", "row"))
    alpha, gain, alpha_next = step_sizes(totals[0], totals[1], totals[2], totals[3])
    direction = gain * first - alpha * second
    solution_field = start_field + alpha * first + alpha_next * direction
    image = gain * first_image - alpha * second_image
    return solution_field, residual - alpha * first_image - alpha_next * image


def high_low(value):
    high = value.astype(jnp.bfloat16)
    return high, (value - high.astype(jnp.float32)).astype(jnp.bfloat16)


def leader(devices):
    return devices // 2 + 1


def seat(slab, devices):
    return lax.rem(leader(devices) - slab + devices, devices)


def own_share(weights, devices):
    slots = weights.shape[1]
    per = slots // devices // 2
    slot = lax.broadcasted_iota(jnp.int32, (slots, slots // 2), 0)
    place = lax.broadcasted_iota(jnp.int32, (slots, slots // 2), 1)
    source = seat(place // per, devices)
    wanted = source * (2 * per) + lax.axis_index("row") * per + place % per
    picker = jnp.where(slot == wanted, 1.0, 0.0).astype(jnp.bfloat16)
    return jnp.dot(weights, picker, preferred_element_type=jnp.float32).astype(jnp.bfloat16)


def column_kernel(
    mag_hbm,
    theta_hbm,
    owner_hbm,
    offset_hbm,
    out_ref,
    chosen_ref,
    mag_ref,
    theta_ref,
    owner_ref,
    offset_ref,
    done,
):
    pairs = (
        (theta_hbm, theta_ref),
        (mag_hbm, mag_ref),
        (owner_hbm, owner_ref),
        (offset_hbm, offset_ref),
    )
    copies = [pltpu.make_async_copy(*pair, done.at[at]) for at, pair in enumerate(pairs)]
    for copy in copies:
        copy.start()
    for copy in copies:
        copy.wait()
    out_ref[...] = jnp.dot(mag_ref[...], theta_ref[...], preferred_element_type=jnp.float32)
    devices = lax.axis_size("phi")
    per = chosen_ref.shape[0] // devices
    place = offset_ref[...] - lax.axis_index("row") * per
    target = jnp.where((place >= 0) & (place < per), seat(owner_ref[...], devices) * per + place, -1)
    slot = lax.broadcasted_iota(jnp.int32, chosen_ref.shape, 0)
    chosen_ref[...] = jnp.where(slot == target, 1.0, 0.0).astype(jnp.bfloat16)


def pack_kernel(mine_ref, mag_ref, theta_ref, chosen_ref, out_ref):
    devices, rows, width = out_ref.shape
    per = rows // 4
    other = jnp.dot(mag_ref[...], theta_ref[...], preferred_element_type=jnp.float32)
    high, low = high_low(mine_ref[...] + other)
    packed = jnp.dot(
        chosen_ref[...], jnp.concatenate([high, low], axis=1), preferred_element_type=jnp.float32
    ).astype(jnp.bfloat16)
    high = packed[:, :width].reshape(devices, per, width)
    out_ref[:, :per] = high
    out_ref[:, per : 2 * per] = packed[:, width:].reshape(devices, per, width)
    for at in range(devices):
        out_ref[at, 2 * per : 3 * per] = high[(at + 1) % devices]
        out_ref[at, 3 * per :] = high[(at - 1) % devices]


def is_odd():
    return lax.rem(lax.axis_index("phi"), 2) == 1


def edge_kernel(field_ref, other_ref, weight_ref, far_ref, near_ref, share_ref):
    layers, cells, width = field_ref.shape
    odd = is_odd()
    first = lax.axis_index("row") == 0
    share = own_share(weight_ref[...], lax.axis_size("phi"))
    share_ref[...] = share
    weights = share.astype(jnp.float32)

    def put(at, up, down):
        far_ref[at : at + up.shape[0]] = jnp.where(odd, up, down)
        near_ref[at : at + up.shape[0]] = jnp.where(odd, down, up)

    for layer in range(layers):
        up = [ref[layer, cells - REACH :] for ref in (field_ref, other_ref)]
        down = [ref[layer, :REACH] for ref in (field_ref, other_ref)]
        put(layer * REACH, jnp.where(first, *up), jnp.where(first, *down))
        put((layers + layer) * REACH, jnp.where(first, *up[::-1]), jnp.where(first, *down[::-1]))
    for part in range(share.shape[1] // width):
        piece = weights[:, part * width : (part + 1) * width]
        put(2 * layers * REACH + 2 * part, piece[cells - 2 :], piece[:2])


def sides(far_ref, near_ref):
    odd = is_odd()
    return (
        jnp.where(odd, far_ref[...], near_ref[...]),
        jnp.where(odd, near_ref[...], far_ref[...]),
    )


def coef_kernel(
    radial_ref, theta_ref, phi_ref, diag_ref, inv_ref, lon_ref, lat_ref, face_ref
):
    layers, spread, width = inv_ref.shape
    cells = spread - 8
    chunks = phi_ref.shape[0]
    total = chunks * width
    row = lax.broadcasted_iota(jnp.int32, (spread, width), 0)
    lane = lax.broadcasted_iota(jnp.int32, (spread, width), 1)
    cell = lax.axis_index("phi") * cells + jnp.where(row < cells + 4, row, row - spread)
    cell = jnp.where(cell < 0, cell + total, jnp.where(cell >= total, cell - total, cell))
    found = jnp.zeros((spread, width), jnp.float32)
    for chunk in range(chunks):
        found = found + jnp.where(lane + chunk * width == cell, phi_ref[chunk : chunk + 1], 0.0)
    column = jnp.broadcast_to(jnp.sum(found, axis=1, keepdims=True), (spread, width))
    lon_ref[0] = 0.5 * (column + pltpu.roll(column, spread - 1, 0))
    lon_ref[1] = 0.5 * (column + pltpu.roll(column, 1, 0))
    theta = jnp.broadcast_to(theta_ref[...], (8, width))
    ends = lax.broadcasted_iota(jnp.int32, (8, width), 1)
    upper = jnp.where(ends == width - 1, 0.0, 0.5 * (theta + pltpu.roll(theta, width - 1, 1)))
    lower = jnp.where(ends == 0, 0.0, 0.5 * (theta + pltpu.roll(theta, 1, 1)))
    lat_ref[0], lat_ref[1] = upper, lower
    flat = lon_ref[0] + lon_ref[1] + (upper + lower)[:1]
    faces = [
        0.5 * (radial_ref[max(face - 1, 0)] + radial_ref[min(face, layers - 1)])
        for face in range(layers + 1)
    ]
    for face in range(layers + 1):
        face_ref[face : face + 1] = jnp.full((1, width), faces[face], jnp.float32)
    for layer in range(layers):
        diag = flat + (faces[layer] + faces[layer + 1])
        diag_ref[layer] = diag
        inv_ref[layer] = 1.0 / diag


def boundary_kernel(got_ref, share_ref, far_ref, near_ref, out_ref):
    devices, rows, width = got_ref.shape
    cells, count = share_ref.shape
    per, spread = rows // 4, cells + 8
    above, below = sides(far_ref, near_ref)
    edge_rows = above.shape[0]

    def product(weights, first):
        data = [
            got_ref[:, which * per : (which + 1) * per].reshape(count, width)
            for which in (first, first + 1)
        ]
        total = jnp.dot(weights, jnp.concatenate(data, axis=1), preferred_element_type=jnp.float32)
        return total[:, :width], total[:, width:]

    def edge_weights(edge):
        at = edge_rows - 2 * count // width
        parts = [edge[at + 2 * k : at + 2 * k + 2] for k in range(count // width)]
        return jnp.concatenate(parts, axis=1)

    high, low = product(share_ref[...], 0)
    out_ref[:cells] = high + low
    weights = jnp.concatenate(
        [edge_weights(above), jnp.zeros((4, count), jnp.float32), edge_weights(below)], axis=0
    )
    from_below, from_above = product(weights.astype(jnp.bfloat16), 2)
    row = lax.broadcasted_iota(jnp.int32, (8, width), 0)
    out_ref[cells:spread] = jnp.where(row < 4, from_above, from_below)


def neighbours(values, layer, faces, lon, lat):
    mid = values[layer]
    spread, width = mid.shape
    total = lat[0] * pltpu.roll(mid, width - 1, 1) + lat[1] * pltpu.roll(mid, 1, 1)
    total = total + lon[0] * pltpu.roll(mid, spread - 1, 0)
    total = total + lon[1] * pltpu.roll(mid, 1, 0)
    for at, face in ((layer - 1, layer), (layer + 1, layer + 1)):
        if at in values:
            total = total + faces[face] * values[at]
    return total


def krylov_kernel(
    face_ref,
    part_ref,
    rest_ref,
    field_ref,
    other_ref,
    far_ref,
    near_ref,
    diag_ref,
    inv_ref,
    lon_ref,
    lat_ref,
    sums_ref,
    *vector_refs,
):
    layers, cells, width = field_ref.shape
    every, spread, _ = inv_ref.shape
    above, below = sides(far_ref, near_ref)
    gap = jnp.zeros((8 - 2 * REACH, width), jnp.float32)
    upper = lax.axis_index("row") == 1
    faces = [face_ref[face : face + 1] for face in range(every + 1)]
    lon, lat = (lon_ref[0], lon_ref[1]), (lat_ref[0, :1], lat_ref[1, :1])
    field = {}
    for layer in range(every):
        edge = slice(layer * REACH, (layer + 1) * REACH)
        at, high = layer % layers, layer >= layers
        block = jnp.where(upper == high, field_ref[at], other_ref[at])
        field[layer] = jnp.concatenate([block, above[edge], gap, below[edge]], axis=0)
    residual, first, image, second, image2 = {}, {}, {}, {}, {}
    for layer in range(every):
        value = neighbours(field, layer, faces, lon, lat) - diag_ref[layer] * field[layer]
        if layer == 0:
            value = value + faces[0] * (part_ref[...] + rest_ref[...])
        residual[layer] = value
        first[layer] = value * inv_ref[layer]
    for layer in range(every):
        image[layer] = residual[layer] - neighbours(first, layer, faces, lon, lat)
        second[layer] = image[layer] * inv_ref[layer]
    totals = [jnp.zeros((8, width), jnp.float32)] * 4
    for layer in range(every):
        image2[layer] = image[layer] - neighbours(second, layer, faces, lon, lat)
        vectors = [each[layer] for each in (residual, first, image, second, image2)]
        for which in range(4):
            product = vectors[which] * vectors[which + 1]
            for begin in range(0, cells, 8):
                totals[which] = totals[which] + product[begin : begin + 8]
    for ref, vector in zip(vector_refs, (residual, first, image, second, image2)):
        for at in range(layers):
            ref[at] = jnp.where(upper, vector[layers + at], vector[at])[:cells]
    lane = lax.broadcasted_iota(jnp.int32, (8, width), 1)
    packed = jnp.zeros((8, width), jnp.float32)
    for which, total in enumerate(totals):
        packed = jnp.where(lane == which, jnp.sum(total, axis=1, keepdims=True), packed)
    sums_ref[...] = jnp.broadcast_to(jnp.sum(packed, axis=0, keepdims=True), sums_ref.shape)


def update_kernel(
    sums_ref,
    field_ref,
    residual_ref,
    first_ref,
    image_ref,
    second_ref,
    image2_ref,
    out_ref,
    left_ref,
):
    totals = jnp.sum(sums_ref[...], axis=0, keepdims=True)
    lane = lax.broadcasted_iota(jnp.int32, totals.shape, 1)
    a, b, c, e = (
        jnp.sum(jnp.where(lane == which, totals, 0.0), axis=1, keepdims=True) for which in range(4)
    )
    alpha, gain, alpha_next = step_sizes(a, b, c, e)
    along, back = alpha + alpha_next * gain, alpha_next * alpha
    for layer in range(field_ref.shape[0]):
        out_ref[layer] = field_ref[layer] + (along * first_ref[layer] - back * second_ref[layer])
        left_ref[layer] = residual_ref[layer] - (along * image_ref[layer] - back * image2_ref[layer])


SMALL = pltpu.CompilerParams(vmem_limit_bytes=8 << 20)


def in_vmem(count):
    return [pl.BlockSpec(memory_space=pltpu.VMEM)] * count


def paired_body(
    magnetogram,
    col_owner,
    col_offset,
    phi_weight,
    theta_weight,
    radial_coef,
    theta_coef,
    phi_coef,
    start_field,
):
    layers, cells, width = start_field.shape
    phi_devices = lax.axis_size("phi")
    per = phi_weight.shape[0] // phi_devices // 2
    count = phi_devices * per
    columns = magnetogram.shape[0]
    every, spread = 2 * layers, cells + 8
    real, half = jnp.float32, jnp.bfloat16
    struct = jax.ShapeDtypeStruct
    in_smem = [pl.BlockSpec(memory_space=pltpu.SMEM)]

    def swap(value):
        return lax.ppermute(value, "row", [(0, 1), (1, 0)])

    inner = [(i, i ^ 1) for i in range(phi_devices)]
    outer = [(i, (i + (1 if i % 2 else -1)) % phi_devices) for i in range(phi_devices)]

    order = [(leader(phi_devices) - i) % phi_devices for i in range(phi_devices)]

    def over_slabs(value):
        return lax.all_to_all(
            value, "phi", split_axis=0, concat_axis=0, axis_index_groups=[order], tiled=True
        )

    def in_hbm(value):
        return pltpu.with_memory_space_constraint(value, pltpu.HBM)

    mine, chosen = pl.pallas_call(
        column_kernel,
        compiler_params=SMALL,
        out_shape=[struct((columns, width), real), struct((count, columns), half)],
        in_specs=[pl.BlockSpec(memory_space=pltpu.HBM)] * 4,
        out_specs=in_vmem(2),
        scratch_shapes=[
            pltpu.VMEM(magnetogram.shape, half),
            pltpu.VMEM(theta_weight.shape, half),
            pltpu.VMEM((1, columns), jnp.int32),
            pltpu.VMEM((1, columns), jnp.int32),
            pltpu.SemaphoreType.DMA((4,)),
        ],
    )(
        in_hbm(magnetogram),
        in_hbm(theta_weight),
        in_hbm(col_owner.reshape(1, -1)),
        in_hbm(col_offset.reshape(1, -1)),
    )
    partner = swap(magnetogram), swap(theta_weight)
    other = swap(start_field)
    sent = pl.pallas_call(
        pack_kernel,
        compiler_params=SMALL,
        out_shape=struct((phi_devices, 4 * per, width), half),
        in_specs=in_vmem(4),
        out_specs=in_vmem(1)[0],
    )(mine, *partner, chosen)
    sent, radial_coef, theta_coef, phi_coef, field, other, weights = lax.optimization_barrier(
        (sent, radial_coef, theta_coef, phi_coef, start_field, other, phi_weight.T)
    )
    got = over_slabs(sent)
    edge = struct((every * REACH + 2 * count // width, width), real)
    far_edge, near_edge, share = pl.pallas_call(
        edge_kernel,
        compiler_params=SMALL,
        out_shape=[edge, edge, struct((cells, count), half)],
        in_specs=in_vmem(3),
        out_specs=in_vmem(3),
    )(field, other, weights)
    far_edge, near_edge = lax.ppermute(far_edge, "phi", outer), lax.ppermute(near_edge, "phi", inner)
    lines = struct((every, spread, width), real)
    diag, inv, lon, lat, faces = pl.pallas_call(
        coef_kernel,
        compiler_params=SMALL,
        out_shape=[
            lines,
            lines,
            struct((2, spread, width), real),
            struct((2, 8, width), real),
            struct((every + 1, width), real),
        ],
        in_specs=in_smem + in_vmem(2),
        out_specs=in_vmem(5),
    )(radial_coef, theta_coef.reshape(1, width), phi_coef.reshape(-1, width))
    got, far_edge, near_edge, diag, inv, lon, lat, faces = lax.optimization_barrier(
        (got, far_edge, near_edge, diag, inv, lon, lat, faces)
    )
    part = pl.pallas_call(
        boundary_kernel,
        compiler_params=SMALL,
        out_shape=struct((spread, width), real),
        in_specs=in_vmem(4),
        out_specs=in_vmem(1)[0],
    )(got, share, far_edge, near_edge)
    block = struct((layers, cells, width), real)
    sums, *vectors = pl.pallas_call(
        krylov_kernel,
        compiler_params=SMALL,
        out_shape=[struct((phi_devices, width), real)] + [block] * 5,
        in_specs=in_vmem(11),
        out_specs=in_vmem(6),
    )(faces, part, swap(part), field, other, far_edge, near_edge, diag, inv, lon, lat)
    sums = over_slabs(sums)
    return pl.pallas_call(
        update_kernel,
        compiler_params=SMALL,
        out_shape=[block] * 2,
        in_specs=in_vmem(7),
        out_specs=in_vmem(2),
    )(sums, field, *vectors)


def body(*args):
    phi_weight, phi_coef, start_field = args[3], args[7], args[8]
    layers, cells, width = start_field.shape
    phi_devices = lax.axis_size("phi")
    fits = (
        lax.axis_size("row") == 2
        and phi_devices > 2
        and phi_devices % 2 == 0
        and phi_weight.shape[0] % (32 * phi_devices) == 0
        and layers >= REACH
        and cells % 8 == 0
        and cells >= 16
        and width % 128 == 0
        and phi_coef.shape[0] % width == 0
        and phi_weight.shape[0] % (2 * width) == 0
        and (2 * layers * REACH) % 8 == 0
    )
    return (paired_body if fits else general_body)(*args)


def solution(mesh):
    in_specs = (
        P("phi", "row"),
        P("phi"),
        P("phi"),
        P(None, "phi"),
        P("row", None),
        P(),
        P(),
        P(),
        P("row", "phi", None),
    )
    out_specs = (P("row", "phi", None), P("row", "phi", None))
    return jax.shard_map(body, mesh=mesh, in_specs=in_specs, out_specs=out_specs, check_vma=False)
```

```python
import jax
import jax.numpy as jnp
from jax import lax
from jax.experimental import pallas as pl
from jax.experimental.pallas import tpu as pltpu
from jax.sharding import PartitionSpec as P

REACH = 3


def face_coefs(radial_coef, theta_coef, phi_coef):
    radial_mid = 0.5 * (radial_coef[:-1] + radial_coef[1:])
    radial_upper = jnp.concatenate([radial_mid, radial_coef[-1:]])
    radial_lower = jnp.concatenate([radial_coef[:1], radial_mid])
    theta_mid = 0.5 * (theta_coef[:-1] + theta_coef[1:])
    zero_one = jnp.zeros((1,), jnp.float32)
    theta_upper = jnp.concatenate([theta_mid, zero_one])
    theta_lower = jnp.concatenate([zero_one, theta_mid])
    phi_upper = 0.5 * (phi_coef + jnp.roll(phi_coef, -1))
    phi_lower = jnp.roll(phi_upper, 1)
    return (radial_upper, radial_lower, theta_upper, theta_lower, phi_upper, phi_lower)


def row_sum(value, rows):
    if rows == 2:
        return value + lax.ppermute(value, "row", [(0, 1), (1, 0)])
    return lax.psum(value, "row")


def pick(chunks, index):
    return lax.dynamic_index_in_dim(chunks, index, 0, keepdims=False)


def step_sizes(a, b, c, e):
    alpha = a / b
    beta = (alpha * alpha * c - a) / a
    gain = 1.0 + beta
    curvature = gain * gain * b - 2.0 * gain * alpha * c + alpha * alpha * e
    return alpha, gain, beta * a / curvature


def general_body(
    magnetogram,
    col_owner,
    col_offset,
    phi_weight,
    theta_weight,
    radial_coef,
    theta_coef,
    phi_coef,
    start_field,
):
    layers, cells, width = start_field.shape
    phi_devices = lax.axis_size("phi")
    rows = lax.axis_size("row")
    slots = phi_weight.shape[0]
    capacity = slots // phi_devices
    per = capacity // rows
    here = lax.axis_index("phi")
    row = lax.axis_index("row")
    above = lax.rem(here + 1, phi_devices)
    below = lax.rem(here + phi_devices - 1, phi_devices)

    climb = [(i, i + 1) for i in range(rows - 1)]
    low_layers = lax.ppermute(start_field[layers - REACH :], "row", climb)
    high_layers = lax.ppermute(start_field[:REACH], "row", [(t, s) for s, t in climb])
    window = jnp.concatenate([low_layers, start_field, high_layers], axis=0)

    columns = jnp.dot(magnetogram, theta_weight, preferred_element_type=jnp.float32)
    columns = row_sum(columns, rows)
    upper_part = lax.optimization_barrier(columns.astype(jnp.bfloat16))
    lower_part = (columns - upper_part.astype(jnp.float32)).astype(jnp.bfloat16)

    place = col_offset - row * per
    target = jnp.where((place >= 0) & (place < per), col_owner * per + place, -1)
    chosen = (target[None, :] == jnp.arange(phi_devices * per, dtype=jnp.int32)[:, None]).astype(
        jnp.bfloat16
    )
    packed = jnp.dot(chosen, upper_part, preferred_element_type=jnp.float32)
    packed = packed + jnp.dot(chosen, lower_part, preferred_element_type=jnp.float32)
    packed = packed.reshape(phi_devices, per, width)
    share = phi_weight.reshape(phi_devices, rows, per, cells)
    share = lax.dynamic_index_in_dim(share, row, 1, keepdims=False)
    share = share.reshape(phi_devices * per, cells)

    def edge(start):
        field = window[:, start : start + REACH].reshape(-1, width)
        lo = start + 1 if start else 0
        weights = share[:, lo : lo + 2].astype(jnp.float32).T.reshape(-1, width)
        return jnp.concatenate([field, weights], axis=0)

    to_above, to_below = edge(cells - REACH), edge(0)
    who = jnp.arange(phi_devices, dtype=jnp.int32)[:, None, None]
    edges = jnp.where(who == above, to_above[None], jnp.where(who == below, to_below[None], 0.0))
    sent = jnp.concatenate(
        [packed, jnp.roll(packed, 1, axis=0), jnp.roll(packed, -1, axis=0), edges], axis=1
    )
    got = lax.all_to_all(sent, "phi", split_axis=0, concat_axis=0, tiled=True)
    edge_low, edge_high = pick(got, below)[3 * per :], pick(got, above)[3 * per :]
    reach_rows = window.shape[0] * REACH

    def weigh(weights, which):
        data = got[:, which * per : (which + 1) * per].reshape(phi_devices * per, width)
        part = lax.optimization_barrier(data.astype(jnp.bfloat16))
        rest = (data - part.astype(jnp.float32)).astype(jnp.bfloat16)
        total = jnp.dot(weights, part, preferred_element_type=jnp.float32)
        return total + jnp.dot(weights, rest, preferred_element_type=jnp.float32)

    def ghost_weights(edge_rows):
        return edge_rows[reach_rows:].reshape(2, phi_devices * per).astype(jnp.bfloat16)

    boundary = row_sum(
        jnp.concatenate(
            [
                weigh(ghost_weights(edge_low), 1),
                weigh(share.T, 0),
                weigh(ghost_weights(edge_high), 2),
            ],
            axis=0,
        ),
        rows,
    )
    field = jnp.concatenate(
        [
            edge_low[:reach_rows].reshape(-1, REACH, width),
            window,
            edge_high[:reach_rows].reshape(-1, REACH, width),
        ],
        axis=1,
    )

    faces = face_coefs(radial_coef, theta_coef, phi_coef)
    spread = layers + 2 * REACH

    def radial_window(coef):
        padded = jnp.pad(coef, (REACH, REACH))
        return lax.dynamic_slice_in_dim(padded, row * layers, spread)[:, None, None]

    def phi_window(coef):
        padded = jnp.concatenate([coef[-REACH:], coef, coef[:REACH]])
        return lax.dynamic_slice_in_dim(padded, here * cells, cells + 2 * REACH)[None, :, None]

    rad_upper, rad_lower = radial_window(faces[0]), radial_window(faces[1])
    lon_upper, lon_lower = phi_window(faces[4]), phi_window(faces[5])
    lat_upper, lat_lower = faces[2][None, None, :], faces[3][None, None, :]
    inside = radial_window(jnp.ones_like(radial_coef))
    inv_diag = inside / (
        rad_upper + rad_lower + lat_upper + lat_lower + lon_upper + lon_lower + (1.0 - inside)
    )

    def apply_operator(value, depth):
        mid = value[1:-1, 1:-1]
        theta_pad = jnp.pad(mid, ((0, 0), (0, 0), (1, 1)))
        result = rad_upper[depth:-depth] * (mid - value[2:, 1:-1])
        result = result + rad_lower[depth:-depth] * (mid - value[:-2, 1:-1])
        result = result + lat_upper * (mid - theta_pad[:, :, 2:])
        result = result + lat_lower * (mid - theta_pad[:, :, :-2])
        result = result + lon_upper[:, depth:-depth] * (mid - value[1:-1, 2:])
        return result + lon_lower[:, depth:-depth] * (mid - value[1:-1, :-2])

    def inner(value, by):
        return value[by:-by, by:-by] if by else value

    level = row * layers - REACH + 1 + jnp.arange(spread - 2, dtype=jnp.int32)[:, None, None]
    source = jnp.where(level == 0, (faces[1][0] * boundary)[None], 0.0)
    residual = source - apply_operator(field, 1)
    first = residual * inner(inv_diag, 1)
    first_image = apply_operator(first, 2)
    second = first_image * inner(inv_diag, 2)
    second_image = apply_operator(second, 3)
    residual, first = inner(residual, 2), inner(first, 2)
    first_image, second = inner(first_image, 1), inner(second, 1)

    pairs = (
        (residual, first),
        (first, first_image),
        (first_image, second),
        (second, second_image),
    )
    sums = jnp.stack([jnp.sum(u * v, axis=(0, 1)) for u, v in pairs] * 2)
    devices = phi_devices * rows
    if devices <= 64:
        shared = jnp.broadcast_to(sums[None], (devices,) + sums.shape)
        shared = lax.all_to_all(shared, ("phi", "row"), split_axis=0, concat_axis=0, tiled=True)
        totals = jnp.sum(shared, axis=(0, 2))
    else:
        totals = lax.psum(jnp.sum(sums, axis=1), ("phi", "row"))
    alpha, gain, alpha_next = step_sizes(totals[0], totals[1], totals[2], totals[3])
    direction = gain * first - alpha * second
    solution_field = start_field + alpha * first + alpha_next * direction
    image = gain * first_image - alpha * second_image
    return solution_field, residual - alpha * first_image - alpha_next * image


def high_low(value):
    high = value.astype(jnp.bfloat16)
    return high, (value - high.astype(jnp.float32)).astype(jnp.bfloat16)


def leader(devices):
    return devices // 2 + 1


def seat(slab, devices):
    return lax.rem(leader(devices) - slab + devices, devices)


def own_share(weights, devices):
    slots = weights.shape[1]
    per = slots // devices // 2
    slot = lax.broadcasted_iota(jnp.int32, (slots, slots // 2), 0)
    place = lax.broadcasted_iota(jnp.int32, (slots, slots // 2), 1)
    source = seat(place // per, devices)
    wanted = source * (2 * per) + lax.axis_index("row") * per + place % per
    picker = jnp.where(slot == wanted, 1.0, 0.0).astype(jnp.bfloat16)
    return jnp.dot(weights, picker, preferred_element_type=jnp.float32).astype(jnp.bfloat16)


def column_kernel(
    mag_hbm,
    theta_hbm,
    owner_hbm,
    offset_hbm,
    out_ref,
    chosen_ref,
    mag_ref,
    theta_ref,
    owner_ref,
    offset_ref,
    done,
):
    pairs = (
        (theta_hbm, theta_ref),
        (mag_hbm, mag_ref),
        (owner_hbm, owner_ref),
        (offset_hbm, offset_ref),
    )
    copies = [pltpu.make_async_copy(*pair, done.at[at]) for at, pair in enumerate(pairs)]
    for copy in copies:
        copy.start()
    for copy in copies:
        copy.wait()
    out_ref[...] = jnp.dot(mag_ref[...], theta_ref[...], preferred_element_type=jnp.float32)
    devices = lax.axis_size("phi")
    per = chosen_ref.shape[0] // devices
    place = offset_ref[...] - lax.axis_index("row") * per
    target = jnp.where((place >= 0) & (place < per), seat(owner_ref[...], devices) * per + place, -1)
    slot = lax.broadcasted_iota(jnp.int32, chosen_ref.shape, 0)
    chosen_ref[...] = jnp.where(slot == target, 1.0, 0.0).astype(jnp.bfloat16)


def pack_kernel(mine_ref, mag_ref, theta_ref, chosen_ref, out_ref):
    devices, rows, width = out_ref.shape
    per = rows // 4
    other = jnp.dot(mag_ref[...], theta_ref[...], preferred_element_type=jnp.float32)
    high, low = high_low(mine_ref[...] + other)
    packed = jnp.dot(
        chosen_ref[...], jnp.concatenate([high, low], axis=1), preferred_element_type=jnp.float32
    ).astype(jnp.bfloat16)
    high = packed[:, :width].reshape(devices, per, width)
    out_ref[:, :per] = high
    out_ref[:, per : 2 * per] = packed[:, width:].reshape(devices, per, width)
    for at in range(devices):
        out_ref[at, 2 * per : 3 * per] = high[(at + 1) % devices]
        out_ref[at, 3 * per :] = high[(at - 1) % devices]


def is_odd():
    return lax.rem(lax.axis_index("phi"), 2) == 1


def edge_kernel(field_ref, other_ref, weight_ref, far_ref, near_ref, share_ref):
    layers, cells, width = field_ref.shape
    odd = is_odd()
    first = lax.axis_index("row") == 0
    share = own_share(weight_ref[...], lax.axis_size("phi"))
    share_ref[...] = share
    weights = share.astype(jnp.float32)

    def put(at, up, down):
        far_ref[at : at + up.shape[0]] = jnp.where(odd, up, down)
        near_ref[at : at + up.shape[0]] = jnp.where(odd, down, up)

    for layer in range(layers):
        up = [ref[layer, cells - REACH :] for ref in (field_ref, other_ref)]
        down = [ref[layer, :REACH] for ref in (field_ref, other_ref)]
        put(layer * REACH, jnp.where(first, *up), jnp.where(first, *down))
        put((layers + layer) * REACH, jnp.where(first, *up[::-1]), jnp.where(first, *down[::-1]))
    for part in range(share.shape[1] // width):
        piece = weights[:, part * width : (part + 1) * width]
        put(2 * layers * REACH + 2 * part, piece[cells - 2 :], piece[:2])


def sides(far_ref, near_ref):
    odd = is_odd()
    return (
        jnp.where(odd, far_ref[...], near_ref[...]),
        jnp.where(odd, near_ref[...], far_ref[...]),
    )


def coef_kernel(
    radial_ref, theta_ref, phi_ref, diag_ref, inv_ref, lon_ref, lat_ref, face_ref
):
    layers, spread, width = inv_ref.shape
    cells = spread - 8
    chunks = phi_ref.shape[0]
    total = chunks * width
    row = lax.broadcasted_iota(jnp.int32, (spread, width), 0)
    lane = lax.broadcasted_iota(jnp.int32, (spread, width), 1)
    cell = lax.axis_index("phi") * cells + jnp.where(row < cells + 4, row, row - spread)
    cell = jnp.where(cell < 0, cell + total, jnp.where(cell >= total, cell - total, cell))
    found = jnp.zeros((spread, width), jnp.float32)
    for chunk in range(chunks):
        found = found + jnp.where(lane + chunk * width == cell, phi_ref[chunk : chunk + 1], 0.0)
    column = jnp.broadcast_to(jnp.sum(found, axis=1, keepdims=True), (spread, width))
    lon_ref[0] = 0.5 * (column + pltpu.roll(column, spread - 1, 0))
    lon_ref[1] = 0.5 * (column + pltpu.roll(column, 1, 0))
    theta = jnp.broadcast_to(theta_ref[...], (8, width))
    ends = lax.broadcasted_iota(jnp.int32, (8, width), 1)
    upper = jnp.where(ends == width - 1, 0.0, 0.5 * (theta + pltpu.roll(theta, width - 1, 1)))
    lower = jnp.where(ends == 0, 0.0, 0.5 * (theta + pltpu.roll(theta, 1, 1)))
    lat_ref[0], lat_ref[1] = upper, lower
    flat = lon_ref[0] + lon_ref[1] + (upper + lower)[:1]
    faces = [
        0.5 * (radial_ref[max(face - 1, 0)] + radial_ref[min(face, layers - 1)])
        for face in range(layers + 1)
    ]
    for face in range(layers + 1):
        face_ref[face : face + 1] = jnp.full((1, width), faces[face], jnp.float32)
    for layer in range(layers):
        diag = flat + (faces[layer] + faces[layer + 1])
        diag_ref[layer] = diag
        inv_ref[layer] = 1.0 / diag


def boundary_kernel(got_ref, share_ref, far_ref, near_ref, out_ref):
    devices, rows, width = got_ref.shape
    cells, count = share_ref.shape
    per, spread = rows // 4, cells + 8
    above, below = sides(far_ref, near_ref)
    edge_rows = above.shape[0]

    def product(weights, first):
        data = [
            got_ref[:, which * per : (which + 1) * per].reshape(count, width)
            for which in (first, first + 1)
        ]
        total = jnp.dot(weights, jnp.concatenate(data, axis=1), preferred_element_type=jnp.float32)
        return total[:, :width], total[:, width:]

    def edge_weights(edge):
        at = edge_rows - 2 * count // width
        parts = [edge[at + 2 * k : at + 2 * k + 2] for k in range(count // width)]
        return jnp.concatenate(parts, axis=1)

    high, low = product(share_ref[...], 0)
    out_ref[:cells] = high + low
    weights = jnp.concatenate(
        [edge_weights(above), jnp.zeros((4, count), jnp.float32), edge_weights(below)], axis=0
    )
    from_below, from_above = product(weights.astype(jnp.bfloat16), 2)
    row = lax.broadcasted_iota(jnp.int32, (8, width), 0)
    out_ref[cells:spread] = jnp.where(row < 4, from_above, from_below)


def neighbours(values, layer, faces, lon, lat):
    mid = values[layer]
    spread, width = mid.shape
    total = lat[0] * pltpu.roll(mid, width - 1, 1) + lat[1] * pltpu.roll(mid, 1, 1)
    total = total + lon[0] * pltpu.roll(mid, spread - 1, 0)
    total = total + lon[1] * pltpu.roll(mid, 1, 0)
    for at, face in ((layer - 1, layer), (layer + 1, layer + 1)):
        if at in values:
            total = total + faces[face] * values[at]
    return total


def krylov_kernel(
    face_ref,
    field_ref,
    other_ref,
    far_ref,
    near_ref,
    diag_ref,
    inv_ref,
    lon_ref,
    lat_ref,
    totals_ref,
    low_ref,
    *vector_refs,
):
    layers, cells, width = field_ref.shape
    every, spread, _ = inv_ref.shape
    above, below = sides(far_ref, near_ref)
    gap = jnp.zeros((8 - 2 * REACH, width), jnp.float32)
    upper = lax.axis_index("row") == 1
    faces = [face_ref[face : face + 1] for face in range(every + 1)]
    lon, lat = (lon_ref[0], lon_ref[1]), (lat_ref[0, :1], lat_ref[1, :1])
    field = {}
    for layer in range(every):
        edge = slice(layer * REACH, (layer + 1) * REACH)
        at, high = layer % layers, layer >= layers
        block = jnp.where(upper == high, field_ref[at], other_ref[at])
        field[layer] = jnp.concatenate([block, above[edge], gap, below[edge]], axis=0)
    residual, first, image, second, image2 = {}, {}, {}, {}, {}
    for layer in range(every):
        value = neighbours(field, layer, faces, lon, lat) - diag_ref[layer] * field[layer]
        residual[layer] = value
        first[layer] = value * inv_ref[layer]
    for layer in range(every):
        image[layer] = residual[layer] - neighbours(first, layer, faces, lon, lat)
        second[layer] = image[layer] * inv_ref[layer]
    totals = [jnp.zeros((8, width), jnp.float32)] * 4
    for layer in range(every):
        image2[layer] = image[layer] - neighbours(second, layer, faces, lon, lat)
        vectors = [each[layer][:cells] for each in (residual, first, image, second, image2)]
        if layer < REACH:
            for which, vector in enumerate(vectors):
                low_ref[which, layer] = vector
        else:
            for which in range(4):
                product = vectors[which] * vectors[which + 1]
                for begin in range(0, cells, 8):
                    totals[which] = totals[which] + product[begin : begin + 8]
    for ref, vector in zip(vector_refs, (residual, first, image, second, image2)):
        for at in range(layers):
            ref[at] = jnp.where(upper, vector[layers + at], vector[at])[:cells]
    for which in range(4):
        totals_ref[which] = totals[which]


def boundary_effect_kernel(
    face_ref, part_ref, rest_ref, inv_ref, lon_ref, lat_ref, totals_ref, low_ref, sums_ref, change_ref
):
    _, reach, cells, width = low_ref.shape
    faces = [face_ref[face : face + 1] for face in range(reach + 1)]
    lon, lat = (lon_ref[0], lon_ref[1]), (lat_ref[0, :1], lat_ref[1, :1])
    source = faces[0] * (part_ref[...] + rest_ref[...])
    first = {0: source * inv_ref[0]}
    image = {0: source - neighbours(first, 0, faces, lon, lat), 1: -faces[1] * first[0]}
    second = {layer: image[layer] * inv_ref[layer] for layer in range(2)}
    image2 = {layer: image[layer] - neighbours(second, layer, faces, lon, lat) for layer in range(2)}
    image2[2] = -faces[2] * second[1]
    totals = [totals_ref[which] for which in range(4)]
    for layer in range(reach):
        vectors = []
        for which, change in enumerate(({0: source}, first, image, second, image2)):
            vector = low_ref[which, layer]
            if layer in change:
                change_ref[which, layer] = change[layer][:cells]
                vector = vector + change[layer][:cells]
            vectors.append(vector)
        for which in range(4):
            product = vectors[which] * vectors[which + 1]
            for begin in range(0, cells, 8):
                totals[which] = totals[which] + product[begin : begin + 8]
    lane = lax.broadcasted_iota(jnp.int32, (8, width), 1)
    packed = jnp.zeros((8, width), jnp.float32)
    for which, total in enumerate(totals):
        packed = jnp.where(lane == which, jnp.sum(total, axis=1, keepdims=True), packed)
    sums_ref[...] = jnp.broadcast_to(jnp.sum(packed, axis=0, keepdims=True), sums_ref.shape)


def update_kernel(
    sums_ref,
    field_ref,
    residual_ref,
    first_ref,
    image_ref,
    second_ref,
    image2_ref,
    change_ref,
    out_ref,
    left_ref,
):
    totals = jnp.sum(sums_ref[...], axis=0, keepdims=True)
    lane = lax.broadcasted_iota(jnp.int32, totals.shape, 1)
    a, b, c, e = (
        jnp.sum(jnp.where(lane == which, totals, 0.0), axis=1, keepdims=True) for which in range(4)
    )
    alpha, gain, alpha_next = step_sizes(a, b, c, e)
    along, back = alpha + alpha_next * gain, alpha_next * alpha
    here = jnp.where(lax.axis_index("row") == 0, 1.0, 0.0)
    reached = dict(zip(range(5), (1, 1, 2, 2, 3)))
    for layer in range(field_ref.shape[0]):
        vectors = []
        for which, ref in enumerate((residual_ref, first_ref, image_ref, second_ref, image2_ref)):
            vector = ref[layer]
            if layer < reached[which]:
                vector = vector + here * change_ref[which, layer]
            vectors.append(vector)
        residual, first, image, second, image2 = vectors
        out_ref[layer] = field_ref[layer] + (along * first - back * second)
        left_ref[layer] = residual - (along * image - back * image2)


SMALL = pltpu.CompilerParams(vmem_limit_bytes=8 << 20)


def in_vmem(count):
    return [pl.BlockSpec(memory_space=pltpu.VMEM)] * count


def paired_body(
    magnetogram,
    col_owner,
    col_offset,
    phi_weight,
    theta_weight,
    radial_coef,
    theta_coef,
    phi_coef,
    start_field,
):
    layers, cells, width = start_field.shape
    phi_devices = lax.axis_size("phi")
    per = phi_weight.shape[0] // phi_devices // 2
    count = phi_devices * per
    columns = magnetogram.shape[0]
    every, spread = 2 * layers, cells + 8
    real, half = jnp.float32, jnp.bfloat16
    struct = jax.ShapeDtypeStruct
    in_smem = [pl.BlockSpec(memory_space=pltpu.SMEM)]

    def swap(value):
        return lax.ppermute(value, "row", [(0, 1), (1, 0)])

    inner = [(i, i ^ 1) for i in range(phi_devices)]
    outer = [(i, (i + (1 if i % 2 else -1)) % phi_devices) for i in range(phi_devices)]

    order = [(leader(phi_devices) - i) % phi_devices for i in range(phi_devices)]

    def over_slabs(value):
        return lax.all_to_all(
            value, "phi", split_axis=0, concat_axis=0, axis_index_groups=[order], tiled=True
        )

    def in_hbm(value):
        return pltpu.with_memory_space_constraint(value, pltpu.HBM)

    mine, chosen = pl.pallas_call(
        column_kernel,
        compiler_params=SMALL,
        out_shape=[struct((columns, width), real), struct((count, columns), half)],
        in_specs=[pl.BlockSpec(memory_space=pltpu.HBM)] * 4,
        out_specs=in_vmem(2),
        scratch_shapes=[
            pltpu.VMEM(magnetogram.shape, half),
            pltpu.VMEM(theta_weight.shape, half),
            pltpu.VMEM((1, columns), jnp.int32),
            pltpu.VMEM((1, columns), jnp.int32),
            pltpu.SemaphoreType.DMA((4,)),
        ],
    )(
        in_hbm(magnetogram),
        in_hbm(theta_weight),
        in_hbm(col_owner.reshape(1, -1)),
        in_hbm(col_offset.reshape(1, -1)),
    )
    partner = swap(magnetogram), swap(theta_weight)
    other = swap(start_field)
    sent = pl.pallas_call(
        pack_kernel,
        compiler_params=SMALL,
        out_shape=struct((phi_devices, 4 * per, width), half),
        in_specs=in_vmem(4),
        out_specs=in_vmem(1)[0],
    )(mine, *partner, chosen)
    sent, radial_coef, theta_coef, phi_coef, field, other, weights = lax.optimization_barrier(
        (sent, radial_coef, theta_coef, phi_coef, start_field, other, phi_weight.T)
    )
    got = over_slabs(sent)
    edge = struct((every * REACH + 2 * count // width, width), real)
    far_edge, near_edge, share = pl.pallas_call(
        edge_kernel,
        compiler_params=SMALL,
        out_shape=[edge, edge, struct((cells, count), half)],
        in_specs=in_vmem(3),
        out_specs=in_vmem(3),
    )(field, other, weights)
    far_edge, near_edge = lax.ppermute(far_edge, "phi", outer), lax.ppermute(near_edge, "phi", inner)
    lines = struct((every, spread, width), real)
    diag, inv, lon, lat, faces = pl.pallas_call(
        coef_kernel,
        compiler_params=SMALL,
        out_shape=[
            lines,
            lines,
            struct((2, spread, width), real),
            struct((2, 8, width), real),
            struct((every + 1, width), real),
        ],
        in_specs=in_smem + in_vmem(2),
        out_specs=in_vmem(5),
    )(radial_coef, theta_coef.reshape(1, width), phi_coef.reshape(-1, width))
    got, far_edge, near_edge, diag, inv, lon, lat, faces = lax.optimization_barrier(
        (got, far_edge, near_edge, diag, inv, lon, lat, faces)
    )
    part = pl.pallas_call(
        boundary_kernel,
        compiler_params=SMALL,
        out_shape=struct((spread, width), real),
        in_specs=in_vmem(4),
        out_specs=in_vmem(1)[0],
    )(got, share, far_edge, near_edge)
    block = struct((layers, cells, width), real)
    totals, low, *vectors = pl.pallas_call(
        krylov_kernel,
        compiler_params=SMALL,
        out_shape=[struct((4, 8, width), real), struct((5, REACH, cells, width), real)]
        + [block] * 5,
        in_specs=in_vmem(9),
        out_specs=in_vmem(7),
    )(faces, field, other, far_edge, near_edge, diag, inv, lon, lat)
    sums, change = pl.pallas_call(
        boundary_effect_kernel,
        compiler_params=SMALL,
        out_shape=[struct((phi_devices, width), real), struct((5, REACH, cells, width), real)],
        in_specs=in_vmem(8),
        out_specs=in_vmem(2),
    )(faces, part, swap(part), inv, lon, lat, totals, low)
    sums = over_slabs(sums)
    return pl.pallas_call(
        update_kernel,
        compiler_params=SMALL,
        out_shape=[block] * 2,
        in_specs=in_vmem(8),
        out_specs=in_vmem(2),
    )(sums, field, *vectors, change)


def body(*args):
    phi_weight, phi_coef, start_field = args[3], args[7], args[8]
    layers, cells, width = start_field.shape
    phi_devices = lax.axis_size("phi")
    fits = (
        lax.axis_size("row") == 2
        and phi_devices > 2
        and phi_devices % 2 == 0
        and phi_weight.shape[0] % (32 * phi_devices) == 0
        and layers >= REACH
        and cells % 8 == 0
        and cells >= 16
        and width % 128 == 0
        and phi_coef.shape[0] % width == 0
        and phi_weight.shape[0] % (2 * width) == 0
        and (2 * layers * REACH) % 8 == 0
    )
    return (paired_body if fits else general_body)(*args)


def solution(mesh):
    in_specs = (
        P("phi", "row"),
        P("phi"),
        P("phi"),
        P(None, "phi"),
        P("row", None),
        P(),
        P(),
        P(),
        P("row", "phi", None),
    )
    out_specs = (P("row", "phi", None), P("row", "phi", None))
    return jax.shard_map(body, mesh=mesh, in_specs=in_specs, out_specs=out_specs, check_vma=False)
```

```python
import jax
import jax.numpy as jnp
from jax import lax
from jax.experimental import pallas as pl
from jax.experimental.pallas import tpu as pltpu
from jax.sharding import PartitionSpec as P

REACH = 3


def face_coefs(radial_coef, theta_coef, phi_coef):
    radial_mid = 0.5 * (radial_coef[:-1] + radial_coef[1:])
    radial_upper = jnp.concatenate([radial_mid, radial_coef[-1:]])
    radial_lower = jnp.concatenate([radial_coef[:1], radial_mid])
    theta_mid = 0.5 * (theta_coef[:-1] + theta_coef[1:])
    zero_one = jnp.zeros((1,), jnp.float32)
    theta_upper = jnp.concatenate([theta_mid, zero_one])
    theta_lower = jnp.concatenate([zero_one, theta_mid])
    phi_upper = 0.5 * (phi_coef + jnp.roll(phi_coef, -1))
    phi_lower = jnp.roll(phi_upper, 1)
    return (radial_upper, radial_lower, theta_upper, theta_lower, phi_upper, phi_lower)


def row_sum(value, rows):
    if rows == 2:
        return value + lax.ppermute(value, "row", [(0, 1), (1, 0)])
    return lax.psum(value, "row")


def pick(chunks, index):
    return lax.dynamic_index_in_dim(chunks, index, 0, keepdims=False)


def step_sizes(a, b, c, e):
    alpha = a / b
    beta = (alpha * alpha * c - a) / a
    gain = 1.0 + beta
    curvature = gain * gain * b - 2.0 * gain * alpha * c + alpha * alpha * e
    return alpha, gain, beta * a / curvature


def general_body(
    magnetogram,
    col_owner,
    col_offset,
    phi_weight,
    theta_weight,
    radial_coef,
    theta_coef,
    phi_coef,
    start_field,
):
    layers, cells, width = start_field.shape
    phi_devices = lax.axis_size("phi")
    rows = lax.axis_size("row")
    slots = phi_weight.shape[0]
    capacity = slots // phi_devices
    per = capacity // rows
    here = lax.axis_index("phi")
    row = lax.axis_index("row")
    above = lax.rem(here + 1, phi_devices)
    below = lax.rem(here + phi_devices - 1, phi_devices)

    climb = [(i, i + 1) for i in range(rows - 1)]
    low_layers = lax.ppermute(start_field[layers - REACH :], "row", climb)
    high_layers = lax.ppermute(start_field[:REACH], "row", [(t, s) for s, t in climb])
    window = jnp.concatenate([low_layers, start_field, high_layers], axis=0)

    columns = jnp.dot(magnetogram, theta_weight, preferred_element_type=jnp.float32)
    columns = row_sum(columns, rows)
    upper_part = lax.optimization_barrier(columns.astype(jnp.bfloat16))
    lower_part = (columns - upper_part.astype(jnp.float32)).astype(jnp.bfloat16)

    place = col_offset - row * per
    target = jnp.where((place >= 0) & (place < per), col_owner * per + place, -1)
    chosen = (target[None, :] == jnp.arange(phi_devices * per, dtype=jnp.int32)[:, None]).astype(
        jnp.bfloat16
    )
    packed = jnp.dot(chosen, upper_part, preferred_element_type=jnp.float32)
    packed = packed + jnp.dot(chosen, lower_part, preferred_element_type=jnp.float32)
    packed = packed.reshape(phi_devices, per, width)
    share = phi_weight.reshape(phi_devices, rows, per, cells)
    share = lax.dynamic_index_in_dim(share, row, 1, keepdims=False)
    share = share.reshape(phi_devices * per, cells)

    def edge(start):
        field = window[:, start : start + REACH].reshape(-1, width)
        lo = start + 1 if start else 0
        weights = share[:, lo : lo + 2].astype(jnp.float32).T.reshape(-1, width)
        return jnp.concatenate([field, weights], axis=0)

    to_above, to_below = edge(cells - REACH), edge(0)
    who = jnp.arange(phi_devices, dtype=jnp.int32)[:, None, None]
    edges = jnp.where(who == above, to_above[None], jnp.where(who == below, to_below[None], 0.0))
    sent = jnp.concatenate(
        [packed, jnp.roll(packed, 1, axis=0), jnp.roll(packed, -1, axis=0), edges], axis=1
    )
    got = lax.all_to_all(sent, "phi", split_axis=0, concat_axis=0, tiled=True)
    edge_low, edge_high = pick(got, below)[3 * per :], pick(got, above)[3 * per :]
    reach_rows = window.shape[0] * REACH

    def weigh(weights, which):
        data = got[:, which * per : (which + 1) * per].reshape(phi_devices * per, width)
        part = lax.optimization_barrier(data.astype(jnp.bfloat16))
        rest = (data - part.astype(jnp.float32)).astype(jnp.bfloat16)
        total = jnp.dot(weights, part, preferred_element_type=jnp.float32)
        return total + jnp.dot(weights, rest, preferred_element_type=jnp.float32)

    def ghost_weights(edge_rows):
        return edge_rows[reach_rows:].reshape(2, phi_devices * per).astype(jnp.bfloat16)

    boundary = row_sum(
        jnp.concatenate(
            [
                weigh(ghost_weights(edge_low), 1),
                weigh(share.T, 0),
                weigh(ghost_weights(edge_high), 2),
            ],
            axis=0,
        ),
        rows,
    )
    field = jnp.concatenate(
        [
            edge_low[:reach_rows].reshape(-1, REACH, width),
            window,
            edge_high[:reach_rows].reshape(-1, REACH, width),
        ],
        axis=1,
    )

    faces = face_coefs(radial_coef, theta_coef, phi_coef)
    spread = layers + 2 * REACH

    def radial_window(coef):
        padded = jnp.pad(coef, (REACH, REACH))
        return lax.dynamic_slice_in_dim(padded, row * layers, spread)[:, None, None]

    def phi_window(coef):
        padded = jnp.concatenate([coef[-REACH:], coef, coef[:REACH]])
        return lax.dynamic_slice_in_dim(padded, here * cells, cells + 2 * REACH)[None, :, None]

    rad_upper, rad_lower = radial_window(faces[0]), radial_window(faces[1])
    lon_upper, lon_lower = phi_window(faces[4]), phi_window(faces[5])
    lat_upper, lat_lower = faces[2][None, None, :], faces[3][None, None, :]
    inside = radial_window(jnp.ones_like(radial_coef))
    inv_diag = inside / (
        rad_upper + rad_lower + lat_upper + lat_lower + lon_upper + lon_lower + (1.0 - inside)
    )

    def apply_operator(value, depth):
        mid = value[1:-1, 1:-1]
        theta_pad = jnp.pad(mid, ((0, 0), (0, 0), (1, 1)))
        result = rad_upper[depth:-depth] * (mid - value[2:, 1:-1])
        result = result + rad_lower[depth:-depth] * (mid - value[:-2, 1:-1])
        result = result + lat_upper * (mid - theta_pad[:, :, 2:])
        result = result + lat_lower * (mid - theta_pad[:, :, :-2])
        result = result + lon_upper[:, depth:-depth] * (mid - value[1:-1, 2:])
        return result + lon_lower[:, depth:-depth] * (mid - value[1:-1, :-2])

    def inner(value, by):
        return value[by:-by, by:-by] if by else value

    level = row * layers - REACH + 1 + jnp.arange(spread - 2, dtype=jnp.int32)[:, None, None]
    source = jnp.where(level == 0, (faces[1][0] * boundary)[None], 0.0)
    residual = source - apply_operator(field, 1)
    first = residual * inner(inv_diag, 1)
    first_image = apply_operator(first, 2)
    second = first_image * inner(inv_diag, 2)
    second_image = apply_operator(second, 3)
    residual, first = inner(residual, 2), inner(first, 2)
    first_image, second = inner(first_image, 1), inner(second, 1)

    pairs = (
        (residual, first),
        (first, first_image),
        (first_image, second),
        (second, second_image),
    )
    sums = jnp.stack([jnp.sum(u * v, axis=(0, 1)) for u, v in pairs] * 2)
    devices = phi_devices * rows
    if devices <= 64:
        shared = jnp.broadcast_to(sums[None], (devices,) + sums.shape)
        shared = lax.all_to_all(shared, ("phi", "row"), split_axis=0, concat_axis=0, tiled=True)
        totals = jnp.sum(shared, axis=(0, 2))
    else:
        totals = lax.psum(jnp.sum(sums, axis=1), ("phi", "row"))
    alpha, gain, alpha_next = step_sizes(totals[0], totals[1], totals[2], totals[3])
    direction = gain * first - alpha * second
    solution_field = start_field + alpha * first + alpha_next * direction
    image = gain * first_image - alpha * second_image
    return solution_field, residual - alpha * first_image - alpha_next * image


def high_low(value):
    high = value.astype(jnp.bfloat16)
    return high, (value - high.astype(jnp.float32)).astype(jnp.bfloat16)


def leader(devices):
    return 11 * devices // 16


def seat(slab, devices):
    return lax.rem(leader(devices) - slab + devices, devices)


def share_of(slab, row, devices):
    return row ^ (slab >= devices // 2)


def own_half():
    devices = lax.axis_size("phi")
    return share_of(lax.axis_index("phi"), lax.axis_index("row"), devices)


def share_weights(weights, half):
    slots = weights.shape[1]
    devices = lax.axis_size("phi")
    per = slots // devices // 2
    slot = lax.broadcasted_iota(jnp.int32, (slots, slots // 2), 0)
    place = lax.broadcasted_iota(jnp.int32, (slots, slots // 2), 1)
    source = seat(place // per, devices)
    wanted = source * (2 * per) + half * per + place % per
    picker = jnp.where(slot == wanted, 1.0, 0.0).astype(jnp.bfloat16)
    return jnp.dot(weights, picker, preferred_element_type=jnp.float32).astype(jnp.bfloat16)


def column_kernel(
    mag_hbm,
    theta_hbm,
    owner_hbm,
    offset_hbm,
    out_ref,
    chosen_ref,
    mag_ref,
    theta_ref,
    owner_ref,
    offset_ref,
    done,
):
    pairs = (
        (theta_hbm, theta_ref),
        (mag_hbm, mag_ref),
        (owner_hbm, owner_ref),
        (offset_hbm, offset_ref),
    )
    copies = [pltpu.make_async_copy(*pair, done.at[at]) for at, pair in enumerate(pairs)]
    for copy in copies:
        copy.start()
    for copy in copies:
        copy.wait()
    out_ref[...] = jnp.dot(mag_ref[...], theta_ref[...], preferred_element_type=jnp.float32)
    devices = lax.axis_size("phi")
    per = chosen_ref.shape[0] // devices
    place = offset_ref[...] - own_half() * per
    target = jnp.where((place >= 0) & (place < per), seat(owner_ref[...], devices) * per + place, -1)
    slot = lax.broadcasted_iota(jnp.int32, chosen_ref.shape, 0)
    chosen_ref[...] = jnp.where(slot == target, 1.0, 0.0).astype(jnp.bfloat16)


def pack_kernel(mine_ref, mag_ref, theta_ref, chosen_ref, out_ref):
    devices, rows, width = out_ref.shape
    per = rows // 4
    other = jnp.dot(mag_ref[...], theta_ref[...], preferred_element_type=jnp.float32)
    high, low = high_low(mine_ref[...] + other)
    packed = jnp.dot(
        chosen_ref[...], jnp.concatenate([high, low], axis=1), preferred_element_type=jnp.float32
    ).astype(jnp.bfloat16)
    high = packed[:, :width].reshape(devices, per, width)
    out_ref[:, :per] = high
    out_ref[:, per : 2 * per] = packed[:, width:].reshape(devices, per, width)
    for at in range(devices):
        out_ref[at, 2 * per : 3 * per] = high[(at + 1) % devices]
        out_ref[at, 3 * per :] = high[(at - 1) % devices]


def is_odd():
    return lax.rem(lax.axis_index("phi"), 2) == 1


def edge_kernel(field_ref, other_ref, weight_ref, far_ref, near_ref, share_ref):
    layers, cells, width = field_ref.shape
    odd = is_odd()
    first = lax.axis_index("row") == 0
    slab, devices = lax.axis_index("phi"), lax.axis_size("phi")
    outer = lax.rem(slab + jnp.where(odd, 1, devices - 1), devices)
    share = share_weights(weight_ref[...], own_half())
    share_ref[...] = share
    far_share = share_weights(weight_ref[...], share_of(outer, lax.axis_index("row"), devices))
    near_weights, far_weights = share.astype(jnp.float32), far_share.astype(jnp.float32)

    def put(at, up, down):
        far_ref[at : at + up.shape[0]] = jnp.where(odd, up, down)
        near_ref[at : at + up.shape[0]] = jnp.where(odd, down, up)

    for layer in range(layers):
        up = [ref[layer, cells - REACH :] for ref in (field_ref, other_ref)]
        down = [ref[layer, :REACH] for ref in (field_ref, other_ref)]
        put(layer * REACH, jnp.where(first, *up), jnp.where(first, *down))
        put((layers + layer) * REACH, jnp.where(first, *up[::-1]), jnp.where(first, *down[::-1]))
    for part in range(share.shape[1] // width):
        at, piece = 2 * layers * REACH + 2 * part, slice(part * width, (part + 1) * width)
        near, far = near_weights[:, piece], far_weights[:, piece]
        far_ref[at : at + 2] = jnp.where(odd, far[cells - 2 :], far[:2])
        near_ref[at : at + 2] = jnp.where(odd, near[:2], near[cells - 2 :])


def sides(far_ref, near_ref):
    odd = is_odd()
    return (
        jnp.where(odd, far_ref[...], near_ref[...]),
        jnp.where(odd, near_ref[...], far_ref[...]),
    )


def coef_kernel(
    radial_ref, theta_ref, phi_ref, diag_ref, inv_ref, lon_ref, lat_ref, face_ref
):
    layers, spread, width = inv_ref.shape
    cells = spread - 8
    chunks = phi_ref.shape[0]
    total = chunks * width
    row = lax.broadcasted_iota(jnp.int32, (spread, width), 0)
    lane = lax.broadcasted_iota(jnp.int32, (spread, width), 1)
    cell = lax.axis_index("phi") * cells + jnp.where(row < cells + 4, row, row - spread)
    cell = jnp.where(cell < 0, cell + total, jnp.where(cell >= total, cell - total, cell))
    found = jnp.zeros((spread, width), jnp.float32)
    for chunk in range(chunks):
        found = found + jnp.where(lane + chunk * width == cell, phi_ref[chunk : chunk + 1], 0.0)
    column = jnp.broadcast_to(jnp.sum(found, axis=1, keepdims=True), (spread, width))
    lon_ref[0] = 0.5 * (column + pltpu.roll(column, spread - 1, 0))
    lon_ref[1] = 0.5 * (column + pltpu.roll(column, 1, 0))
    theta = jnp.broadcast_to(theta_ref[...], (8, width))
    ends = lax.broadcasted_iota(jnp.int32, (8, width), 1)
    upper = jnp.where(ends == width - 1, 0.0, 0.5 * (theta + pltpu.roll(theta, width - 1, 1)))
    lower = jnp.where(ends == 0, 0.0, 0.5 * (theta + pltpu.roll(theta, 1, 1)))
    lat_ref[0], lat_ref[1] = upper, lower
    flat = lon_ref[0] + lon_ref[1] + (upper + lower)[:1]
    faces = [
        0.5 * (radial_ref[max(face - 1, 0)] + radial_ref[min(face, layers - 1)])
        for face in range(layers + 1)
    ]
    for face in range(layers + 1):
        face_ref[face : face + 1] = jnp.full((1, width), faces[face], jnp.float32)
    for layer in range(layers):
        diag = flat + (faces[layer] + faces[layer + 1])
        diag_ref[layer] = diag
        inv_ref[layer] = 1.0 / diag


def boundary_kernel(got_ref, share_ref, far_ref, near_ref, out_ref):
    devices, rows, width = got_ref.shape
    cells, count = share_ref.shape
    per, spread = rows // 4, cells + 8
    above, below = sides(far_ref, near_ref)
    edge_rows = above.shape[0]

    def product(weights, first):
        data = [
            got_ref[:, which * per : (which + 1) * per].reshape(count, width)
            for which in (first, first + 1)
        ]
        total = jnp.dot(weights, jnp.concatenate(data, axis=1), preferred_element_type=jnp.float32)
        return total[:, :width], total[:, width:]

    def edge_weights(edge):
        at = edge_rows - 2 * count // width
        parts = [edge[at + 2 * k : at + 2 * k + 2] for k in range(count // width)]
        return jnp.concatenate(parts, axis=1)

    high, low = product(share_ref[...], 0)
    out_ref[:cells] = high + low
    weights = jnp.concatenate(
        [edge_weights(above), jnp.zeros((4, count), jnp.float32), edge_weights(below)], axis=0
    )
    from_below, from_above = product(weights.astype(jnp.bfloat16), 2)
    row = lax.broadcasted_iota(jnp.int32, (8, width), 0)
    out_ref[cells:spread] = jnp.where(row < 4, from_above, from_below)


def neighbours(values, layer, faces, lon, lat):
    mid = values[layer]
    spread, width = mid.shape
    total = lat[0] * pltpu.roll(mid, width - 1, 1) + lat[1] * pltpu.roll(mid, 1, 1)
    total = total + lon[0] * pltpu.roll(mid, spread - 1, 0)
    total = total + lon[1] * pltpu.roll(mid, 1, 0)
    for at, face in ((layer - 1, layer), (layer + 1, layer + 1)):
        if at in values:
            total = total + faces[face] * values[at]
    return total


def krylov_kernel(
    face_ref,
    field_ref,
    other_ref,
    far_ref,
    near_ref,
    diag_ref,
    inv_ref,
    lon_ref,
    lat_ref,
    totals_ref,
    low_ref,
    *vector_refs,
):
    layers, cells, width = field_ref.shape
    every, spread, _ = inv_ref.shape
    above, below = sides(far_ref, near_ref)
    gap = jnp.zeros((8 - 2 * REACH, width), jnp.float32)
    upper = lax.axis_index("row") == 1
    faces = [face_ref[face : face + 1] for face in range(every + 1)]
    lon, lat = (lon_ref[0], lon_ref[1]), (lat_ref[0, :1], lat_ref[1, :1])
    field = {}
    for layer in range(every):
        edge = slice(layer * REACH, (layer + 1) * REACH)
        at, high = layer % layers, layer >= layers
        block = jnp.where(upper == high, field_ref[at], other_ref[at])
        field[layer] = jnp.concatenate([block, above[edge], gap, below[edge]], axis=0)
    residual, first, image, second, image2 = {}, {}, {}, {}, {}
    for layer in range(every):
        value = neighbours(field, layer, faces, lon, lat) - diag_ref[layer] * field[layer]
        residual[layer] = value
        first[layer] = value * inv_ref[layer]
    for layer in range(every):
        image[layer] = residual[layer] - neighbours(first, layer, faces, lon, lat)
        second[layer] = image[layer] * inv_ref[layer]
    totals = [jnp.zeros((8, width), jnp.float32)] * 4
    for layer in range(every):
        image2[layer] = image[layer] - neighbours(second, layer, faces, lon, lat)
        vectors = [each[layer][:cells] for each in (residual, first, image, second, image2)]
        if layer < REACH:
            for which, vector in enumerate(vectors):
                low_ref[which, layer] = vector
        else:
            for which in range(4):
                product = vectors[which] * vectors[which + 1]
                for begin in range(0, cells, 8):
                    totals[which] = totals[which] + product[begin : begin + 8]
    for ref, vector in zip(vector_refs, (residual, first, image, second, image2)):
        for at in range(layers):
            ref[at] = jnp.where(upper, vector[layers + at], vector[at])[:cells]
    for which in range(4):
        totals_ref[which] = totals[which]


def boundary_effect_kernel(
    face_ref, part_ref, rest_ref, inv_ref, lon_ref, lat_ref, totals_ref, low_ref, sums_ref, change_ref
):
    _, reach, cells, width = low_ref.shape
    faces = [face_ref[face : face + 1] for face in range(reach + 1)]
    lon, lat = (lon_ref[0], lon_ref[1]), (lat_ref[0, :1], lat_ref[1, :1])
    source = faces[0] * (part_ref[...] + rest_ref[...])
    first = {0: source * inv_ref[0]}
    image = {0: source - neighbours(first, 0, faces, lon, lat), 1: -faces[1] * first[0]}
    second = {layer: image[layer] * inv_ref[layer] for layer in range(2)}
    image2 = {layer: image[layer] - neighbours(second, layer, faces, lon, lat) for layer in range(2)}
    image2[2] = -faces[2] * second[1]
    totals = [totals_ref[which] for which in range(4)]
    for layer in range(reach):
        vectors = []
        for which, change in enumerate(({0: source}, first, image, second, image2)):
            vector = low_ref[which, layer]
            if layer in change:
                change_ref[which, layer] = change[layer][:cells]
                vector = vector + change[layer][:cells]
            vectors.append(vector)
        for which in range(4):
            product = vectors[which] * vectors[which + 1]
            for begin in range(0, cells, 8):
                totals[which] = totals[which] + product[begin : begin + 8]
    lane = lax.broadcasted_iota(jnp.int32, (8, width), 1)
    packed = jnp.zeros((8, width), jnp.float32)
    for which, total in enumerate(totals):
        packed = jnp.where(lane == which, jnp.sum(total, axis=1, keepdims=True), packed)
    sums_ref[...] = jnp.broadcast_to(jnp.sum(packed, axis=0, keepdims=True), sums_ref.shape)


def update_kernel(
    sums_ref,
    field_ref,
    residual_ref,
    first_ref,
    image_ref,
    second_ref,
    image2_ref,
    change_ref,
    out_ref,
    left_ref,
):
    totals = jnp.sum(sums_ref[...], axis=0, keepdims=True)
    lane = lax.broadcasted_iota(jnp.int32, totals.shape, 1)
    a, b, c, e = (
        jnp.sum(jnp.where(lane == which, totals, 0.0), axis=1, keepdims=True) for which in range(4)
    )
    alpha, gain, alpha_next = step_sizes(a, b, c, e)
    along, back = alpha + alpha_next * gain, alpha_next * alpha
    here = jnp.where(lax.axis_index("row") == 0, 1.0, 0.0)
    reached = dict(zip(range(5), (1, 1, 2, 2, 3)))
    for layer in range(field_ref.shape[0]):
        vectors = []
        for which, ref in enumerate((residual_ref, first_ref, image_ref, second_ref, image2_ref)):
            vector = ref[layer]
            if layer < reached[which]:
                vector = vector + here * change_ref[which, layer]
            vectors.append(vector)
        residual, first, image, second, image2 = vectors
        out_ref[layer] = field_ref[layer] + (along * first - back * second)
        left_ref[layer] = residual - (along * image - back * image2)


SMALL = pltpu.CompilerParams(vmem_limit_bytes=8 << 20)


def in_vmem(count):
    return [pl.BlockSpec(memory_space=pltpu.VMEM)] * count


def paired_body(
    magnetogram,
    col_owner,
    col_offset,
    phi_weight,
    theta_weight,
    radial_coef,
    theta_coef,
    phi_coef,
    start_field,
):
    layers, cells, width = start_field.shape
    phi_devices = lax.axis_size("phi")
    per = phi_weight.shape[0] // phi_devices // 2
    count = phi_devices * per
    columns = magnetogram.shape[0]
    every, spread = 2 * layers, cells + 8
    real, half = jnp.float32, jnp.bfloat16
    struct = jax.ShapeDtypeStruct
    in_smem = [pl.BlockSpec(memory_space=pltpu.SMEM)]

    def swap(value):
        return lax.ppermute(value, "row", [(0, 1), (1, 0)])

    inner = [(i, i ^ 1) for i in range(phi_devices)]
    outer = [(i, (i + (1 if i % 2 else -1)) % phi_devices) for i in range(phi_devices)]

    def over_slabs(value, member, lead):
        order = [(lead - i) % phi_devices for i in range(phi_devices)]
        groups = [[2 * slab + member(slab, half) for slab in order] for half in range(2)]
        return lax.all_to_all(
            value,
            ("phi", "row"),
            split_axis=0,
            concat_axis=0,
            axis_index_groups=groups,
            tiled=True,
        )

    def in_hbm(value):
        return pltpu.with_memory_space_constraint(value, pltpu.HBM)

    mine, chosen = pl.pallas_call(
        column_kernel,
        compiler_params=SMALL,
        out_shape=[struct((columns, width), real), struct((count, columns), half)],
        in_specs=[pl.BlockSpec(memory_space=pltpu.HBM)] * 4,
        out_specs=in_vmem(2),
        scratch_shapes=[
            pltpu.VMEM(magnetogram.shape, half),
            pltpu.VMEM(theta_weight.shape, half),
            pltpu.VMEM((1, columns), jnp.int32),
            pltpu.VMEM((1, columns), jnp.int32),
            pltpu.SemaphoreType.DMA((4,)),
        ],
    )(
        in_hbm(magnetogram),
        in_hbm(theta_weight),
        in_hbm(col_owner.reshape(1, -1)),
        in_hbm(col_offset.reshape(1, -1)),
    )
    partner = swap(magnetogram), swap(theta_weight)
    other = swap(start_field)
    sent = pl.pallas_call(
        pack_kernel,
        compiler_params=SMALL,
        out_shape=struct((phi_devices, 4 * per, width), half),
        in_specs=in_vmem(4),
        out_specs=in_vmem(1)[0],
    )(mine, *partner, chosen)
    sent, radial_coef, theta_coef, phi_coef, field, other, weights = lax.optimization_barrier(
        (sent, radial_coef, theta_coef, phi_coef, start_field, other, phi_weight.T)
    )
    got = over_slabs(
        sent, lambda slab, half: int(share_of(slab, half, phi_devices)), leader(phi_devices)
    )
    edge = struct((every * REACH + 2 * count // width, width), real)
    far_edge, near_edge, share = pl.pallas_call(
        edge_kernel,
        compiler_params=SMALL,
        out_shape=[edge, edge, struct((cells, count), half)],
        in_specs=in_vmem(3),
        out_specs=in_vmem(3),
    )(field, other, weights)
    far_edge, near_edge = lax.ppermute(far_edge, "phi", outer), lax.ppermute(near_edge, "phi", inner)
    lines = struct((every, spread, width), real)
    diag, inv, lon, lat, faces = pl.pallas_call(
        coef_kernel,
        compiler_params=SMALL,
        out_shape=[
            lines,
            lines,
            struct((2, spread, width), real),
            struct((2, 8, width), real),
            struct((every + 1, width), real),
        ],
        in_specs=in_smem + in_vmem(2),
        out_specs=in_vmem(5),
    )(radial_coef, theta_coef.reshape(1, width), phi_coef.reshape(-1, width))
    got, far_edge, near_edge, diag, inv, lon, lat, faces = lax.optimization_barrier(
        (got, far_edge, near_edge, diag, inv, lon, lat, faces)
    )
    part = pl.pallas_call(
        boundary_kernel,
        compiler_params=SMALL,
        out_shape=struct((spread, width), real),
        in_specs=in_vmem(4),
        out_specs=in_vmem(1)[0],
    )(got, share, far_edge, near_edge)
    block = struct((layers, cells, width), real)
    totals, low, *vectors = pl.pallas_call(
        krylov_kernel,
        compiler_params=SMALL,
        out_shape=[struct((4, 8, width), real), struct((5, REACH, cells, width), real)]
        + [block] * 5,
        in_specs=in_vmem(9),
        out_specs=in_vmem(7),
    )(faces, field, other, far_edge, near_edge, diag, inv, lon, lat)
    sums, change = pl.pallas_call(
        boundary_effect_kernel,
        compiler_params=SMALL,
        out_shape=[struct((phi_devices, width), real), struct((5, REACH, cells, width), real)],
        in_specs=in_vmem(8),
        out_specs=in_vmem(2),
    )(faces, part, swap(part), inv, lon, lat, totals, low)
    sums = over_slabs(
        sums, lambda slab, half: int(share_of(slab, half, phi_devices)), leader(phi_devices)
    )
    return pl.pallas_call(
        update_kernel,
        compiler_params=SMALL,
        out_shape=[block] * 2,
        in_specs=in_vmem(8),
        out_specs=in_vmem(2),
    )(sums, field, *vectors, change)


def body(*args):
    phi_weight, phi_coef, start_field = args[3], args[7], args[8]
    layers, cells, width = start_field.shape
    phi_devices = lax.axis_size("phi")
    fits = (
        lax.axis_size("row") == 2
        and phi_devices > 2
        and phi_devices % 4 == 0
        and phi_weight.shape[0] % (32 * phi_devices) == 0
        and layers >= REACH
        and cells % 8 == 0
        and cells >= 16
        and width % 128 == 0
        and phi_coef.shape[0] % width == 0
        and phi_weight.shape[0] % (2 * width) == 0
        and (2 * layers * REACH) % 8 == 0
    )
    return (paired_body if fits else general_body)(*args)


def solution(mesh):
    in_specs = (
        P("phi", "row"),
        P("phi"),
        P("phi"),
        P(None, "phi"),
        P("row", None),
        P(),
        P(),
        P(),
        P("row", "phi", None),
    )
    out_specs = (P("row", "phi", None), P("row", "phi", None))
    return jax.shard_map(body, mesh=mesh, in_specs=in_specs, out_specs=out_specs, check_vma=False)
```

```python
import jax
import jax.numpy as jnp
from jax import lax
from jax.experimental import pallas as pl
from jax.experimental.pallas import tpu as pltpu
from jax.sharding import PartitionSpec as P

REACH = 3


def face_coefs(radial_coef, theta_coef, phi_coef):
    radial_mid = 0.5 * (radial_coef[:-1] + radial_coef[1:])
    radial_upper = jnp.concatenate([radial_mid, radial_coef[-1:]])
    radial_lower = jnp.concatenate([radial_coef[:1], radial_mid])
    theta_mid = 0.5 * (theta_coef[:-1] + theta_coef[1:])
    zero_one = jnp.zeros((1,), jnp.float32)
    theta_upper = jnp.concatenate([theta_mid, zero_one])
    theta_lower = jnp.concatenate([zero_one, theta_mid])
    phi_upper = 0.5 * (phi_coef + jnp.roll(phi_coef, -1))
    phi_lower = jnp.roll(phi_upper, 1)
    return (radial_upper, radial_lower, theta_upper, theta_lower, phi_upper, phi_lower)


def row_sum(value, rows):
    if rows == 2:
        return value + lax.ppermute(value, "row", [(0, 1), (1, 0)])
    return lax.psum(value, "row")


def pick(chunks, index):
    return lax.dynamic_index_in_dim(chunks, index, 0, keepdims=False)


def step_sizes(a, b, c, e):
    alpha = a / b
    beta = (alpha * alpha * c - a) / a
    gain = 1.0 + beta
    curvature = gain * gain * b - 2.0 * gain * alpha * c + alpha * alpha * e
    return alpha, gain, beta * a / curvature


def general_body(
    magnetogram,
    col_owner,
    col_offset,
    phi_weight,
    theta_weight,
    radial_coef,
    theta_coef,
    phi_coef,
    start_field,
):
    layers, cells, width = start_field.shape
    phi_devices = lax.axis_size("phi")
    rows = lax.axis_size("row")
    slots = phi_weight.shape[0]
    capacity = slots // phi_devices
    per = capacity // rows
    here = lax.axis_index("phi")
    row = lax.axis_index("row")
    above = lax.rem(here + 1, phi_devices)
    below = lax.rem(here + phi_devices - 1, phi_devices)

    climb = [(i, i + 1) for i in range(rows - 1)]
    low_layers = lax.ppermute(start_field[layers - REACH :], "row", climb)
    high_layers = lax.ppermute(start_field[:REACH], "row", [(t, s) for s, t in climb])
    window = jnp.concatenate([low_layers, start_field, high_layers], axis=0)

    columns = jnp.dot(magnetogram, theta_weight, preferred_element_type=jnp.float32)
    columns = row_sum(columns, rows)
    upper_part = lax.optimization_barrier(columns.astype(jnp.bfloat16))
    lower_part = (columns - upper_part.astype(jnp.float32)).astype(jnp.bfloat16)

    place = col_offset - row * per
    target = jnp.where((place >= 0) & (place < per), col_owner * per + place, -1)
    chosen = (target[None, :] == jnp.arange(phi_devices * per, dtype=jnp.int32)[:, None]).astype(
        jnp.bfloat16
    )
    packed = jnp.dot(chosen, upper_part, preferred_element_type=jnp.float32)
    packed = packed + jnp.dot(chosen, lower_part, preferred_element_type=jnp.float32)
    packed = packed.reshape(phi_devices, per, width)
    share = phi_weight.reshape(phi_devices, rows, per, cells)
    share = lax.dynamic_index_in_dim(share, row, 1, keepdims=False)
    share = share.reshape(phi_devices * per, cells)

    def edge(start):
        field = window[:, start : start + REACH].reshape(-1, width)
        lo = start + 1 if start else 0
        weights = share[:, lo : lo + 2].astype(jnp.float32).T.reshape(-1, width)
        return jnp.concatenate([field, weights], axis=0)

    to_above, to_below = edge(cells - REACH), edge(0)
    who = jnp.arange(phi_devices, dtype=jnp.int32)[:, None, None]
    edges = jnp.where(who == above, to_above[None], jnp.where(who == below, to_below[None], 0.0))
    sent = jnp.concatenate(
        [packed, jnp.roll(packed, 1, axis=0), jnp.roll(packed, -1, axis=0), edges], axis=1
    )
    got = lax.all_to_all(sent, "phi", split_axis=0, concat_axis=0, tiled=True)
    edge_low, edge_high = pick(got, below)[3 * per :], pick(got, above)[3 * per :]
    reach_rows = window.shape[0] * REACH

    def weigh(weights, which):
        data = got[:, which * per : (which + 1) * per].reshape(phi_devices * per, width)
        part = lax.optimization_barrier(data.astype(jnp.bfloat16))
        rest = (data - part.astype(jnp.float32)).astype(jnp.bfloat16)
        total = jnp.dot(weights, part, preferred_element_type=jnp.float32)
        return total + jnp.dot(weights, rest, preferred_element_type=jnp.float32)

    def ghost_weights(edge_rows):
        return edge_rows[reach_rows:].reshape(2, phi_devices * per).astype(jnp.bfloat16)

    boundary = row_sum(
        jnp.concatenate(
            [
                weigh(ghost_weights(edge_low), 1),
                weigh(share.T, 0),
                weigh(ghost_weights(edge_high), 2),
            ],
            axis=0,
        ),
        rows,
    )
    field = jnp.concatenate(
        [
            edge_low[:reach_rows].reshape(-1, REACH, width),
            window,
            edge_high[:reach_rows].reshape(-1, REACH, width),
        ],
        axis=1,
    )

    faces = face_coefs(radial_coef, theta_coef, phi_coef)
    spread = layers + 2 * REACH

    def radial_window(coef):
        padded = jnp.pad(coef, (REACH, REACH))
        return lax.dynamic_slice_in_dim(padded, row * layers, spread)[:, None, None]

    def phi_window(coef):
        padded = jnp.concatenate([coef[-REACH:], coef, coef[:REACH]])
        return lax.dynamic_slice_in_dim(padded, here * cells, cells + 2 * REACH)[None, :, None]

    rad_upper, rad_lower = radial_window(faces[0]), radial_window(faces[1])
    lon_upper, lon_lower = phi_window(faces[4]), phi_window(faces[5])
    lat_upper, lat_lower = faces[2][None, None, :], faces[3][None, None, :]
    inside = radial_window(jnp.ones_like(radial_coef))
    inv_diag = inside / (
        rad_upper + rad_lower + lat_upper + lat_lower + lon_upper + lon_lower + (1.0 - inside)
    )

    def apply_operator(value, depth):
        mid = value[1:-1, 1:-1]
        theta_pad = jnp.pad(mid, ((0, 0), (0, 0), (1, 1)))
        result = rad_upper[depth:-depth] * (mid - value[2:, 1:-1])
        result = result + rad_lower[depth:-depth] * (mid - value[:-2, 1:-1])
        result = result + lat_upper * (mid - theta_pad[:, :, 2:])
        result = result + lat_lower * (mid - theta_pad[:, :, :-2])
        result = result + lon_upper[:, depth:-depth] * (mid - value[1:-1, 2:])
        return result + lon_lower[:, depth:-depth] * (mid - value[1:-1, :-2])

    def inner(value, by):
        return value[by:-by, by:-by] if by else value

    level = row * layers - REACH + 1 + jnp.arange(spread - 2, dtype=jnp.int32)[:, None, None]
    source = jnp.where(level == 0, (faces[1][0] * boundary)[None], 0.0)
    residual = source - apply_operator(field, 1)
    first = residual * inner(inv_diag, 1)
    first_image = apply_operator(first, 2)
    second = first_image * inner(inv_diag, 2)
    second_image = apply_operator(second, 3)
    residual, first = inner(residual, 2), inner(first, 2)
    first_image, second = inner(first_image, 1), inner(second, 1)

    pairs = (
        (residual, first),
        (first, first_image),
        (first_image, second),
        (second, second_image),
    )
    sums = jnp.stack([jnp.sum(u * v, axis=(0, 1)) for u, v in pairs] * 2)
    devices = phi_devices * rows
    if devices <= 64:
        shared = jnp.broadcast_to(sums[None], (devices,) + sums.shape)
        shared = lax.all_to_all(shared, ("phi", "row"), split_axis=0, concat_axis=0, tiled=True)
        totals = jnp.sum(shared, axis=(0, 2))
    else:
        totals = lax.psum(jnp.sum(sums, axis=1), ("phi", "row"))
    alpha, gain, alpha_next = step_sizes(totals[0], totals[1], totals[2], totals[3])
    direction = gain * first - alpha * second
    solution_field = start_field + alpha * first + alpha_next * direction
    image = gain * first_image - alpha * second_image
    return solution_field, residual - alpha * first_image - alpha_next * image


def high_low(value):
    high = value.astype(jnp.bfloat16)
    return high, (value - high.astype(jnp.float32)).astype(jnp.bfloat16)


def leader(devices):
    return 10 * devices // 16


def seat(slab, devices):
    return lax.rem(leader(devices) - slab + devices, devices)


def share_of(slab, row, devices):
    return row ^ (slab >= devices // 2)


def own_half():
    devices = lax.axis_size("phi")
    return share_of(lax.axis_index("phi"), lax.axis_index("row"), devices)


def share_weights(weights, half):
    slots = weights.shape[1]
    devices = lax.axis_size("phi")
    per = slots // devices // 2
    slot = lax.broadcasted_iota(jnp.int32, (slots, slots // 2), 0)
    place = lax.broadcasted_iota(jnp.int32, (slots, slots // 2), 1)
    source = seat(place // per, devices)
    wanted = source * (2 * per) + half * per + place % per
    picker = jnp.where(slot == wanted, 1.0, 0.0).astype(jnp.bfloat16)
    return jnp.dot(weights, picker, preferred_element_type=jnp.float32).astype(jnp.bfloat16)


def column_kernel(
    mag_hbm,
    theta_hbm,
    owner_hbm,
    offset_hbm,
    out_ref,
    chosen_ref,
    mag_ref,
    theta_ref,
    owner_ref,
    offset_ref,
    done,
):
    pairs = (
        (theta_hbm, theta_ref),
        (mag_hbm, mag_ref),
        (owner_hbm, owner_ref),
        (offset_hbm, offset_ref),
    )
    copies = [pltpu.make_async_copy(*pair, done.at[at]) for at, pair in enumerate(pairs)]
    for copy in copies:
        copy.start()
    for copy in copies:
        copy.wait()
    out_ref[...] = jnp.dot(mag_ref[...], theta_ref[...], preferred_element_type=jnp.float32)
    devices = lax.axis_size("phi")
    per = chosen_ref.shape[0] // devices
    place = offset_ref[...] - own_half() * per
    target = jnp.where((place >= 0) & (place < per), seat(owner_ref[...], devices) * per + place, -1)
    slot = lax.broadcasted_iota(jnp.int32, chosen_ref.shape, 0)
    chosen_ref[...] = jnp.where(slot == target, 1.0, 0.0).astype(jnp.bfloat16)


def pack_kernel(mine_ref, mag_ref, theta_ref, chosen_ref, out_ref):
    devices, rows, width = out_ref.shape
    per = rows // 4
    other = jnp.dot(mag_ref[...], theta_ref[...], preferred_element_type=jnp.float32)
    high, low = high_low(mine_ref[...] + other)
    packed = jnp.dot(
        chosen_ref[...], jnp.concatenate([high, low], axis=1), preferred_element_type=jnp.float32
    ).astype(jnp.bfloat16)
    high = packed[:, :width].reshape(devices, per, width)
    out_ref[:, :per] = high
    out_ref[:, per : 2 * per] = packed[:, width:].reshape(devices, per, width)
    for at in range(devices):
        out_ref[at, 2 * per : 3 * per] = high[(at + 1) % devices]
        out_ref[at, 3 * per :] = high[(at - 1) % devices]


def is_odd():
    return lax.rem(lax.axis_index("phi"), 2) == 1


def edge_kernel(field_ref, other_ref, weight_ref, far_ref, near_ref, share_ref):
    layers, cells, width = field_ref.shape
    odd = is_odd()
    first = lax.axis_index("row") == 0
    slab, devices = lax.axis_index("phi"), lax.axis_size("phi")
    outer = lax.rem(slab + jnp.where(odd, 1, devices - 1), devices)
    share = share_weights(weight_ref[...], own_half())
    share_ref[...] = share
    far_share = share_weights(weight_ref[...], share_of(outer, lax.axis_index("row"), devices))
    near_weights, far_weights = share.astype(jnp.float32), far_share.astype(jnp.float32)

    def put(at, up, down):
        far_ref[at : at + up.shape[0]] = jnp.where(odd, up, down)
        near_ref[at : at + up.shape[0]] = jnp.where(odd, down, up)

    for layer in range(layers):
        up = [ref[layer, cells - REACH :] for ref in (field_ref, other_ref)]
        down = [ref[layer, :REACH] for ref in (field_ref, other_ref)]
        put(layer * REACH, jnp.where(first, *up), jnp.where(first, *down))
        put((layers + layer) * REACH, jnp.where(first, *up[::-1]), jnp.where(first, *down[::-1]))
    for part in range(share.shape[1] // width):
        at, piece = 2 * layers * REACH + 2 * part, slice(part * width, (part + 1) * width)
        near, far = near_weights[:, piece], far_weights[:, piece]
        far_ref[at : at + 2] = jnp.where(odd, far[cells - 2 :], far[:2])
        near_ref[at : at + 2] = jnp.where(odd, near[:2], near[cells - 2 :])


def sides(far_ref, near_ref):
    odd = is_odd()
    return (
        jnp.where(odd, far_ref[...], near_ref[...]),
        jnp.where(odd, near_ref[...], far_ref[...]),
    )


def coef_kernel(
    radial_ref, theta_ref, phi_ref, diag_ref, inv_ref, lon_ref, lat_ref, face_ref
):
    layers, spread, width = inv_ref.shape
    cells = spread - 8
    chunks = phi_ref.shape[0]
    total = chunks * width
    row = lax.broadcasted_iota(jnp.int32, (spread, width), 0)
    lane = lax.broadcasted_iota(jnp.int32, (spread, width), 1)
    cell = lax.axis_index("phi") * cells + jnp.where(row < cells + 4, row, row - spread)
    cell = jnp.where(cell < 0, cell + total, jnp.where(cell >= total, cell - total, cell))
    found = jnp.zeros((spread, width), jnp.float32)
    for chunk in range(chunks):
        found = found + jnp.where(lane + chunk * width == cell, phi_ref[chunk : chunk + 1], 0.0)
    column = jnp.broadcast_to(jnp.sum(found, axis=1, keepdims=True), (spread, width))
    lon_ref[0] = 0.5 * (column + pltpu.roll(column, spread - 1, 0))
    lon_ref[1] = 0.5 * (column + pltpu.roll(column, 1, 0))
    theta = jnp.broadcast_to(theta_ref[...], (8, width))
    ends = lax.broadcasted_iota(jnp.int32, (8, width), 1)
    upper = jnp.where(ends == width - 1, 0.0, 0.5 * (theta + pltpu.roll(theta, width - 1, 1)))
    lower = jnp.where(ends == 0, 0.0, 0.5 * (theta + pltpu.roll(theta, 1, 1)))
    lat_ref[0], lat_ref[1] = upper, lower
    flat = lon_ref[0] + lon_ref[1] + (upper + lower)[:1]
    faces = [
        0.5 * (radial_ref[max(face - 1, 0)] + radial_ref[min(face, layers - 1)])
        for face in range(layers + 1)
    ]
    for face in range(layers + 1):
        face_ref[face : face + 1] = jnp.full((1, width), faces[face], jnp.float32)
    for layer in range(layers):
        diag = flat + (faces[layer] + faces[layer + 1])
        diag_ref[layer] = diag
        inv_ref[layer] = 1.0 / diag


def boundary_kernel(got_ref, share_ref, far_ref, near_ref, out_ref):
    devices, rows, width = got_ref.shape
    cells, count = share_ref.shape
    per, spread = rows // 4, cells + 8
    above, below = sides(far_ref, near_ref)
    edge_rows = above.shape[0]

    def product(weights, first):
        data = [
            got_ref[:, which * per : (which + 1) * per].reshape(count, width)
            for which in (first, first + 1)
        ]
        total = jnp.dot(weights, jnp.concatenate(data, axis=1), preferred_element_type=jnp.float32)
        return total[:, :width], total[:, width:]

    def edge_weights(edge):
        at = edge_rows - 2 * count // width
        parts = [edge[at + 2 * k : at + 2 * k + 2] for k in range(count // width)]
        return jnp.concatenate(parts, axis=1)

    high, low = product(share_ref[...], 0)
    out_ref[:cells] = high + low
    weights = jnp.concatenate(
        [edge_weights(above), jnp.zeros((4, count), jnp.float32), edge_weights(below)], axis=0
    )
    from_below, from_above = product(weights.astype(jnp.bfloat16), 2)
    row = lax.broadcasted_iota(jnp.int32, (8, width), 0)
    out_ref[cells:spread] = jnp.where(row < 4, from_above, from_below)


def neighbours(values, layer, faces, lon, lat):
    mid = values[layer]
    spread, width = mid.shape
    total = lat[0] * pltpu.roll(mid, width - 1, 1) + lat[1] * pltpu.roll(mid, 1, 1)
    total = total + lon[0] * pltpu.roll(mid, spread - 1, 0)
    total = total + lon[1] * pltpu.roll(mid, 1, 0)
    for at, face in ((layer - 1, layer), (layer + 1, layer + 1)):
        if at in values:
            total = total + faces[face] * values[at]
    return total


def krylov_kernel(
    face_ref,
    field_ref,
    other_ref,
    far_ref,
    near_ref,
    diag_ref,
    inv_ref,
    lon_ref,
    lat_ref,
    totals_ref,
    low_ref,
    *vector_refs,
):
    layers, cells, width = field_ref.shape
    every, spread, _ = inv_ref.shape
    above, below = sides(far_ref, near_ref)
    gap = jnp.zeros((8 - 2 * REACH, width), jnp.float32)
    upper = lax.axis_index("row") == 1
    faces = [face_ref[face : face + 1] for face in range(every + 1)]
    lon, lat = (lon_ref[0], lon_ref[1]), (lat_ref[0, :1], lat_ref[1, :1])
    field = {}
    for layer in range(every):
        edge = slice(layer * REACH, (layer + 1) * REACH)
        at, high = layer % layers, layer >= layers
        block = jnp.where(upper == high, field_ref[at], other_ref[at])
        field[layer] = jnp.concatenate([block, above[edge], gap, below[edge]], axis=0)
    residual, first, image, second, image2 = {}, {}, {}, {}, {}
    for layer in range(every):
        value = neighbours(field, layer, faces, lon, lat) - diag_ref[layer] * field[layer]
        residual[layer] = value
        first[layer] = value * inv_ref[layer]
    for layer in range(every):
        image[layer] = residual[layer] - neighbours(first, layer, faces, lon, lat)
        second[layer] = image[layer] * inv_ref[layer]
    totals = [jnp.zeros((8, width), jnp.float32)] * 4
    for layer in range(every):
        image2[layer] = image[layer] - neighbours(second, layer, faces, lon, lat)
        vectors = [each[layer][:cells] for each in (residual, first, image, second, image2)]
        if layer < REACH:
            for which, vector in enumerate(vectors):
                low_ref[which, layer] = vector
        else:
            for which in range(4):
                product = vectors[which] * vectors[which + 1]
                for begin in range(0, cells, 8):
                    totals[which] = totals[which] + product[begin : begin + 8]
    for ref, vector in zip(vector_refs, (residual, first, image, second, image2)):
        for at in range(layers):
            ref[at] = jnp.where(upper, vector[layers + at], vector[at])[:cells]
    for which in range(4):
        totals_ref[which] = totals[which]


def boundary_effect_kernel(
    face_ref, part_ref, rest_ref, inv_ref, lon_ref, lat_ref, totals_ref, low_ref, sums_ref, change_ref
):
    _, reach, cells, width = low_ref.shape
    faces = [face_ref[face : face + 1] for face in range(reach + 1)]
    lon, lat = (lon_ref[0], lon_ref[1]), (lat_ref[0, :1], lat_ref[1, :1])
    source = faces[0] * (part_ref[...] + rest_ref[...])
    first = {0: source * inv_ref[0]}
    image = {0: source - neighbours(first, 0, faces, lon, lat), 1: -faces[1] * first[0]}
    second = {layer: image[layer] * inv_ref[layer] for layer in range(2)}
    image2 = {layer: image[layer] - neighbours(second, layer, faces, lon, lat) for layer in range(2)}
    image2[2] = -faces[2] * second[1]
    totals = [totals_ref[which] for which in range(4)]
    for layer in range(reach):
        vectors = []
        for which, change in enumerate(({0: source}, first, image, second, image2)):
            vector = low_ref[which, layer]
            if layer in change:
                change_ref[which, layer] = change[layer][:cells]
                vector = vector + change[layer][:cells]
            vectors.append(vector)
        for which in range(4):
            product = vectors[which] * vectors[which + 1]
            for begin in range(0, cells, 8):
                totals[which] = totals[which] + product[begin : begin + 8]
    lane = lax.broadcasted_iota(jnp.int32, (8, width), 1)
    packed = jnp.zeros((8, width), jnp.float32)
    for which, total in enumerate(totals):
        packed = jnp.where(lane == which, jnp.sum(total, axis=1, keepdims=True), packed)
    sums_ref[...] = jnp.broadcast_to(jnp.sum(packed, axis=0, keepdims=True), sums_ref.shape)


def update_kernel(
    sums_ref,
    field_ref,
    residual_ref,
    first_ref,
    image_ref,
    second_ref,
    image2_ref,
    change_ref,
    out_ref,
    left_ref,
):
    totals = jnp.sum(sums_ref[...], axis=0, keepdims=True)
    lane = lax.broadcasted_iota(jnp.int32, totals.shape, 1)
    a, b, c, e = (
        jnp.sum(jnp.where(lane == which, totals, 0.0), axis=1, keepdims=True) for which in range(4)
    )
    alpha, gain, alpha_next = step_sizes(a, b, c, e)
    along, back = alpha + alpha_next * gain, alpha_next * alpha
    here = jnp.where(lax.axis_index("row") == 0, 1.0, 0.0)
    reached = dict(zip(range(5), (1, 1, 2, 2, 3)))
    for layer in range(field_ref.shape[0]):
        vectors = []
        for which, ref in enumerate((residual_ref, first_ref, image_ref, second_ref, image2_ref)):
            vector = ref[layer]
            if layer < reached[which]:
                vector = vector + here * change_ref[which, layer]
            vectors.append(vector)
        residual, first, image, second, image2 = vectors
        out_ref[layer] = field_ref[layer] + (along * first - back * second)
        left_ref[layer] = residual - (along * image - back * image2)


SMALL = pltpu.CompilerParams(vmem_limit_bytes=8 << 20)


def in_vmem(count):
    return [pl.BlockSpec(memory_space=pltpu.VMEM)] * count


def paired_body(
    magnetogram,
    col_owner,
    col_offset,
    phi_weight,
    theta_weight,
    radial_coef,
    theta_coef,
    phi_coef,
    start_field,
):
    layers, cells, width = start_field.shape
    phi_devices = lax.axis_size("phi")
    per = phi_weight.shape[0] // phi_devices // 2
    count = phi_devices * per
    columns = magnetogram.shape[0]
    every, spread = 2 * layers, cells + 8
    real, half = jnp.float32, jnp.bfloat16
    struct = jax.ShapeDtypeStruct
    in_smem = [pl.BlockSpec(memory_space=pltpu.SMEM)]

    def swap(value):
        return lax.ppermute(value, "row", [(0, 1), (1, 0)])

    inner = [(i, i ^ 1) for i in range(phi_devices)]
    outer = [(i, (i + (1 if i % 2 else -1)) % phi_devices) for i in range(phi_devices)]

    def over_slabs(value, lead):
        order = [(lead - i) % phi_devices for i in range(phi_devices)]
        groups = [
            [2 * slab + int(share_of(slab, half, phi_devices)) for slab in order]
            for half in range(2)
        ]
        return lax.all_to_all(
            value,
            ("phi", "row"),
            split_axis=0,
            concat_axis=0,
            axis_index_groups=groups,
            tiled=True,
        )

    def in_hbm(value):
        return pltpu.with_memory_space_constraint(value, pltpu.HBM)

    mine, chosen = pl.pallas_call(
        column_kernel,
        compiler_params=SMALL,
        out_shape=[struct((columns, width), real), struct((count, columns), half)],
        in_specs=[pl.BlockSpec(memory_space=pltpu.HBM)] * 4,
        out_specs=in_vmem(2),
        scratch_shapes=[
            pltpu.VMEM(magnetogram.shape, half),
            pltpu.VMEM(theta_weight.shape, half),
            pltpu.VMEM((1, columns), jnp.int32),
            pltpu.VMEM((1, columns), jnp.int32),
            pltpu.SemaphoreType.DMA((4,)),
        ],
    )(
        in_hbm(magnetogram),
        in_hbm(theta_weight),
        in_hbm(col_owner.reshape(1, -1)),
        in_hbm(col_offset.reshape(1, -1)),
    )
    partner = swap(magnetogram), swap(theta_weight)
    other = swap(start_field)
    sent = pl.pallas_call(
        pack_kernel,
        compiler_params=SMALL,
        out_shape=struct((phi_devices, 4 * per, width), half),
        in_specs=in_vmem(4),
        out_specs=in_vmem(1)[0],
    )(mine, *partner, chosen)
    sent, radial_coef, theta_coef, phi_coef, field, other, weights = lax.optimization_barrier(
        (sent, radial_coef, theta_coef, phi_coef, start_field, other, phi_weight.T)
    )
    got = over_slabs(sent, leader(phi_devices))
    edge = struct((every * REACH + 2 * count // width, width), real)
    far_edge, near_edge, share = pl.pallas_call(
        edge_kernel,
        compiler_params=SMALL,
        out_shape=[edge, edge, struct((cells, count), half)],
        in_specs=in_vmem(3),
        out_specs=in_vmem(3),
    )(field, other, weights)
    far_edge, near_edge = lax.ppermute(far_edge, "phi", outer), lax.ppermute(near_edge, "phi", inner)
    lines = struct((every, spread, width), real)
    diag, inv, lon, lat, faces = pl.pallas_call(
        coef_kernel,
        compiler_params=SMALL,
        out_shape=[
            lines,
            lines,
            struct((2, spread, width), real),
            struct((2, 8, width), real),
            struct((every + 1, width), real),
        ],
        in_specs=in_smem + in_vmem(2),
        out_specs=in_vmem(5),
    )(radial_coef, theta_coef.reshape(1, width), phi_coef.reshape(-1, width))
    got, far_edge, near_edge, diag, inv, lon, lat, faces = lax.optimization_barrier(
        (got, far_edge, near_edge, diag, inv, lon, lat, faces)
    )
    part = pl.pallas_call(
        boundary_kernel,
        compiler_params=SMALL,
        out_shape=struct((spread, width), real),
        in_specs=in_vmem(4),
        out_specs=in_vmem(1)[0],
    )(got, share, far_edge, near_edge)
    block = struct((layers, cells, width), real)
    totals, low, *vectors = pl.pallas_call(
        krylov_kernel,
        compiler_params=SMALL,
        out_shape=[struct((4, 8, width), real), struct((5, REACH, cells, width), real)]
        + [block] * 5,
        in_specs=in_vmem(9),
        out_specs=in_vmem(7),
    )(faces, field, other, far_edge, near_edge, diag, inv, lon, lat)
    sums, change = pl.pallas_call(
        boundary_effect_kernel,
        compiler_params=SMALL,
        out_shape=[struct((phi_devices, width), real), struct((5, REACH, cells, width), real)],
        in_specs=in_vmem(8),
        out_specs=in_vmem(2),
    )(faces, part, swap(part), inv, lon, lat, totals, low)
    sums = over_slabs(sums, leader(phi_devices) + 1)
    return pl.pallas_call(
        update_kernel,
        compiler_params=SMALL,
        out_shape=[block] * 2,
        in_specs=in_vmem(8),
        out_specs=in_vmem(2),
    )(sums, field, *vectors, change)


def body(*args):
    phi_weight, phi_coef, start_field = args[3], args[7], args[8]
    layers, cells, width = start_field.shape
    phi_devices = lax.axis_size("phi")
    fits = (
        lax.axis_size("row") == 2
        and phi_devices > 2
        and phi_devices % 4 == 0
        and phi_weight.shape[0] % (32 * phi_devices) == 0
        and layers >= REACH
        and cells % 8 == 0
        and cells >= 16
        and width % 128 == 0
        and phi_coef.shape[0] % width == 0
        and phi_weight.shape[0] % (2 * width) == 0
        and (2 * layers * REACH) % 8 == 0
    )
    return (paired_body if fits else general_body)(*args)


def solution(mesh):
    in_specs = (
        P("phi", "row"),
        P("phi"),
        P("phi"),
        P(None, "phi"),
        P("row", None),
        P(),
        P(),
        P(),
        P("row", "phi", None),
    )
    out_specs = (P("row", "phi", None), P("row", "phi", None))
    return jax.shard_map(body, mesh=mesh, in_specs=in_specs, out_specs=out_specs, check_vma=False)
```

```python
import jax
import jax.numpy as jnp
from jax import lax
from jax.experimental import pallas as pl
from jax.experimental.pallas import tpu as pltpu
from jax.sharding import PartitionSpec as P

REACH = 3


def face_coefs(radial_coef, theta_coef, phi_coef):
    radial_mid = 0.5 * (radial_coef[:-1] + radial_coef[1:])
    radial_upper = jnp.concatenate([radial_mid, radial_coef[-1:]])
    radial_lower = jnp.concatenate([radial_coef[:1], radial_mid])
    theta_mid = 0.5 * (theta_coef[:-1] + theta_coef[1:])
    zero_one = jnp.zeros((1,), jnp.float32)
    theta_upper = jnp.concatenate([theta_mid, zero_one])
    theta_lower = jnp.concatenate([zero_one, theta_mid])
    phi_upper = 0.5 * (phi_coef + jnp.roll(phi_coef, -1))
    phi_lower = jnp.roll(phi_upper, 1)
    return (radial_upper, radial_lower, theta_upper, theta_lower, phi_upper, phi_lower)


def row_sum(value, rows):
    if rows == 2:
        return value + lax.ppermute(value, "row", [(0, 1), (1, 0)])
    return lax.psum(value, "row")


def pick(chunks, index):
    return lax.dynamic_index_in_dim(chunks, index, 0, keepdims=False)


def step_sizes(a, b, c, e):
    alpha = a / b
    beta = (alpha * alpha * c - a) / a
    gain = 1.0 + beta
    curvature = gain * gain * b - 2.0 * gain * alpha * c + alpha * alpha * e
    return alpha, gain, beta * a / curvature


def general_body(
    magnetogram,
    col_owner,
    col_offset,
    phi_weight,
    theta_weight,
    radial_coef,
    theta_coef,
    phi_coef,
    start_field,
):
    layers, cells, width = start_field.shape
    phi_devices = lax.axis_size("phi")
    rows = lax.axis_size("row")
    slots = phi_weight.shape[0]
    capacity = slots // phi_devices
    per = capacity // rows
    here = lax.axis_index("phi")
    row = lax.axis_index("row")
    above = lax.rem(here + 1, phi_devices)
    below = lax.rem(here + phi_devices - 1, phi_devices)

    climb = [(i, i + 1) for i in range(rows - 1)]
    low_layers = lax.ppermute(start_field[layers - REACH :], "row", climb)
    high_layers = lax.ppermute(start_field[:REACH], "row", [(t, s) for s, t in climb])
    window = jnp.concatenate([low_layers, start_field, high_layers], axis=0)

    columns = jnp.dot(magnetogram, theta_weight, preferred_element_type=jnp.float32)
    columns = row_sum(columns, rows)
    upper_part = lax.optimization_barrier(columns.astype(jnp.bfloat16))
    lower_part = (columns - upper_part.astype(jnp.float32)).astype(jnp.bfloat16)

    place = col_offset - row * per
    target = jnp.where((place >= 0) & (place < per), col_owner * per + place, -1)
    chosen = (target[None, :] == jnp.arange(phi_devices * per, dtype=jnp.int32)[:, None]).astype(
        jnp.bfloat16
    )
    packed = jnp.dot(chosen, upper_part, preferred_element_type=jnp.float32)
    packed = packed + jnp.dot(chosen, lower_part, preferred_element_type=jnp.float32)
    packed = packed.reshape(phi_devices, per, width)
    share = phi_weight.reshape(phi_devices, rows, per, cells)
    share = lax.dynamic_index_in_dim(share, row, 1, keepdims=False)
    share = share.reshape(phi_devices * per, cells)

    def edge(start):
        field = window[:, start : start + REACH].reshape(-1, width)
        lo = start + 1 if start else 0
        weights = share[:, lo : lo + 2].astype(jnp.float32).T.reshape(-1, width)
        return jnp.concatenate([field, weights], axis=0)

    to_above, to_below = edge(cells - REACH), edge(0)
    who = jnp.arange(phi_devices, dtype=jnp.int32)[:, None, None]
    edges = jnp.where(who == above, to_above[None], jnp.where(who == below, to_below[None], 0.0))
    sent = jnp.concatenate(
        [packed, jnp.roll(packed, 1, axis=0), jnp.roll(packed, -1, axis=0), edges], axis=1
    )
    got = lax.all_to_all(sent, "phi", split_axis=0, concat_axis=0, tiled=True)
    edge_low, edge_high = pick(got, below)[3 * per :], pick(got, above)[3 * per :]
    reach_rows = window.shape[0] * REACH

    def weigh(weights, which):
        data = got[:, which * per : (which + 1) * per].reshape(phi_devices * per, width)
        part = lax.optimization_barrier(data.astype(jnp.bfloat16))
        rest = (data - part.astype(jnp.float32)).astype(jnp.bfloat16)
        total = jnp.dot(weights, part, preferred_element_type=jnp.float32)
        return total + jnp.dot(weights, rest, preferred_element_type=jnp.float32)

    def ghost_weights(edge_rows):
        return edge_rows[reach_rows:].reshape(2, phi_devices * per).astype(jnp.bfloat16)

    boundary = row_sum(
        jnp.concatenate(
            [
                weigh(ghost_weights(edge_low), 1),
                weigh(share.T, 0),
                weigh(ghost_weights(edge_high), 2),
            ],
            axis=0,
        ),
        rows,
    )
    field = jnp.concatenate(
        [
            edge_low[:reach_rows].reshape(-1, REACH, width),
            window,
            edge_high[:reach_rows].reshape(-1, REACH, width),
        ],
        axis=1,
    )

    faces = face_coefs(radial_coef, theta_coef, phi_coef)
    spread = layers + 2 * REACH

    def radial_window(coef):
        padded = jnp.pad(coef, (REACH, REACH))
        return lax.dynamic_slice_in_dim(padded, row * layers, spread)[:, None, None]

    def phi_window(coef):
        padded = jnp.concatenate([coef[-REACH:], coef, coef[:REACH]])
        return lax.dynamic_slice_in_dim(padded, here * cells, cells + 2 * REACH)[None, :, None]

    rad_upper, rad_lower = radial_window(faces[0]), radial_window(faces[1])
    lon_upper, lon_lower = phi_window(faces[4]), phi_window(faces[5])
    lat_upper, lat_lower = faces[2][None, None, :], faces[3][None, None, :]
    inside = radial_window(jnp.ones_like(radial_coef))
    inv_diag = inside / (
        rad_upper + rad_lower + lat_upper + lat_lower + lon_upper + lon_lower + (1.0 - inside)
    )

    def apply_operator(value, depth):
        mid = value[1:-1, 1:-1]
        theta_pad = jnp.pad(mid, ((0, 0), (0, 0), (1, 1)))
        result = rad_upper[depth:-depth] * (mid - value[2:, 1:-1])
        result = result + rad_lower[depth:-depth] * (mid - value[:-2, 1:-1])
        result = result + lat_upper * (mid - theta_pad[:, :, 2:])
        result = result + lat_lower * (mid - theta_pad[:, :, :-2])
        result = result + lon_upper[:, depth:-depth] * (mid - value[1:-1, 2:])
        return result + lon_lower[:, depth:-depth] * (mid - value[1:-1, :-2])

    def inner(value, by):
        return value[by:-by, by:-by] if by else value

    level = row * layers - REACH + 1 + jnp.arange(spread - 2, dtype=jnp.int32)[:, None, None]
    source = jnp.where(level == 0, (faces[1][0] * boundary)[None], 0.0)
    residual = source - apply_operator(field, 1)
    first = residual * inner(inv_diag, 1)
    first_image = apply_operator(first, 2)
    second = first_image * inner(inv_diag, 2)
    second_image = apply_operator(second, 3)
    residual, first = inner(residual, 2), inner(first, 2)
    first_image, second = inner(first_image, 1), inner(second, 1)

    pairs = (
        (residual, first),
        (first, first_image),
        (first_image, second),
        (second, second_image),
    )
    sums = jnp.stack([jnp.sum(u * v, axis=(0, 1)) for u, v in pairs] * 2)
    devices = phi_devices * rows
    if devices <= 64:
        shared = jnp.broadcast_to(sums[None], (devices,) + sums.shape)
        shared = lax.all_to_all(shared, ("phi", "row"), split_axis=0, concat_axis=0, tiled=True)
        totals = jnp.sum(shared, axis=(0, 2))
    else:
        totals = lax.psum(jnp.sum(sums, axis=1), ("phi", "row"))
    alpha, gain, alpha_next = step_sizes(totals[0], totals[1], totals[2], totals[3])
    direction = gain * first - alpha * second
    solution_field = start_field + alpha * first + alpha_next * direction
    image = gain * first_image - alpha * second_image
    return solution_field, residual - alpha * first_image - alpha_next * image


def high_low(value):
    high = value.astype(jnp.bfloat16)
    return high, (value - high.astype(jnp.float32)).astype(jnp.bfloat16)


def leader(devices):
    return 10 * devices // 16


def seat(slab, devices):
    return lax.rem(leader(devices) - slab + devices, devices)


def share_of(slab, row, devices):
    return row ^ (slab >= devices // 2)


def own_half():
    devices = lax.axis_size("phi")
    return share_of(lax.axis_index("phi"), lax.axis_index("row"), devices)


def outer_slab():
    slab, devices = lax.axis_index("phi"), lax.axis_size("phi")
    return lax.rem(slab + jnp.where(is_odd(), 1, devices - 1), devices)


def slot_picker(shape, half):
    devices = lax.axis_size("phi")
    per = shape[1] // devices
    slot = lax.broadcasted_iota(jnp.int32, shape, 0)
    place = lax.broadcasted_iota(jnp.int32, shape, 1)
    wanted = seat(place // per, devices) * (2 * per) + half * per + place % per
    return jnp.where(slot == wanted, 1.0, 0.0).astype(jnp.bfloat16)


def column_kernel(
    mag_hbm,
    theta_hbm,
    owner_hbm,
    offset_hbm,
    out_ref,
    chosen_ref,
    picker_ref,
    mag_ref,
    theta_ref,
    owner_ref,
    offset_ref,
    done,
):
    pairs = (
        (theta_hbm, theta_ref),
        (mag_hbm, mag_ref),
        (owner_hbm, owner_ref),
        (offset_hbm, offset_ref),
    )
    copies = [pltpu.make_async_copy(*pair, done.at[at]) for at, pair in enumerate(pairs)]
    for copy in copies:
        copy.start()
    outer_half = share_of(outer_slab(), lax.axis_index("row"), lax.axis_size("phi"))
    for which, half in enumerate((own_half(), outer_half)):
        picker_ref[which] = slot_picker(picker_ref.shape[1:], half)
    for copy in copies:
        copy.wait()
    out_ref[...] = jnp.dot(mag_ref[...], theta_ref[...], preferred_element_type=jnp.float32)
    devices = lax.axis_size("phi")
    per = chosen_ref.shape[0] // devices
    place = offset_ref[...] - own_half() * per
    target = jnp.where((place >= 0) & (place < per), seat(owner_ref[...], devices) * per + place, -1)
    slot = lax.broadcasted_iota(jnp.int32, chosen_ref.shape, 0)
    chosen_ref[...] = jnp.where(slot == target, 1.0, 0.0).astype(jnp.bfloat16)


def pack_kernel(mine_ref, mag_ref, theta_ref, chosen_ref, out_ref):
    devices, rows, width = out_ref.shape
    per = rows // 4
    other = jnp.dot(mag_ref[...], theta_ref[...], preferred_element_type=jnp.float32)
    high, low = high_low(mine_ref[...] + other)
    packed = jnp.dot(
        chosen_ref[...], jnp.concatenate([high, low], axis=1), preferred_element_type=jnp.float32
    ).astype(jnp.bfloat16)
    high = packed[:, :width].reshape(devices, per, width)
    out_ref[:, :per] = high
    out_ref[:, per : 2 * per] = packed[:, width:].reshape(devices, per, width)
    for at in range(devices):
        out_ref[at, 2 * per : 3 * per] = high[(at + 1) % devices]
        out_ref[at, 3 * per :] = high[(at - 1) % devices]


def is_odd():
    return lax.rem(lax.axis_index("phi"), 2) == 1


def edge_kernel(field_ref, other_ref, weight_ref, picker_ref, far_ref, near_ref, share_ref):
    layers, cells, width = field_ref.shape
    odd = is_odd()
    first = lax.axis_index("row") == 0
    share, far_share = (
        jnp.dot(weight_ref[...], picker_ref[which], preferred_element_type=jnp.float32).astype(
            jnp.bfloat16
        )
        for which in range(2)
    )
    share_ref[...] = share
    near_weights, far_weights = share.astype(jnp.float32), far_share.astype(jnp.float32)

    def put(at, up, down):
        far_ref[at : at + up.shape[0]] = jnp.where(odd, up, down)
        near_ref[at : at + up.shape[0]] = jnp.where(odd, down, up)

    for layer in range(layers):
        up = [ref[layer, cells - REACH :] for ref in (field_ref, other_ref)]
        down = [ref[layer, :REACH] for ref in (field_ref, other_ref)]
        put(layer * REACH, jnp.where(first, *up), jnp.where(first, *down))
        put((layers + layer) * REACH, jnp.where(first, *up[::-1]), jnp.where(first, *down[::-1]))
    for part in range(share.shape[1] // width):
        at, piece = 2 * layers * REACH + 2 * part, slice(part * width, (part + 1) * width)
        near, far = near_weights[:, piece], far_weights[:, piece]
        far_ref[at : at + 2] = jnp.where(odd, far[cells - 2 :], far[:2])
        near_ref[at : at + 2] = jnp.where(odd, near[:2], near[cells - 2 :])


def sides(far_ref, near_ref):
    odd = is_odd()
    return (
        jnp.where(odd, far_ref[...], near_ref[...]),
        jnp.where(odd, near_ref[...], far_ref[...]),
    )


def coef_kernel(
    radial_ref, theta_ref, phi_ref, diag_ref, inv_ref, lon_ref, lat_ref, face_ref
):
    layers, spread, width = inv_ref.shape
    cells = spread - 8
    chunks = phi_ref.shape[0]
    total = chunks * width
    row = lax.broadcasted_iota(jnp.int32, (spread, width), 0)
    lane = lax.broadcasted_iota(jnp.int32, (spread, width), 1)
    cell = lax.axis_index("phi") * cells + jnp.where(row < cells + 4, row, row - spread)
    cell = jnp.where(cell < 0, cell + total, jnp.where(cell >= total, cell - total, cell))
    found = jnp.zeros((spread, width), jnp.float32)
    for chunk in range(chunks):
        found = found + jnp.where(lane + chunk * width == cell, phi_ref[chunk : chunk + 1], 0.0)
    column = jnp.broadcast_to(jnp.sum(found, axis=1, keepdims=True), (spread, width))
    lon_ref[0] = 0.5 * (column + pltpu.roll(column, spread - 1, 0))
    lon_ref[1] = 0.5 * (column + pltpu.roll(column, 1, 0))
    theta = jnp.broadcast_to(theta_ref[...], (8, width))
    ends = lax.broadcasted_iota(jnp.int32, (8, width), 1)
    upper = jnp.where(ends == width - 1, 0.0, 0.5 * (theta + pltpu.roll(theta, width - 1, 1)))
    lower = jnp.where(ends == 0, 0.0, 0.5 * (theta + pltpu.roll(theta, 1, 1)))
    lat_ref[0], lat_ref[1] = upper, lower
    flat = lon_ref[0] + lon_ref[1] + (upper + lower)[:1]
    faces = [
        0.5 * (radial_ref[max(face - 1, 0)] + radial_ref[min(face, layers - 1)])
        for face in range(layers + 1)
    ]
    for face in range(layers + 1):
        face_ref[face : face + 1] = jnp.full((1, width), faces[face], jnp.float32)
    for layer in range(layers):
        diag = flat + (faces[layer] + faces[layer + 1])
        diag_ref[layer] = diag
        inv_ref[layer] = 1.0 / diag


def boundary_kernel(got_ref, share_ref, far_ref, near_ref, out_ref):
    devices, rows, width = got_ref.shape
    cells, count = share_ref.shape
    per, spread = rows // 4, cells + 8
    above, below = sides(far_ref, near_ref)
    edge_rows = above.shape[0]

    def product(weights, first):
        data = [
            got_ref[:, which * per : (which + 1) * per].reshape(count, width)
            for which in (first, first + 1)
        ]
        total = jnp.dot(weights, jnp.concatenate(data, axis=1), preferred_element_type=jnp.float32)
        return total[:, :width], total[:, width:]

    def edge_weights(edge):
        at = edge_rows - 2 * count // width
        parts = [edge[at + 2 * k : at + 2 * k + 2] for k in range(count // width)]
        return jnp.concatenate(parts, axis=1)

    high, low = product(share_ref[...], 0)
    out_ref[:cells] = high + low
    weights = jnp.concatenate(
        [edge_weights(above), jnp.zeros((4, count), jnp.float32), edge_weights(below)], axis=0
    )
    from_below, from_above = product(weights.astype(jnp.bfloat16), 2)
    row = lax.broadcasted_iota(jnp.int32, (8, width), 0)
    out_ref[cells:spread] = jnp.where(row < 4, from_above, from_below)


def neighbours(values, layer, faces, lon, lat):
    mid = values[layer]
    spread, width = mid.shape
    total = lat[0] * pltpu.roll(mid, width - 1, 1) + lat[1] * pltpu.roll(mid, 1, 1)
    total = total + lon[0] * pltpu.roll(mid, spread - 1, 0)
    total = total + lon[1] * pltpu.roll(mid, 1, 0)
    for at, face in ((layer - 1, layer), (layer + 1, layer + 1)):
        if at in values:
            total = total + faces[face] * values[at]
    return total


def krylov_kernel(
    face_ref,
    field_ref,
    other_ref,
    far_ref,
    near_ref,
    diag_ref,
    inv_ref,
    lon_ref,
    lat_ref,
    totals_ref,
    low_ref,
    *vector_refs,
):
    layers, cells, width = field_ref.shape
    every, spread, _ = inv_ref.shape
    above, below = sides(far_ref, near_ref)
    gap = jnp.zeros((8 - 2 * REACH, width), jnp.float32)
    upper = lax.axis_index("row") == 1
    faces = [face_ref[face : face + 1] for face in range(every + 1)]
    lon, lat = (lon_ref[0], lon_ref[1]), (lat_ref[0, :1], lat_ref[1, :1])
    field = {}
    for layer in range(every):
        edge = slice(layer * REACH, (layer + 1) * REACH)
        at, high = layer % layers, layer >= layers
        block = jnp.where(upper == high, field_ref[at], other_ref[at])
        field[layer] = jnp.concatenate([block, above[edge], gap, below[edge]], axis=0)
    residual, first, image, second, image2 = {}, {}, {}, {}, {}
    for layer in range(every):
        value = neighbours(field, layer, faces, lon, lat) - diag_ref[layer] * field[layer]
        residual[layer] = value
        first[layer] = value * inv_ref[layer]
    for layer in range(every):
        image[layer] = residual[layer] - neighbours(first, layer, faces, lon, lat)
        second[layer] = image[layer] * inv_ref[layer]
    totals = [jnp.zeros((8, width), jnp.float32)] * 4
    for layer in range(every):
        image2[layer] = image[layer] - neighbours(second, layer, faces, lon, lat)
        vectors = [each[layer][:cells] for each in (residual, first, image, second, image2)]
        if layer < REACH:
            for which, vector in enumerate(vectors):
                low_ref[which, layer] = vector
        else:
            for which in range(4):
                product = vectors[which] * vectors[which + 1]
                for begin in range(0, cells, 8):
                    totals[which] = totals[which] + product[begin : begin + 8]
    for ref, vector in zip(vector_refs, (residual, first, image, second, image2)):
        for at in range(layers):
            ref[at] = jnp.where(upper, vector[layers + at], vector[at])[:cells]
    for which in range(4):
        totals_ref[which] = totals[which]


def boundary_effect_kernel(
    face_ref, part_ref, rest_ref, inv_ref, lon_ref, lat_ref, totals_ref, low_ref, sums_ref, change_ref
):
    _, reach, cells, width = low_ref.shape
    faces = [face_ref[face : face + 1] for face in range(reach + 1)]
    lon, lat = (lon_ref[0], lon_ref[1]), (lat_ref[0, :1], lat_ref[1, :1])
    source = faces[0] * (part_ref[...] + rest_ref[...])
    first = {0: source * inv_ref[0]}
    image = {0: source - neighbours(first, 0, faces, lon, lat), 1: -faces[1] * first[0]}
    second = {layer: image[layer] * inv_ref[layer] for layer in range(2)}
    image2 = {layer: image[layer] - neighbours(second, layer, faces, lon, lat) for layer in range(2)}
    image2[2] = -faces[2] * second[1]
    totals = [totals_ref[which] for which in range(4)]
    for layer in range(reach):
        vectors = []
        for which, change in enumerate(({0: source}, first, image, second, image2)):
            vector = low_ref[which, layer]
            if layer in change:
                change_ref[which, layer] = change[layer][:cells]
                vector = vector + change[layer][:cells]
            vectors.append(vector)
        for which in range(4):
            product = vectors[which] * vectors[which + 1]
            for begin in range(0, cells, 8):
                totals[which] = totals[which] + product[begin : begin + 8]
    lane = lax.broadcasted_iota(jnp.int32, (8, width), 1)
    packed = jnp.zeros((8, width), jnp.float32)
    for which, total in enumerate(totals):
        packed = jnp.where(lane == which, jnp.sum(total, axis=1, keepdims=True), packed)
    sums_ref[...] = jnp.broadcast_to(jnp.sum(packed, axis=0, keepdims=True), sums_ref.shape)


def update_kernel(
    sums_ref,
    field_ref,
    residual_ref,
    first_ref,
    image_ref,
    second_ref,
    image2_ref,
    change_ref,
    out_ref,
    left_ref,
):
    totals = jnp.sum(sums_ref[...], axis=0, keepdims=True)
    lane = lax.broadcasted_iota(jnp.int32, totals.shape, 1)
    a, b, c, e = (
        jnp.sum(jnp.where(lane == which, totals, 0.0), axis=1, keepdims=True) for which in range(4)
    )
    alpha, gain, alpha_next = step_sizes(a, b, c, e)
    along, back = alpha + alpha_next * gain, alpha_next * alpha
    here = jnp.where(lax.axis_index("row") == 0, 1.0, 0.0)
    reached = dict(zip(range(5), (1, 1, 2, 2, 3)))
    for layer in range(field_ref.shape[0]):
        vectors = []
        for which, ref in enumerate((residual_ref, first_ref, image_ref, second_ref, image2_ref)):
            vector = ref[layer]
            if layer < reached[which]:
                vector = vector + here * change_ref[which, layer]
            vectors.append(vector)
        residual, first, image, second, image2 = vectors
        out_ref[layer] = field_ref[layer] + (along * first - back * second)
        left_ref[layer] = residual - (along * image - back * image2)


SMALL = pltpu.CompilerParams(vmem_limit_bytes=8 << 20)


def in_vmem(count):
    return [pl.BlockSpec(memory_space=pltpu.VMEM)] * count


def paired_body(
    magnetogram,
    col_owner,
    col_offset,
    phi_weight,
    theta_weight,
    radial_coef,
    theta_coef,
    phi_coef,
    start_field,
):
    layers, cells, width = start_field.shape
    phi_devices = lax.axis_size("phi")
    per = phi_weight.shape[0] // phi_devices // 2
    count = phi_devices * per
    columns = magnetogram.shape[0]
    every, spread = 2 * layers, cells + 8
    real, half = jnp.float32, jnp.bfloat16
    struct = jax.ShapeDtypeStruct
    in_smem = [pl.BlockSpec(memory_space=pltpu.SMEM)]

    def swap(value):
        return lax.ppermute(value, "row", [(0, 1), (1, 0)])

    inner = [(i, i ^ 1) for i in range(phi_devices)]
    outer = [(i, (i + (1 if i % 2 else -1)) % phi_devices) for i in range(phi_devices)]

    def over_slabs(value, lead):
        order = [(lead - i) % phi_devices for i in range(phi_devices)]
        groups = [
            [2 * slab + int(share_of(slab, half, phi_devices)) for slab in order]
            for half in range(2)
        ]
        return lax.all_to_all(
            value,
            ("phi", "row"),
            split_axis=0,
            concat_axis=0,
            axis_index_groups=groups,
            tiled=True,
        )

    def in_hbm(value):
        return pltpu.with_memory_space_constraint(value, pltpu.HBM)

    mine, chosen, picker = pl.pallas_call(
        column_kernel,
        compiler_params=SMALL,
        out_shape=[
            struct((columns, width), real),
            struct((count, columns), half),
            struct((2, 2 * count, count), half),
        ],
        in_specs=[pl.BlockSpec(memory_space=pltpu.HBM)] * 4,
        out_specs=in_vmem(3),
        scratch_shapes=[
            pltpu.VMEM(magnetogram.shape, half),
            pltpu.VMEM(theta_weight.shape, half),
            pltpu.VMEM((1, columns), jnp.int32),
            pltpu.VMEM((1, columns), jnp.int32),
            pltpu.SemaphoreType.DMA((4,)),
        ],
    )(
        in_hbm(magnetogram),
        in_hbm(theta_weight),
        in_hbm(col_owner.reshape(1, -1)),
        in_hbm(col_offset.reshape(1, -1)),
    )
    partner = swap(magnetogram), swap(theta_weight)
    other = swap(start_field)
    sent = pl.pallas_call(
        pack_kernel,
        compiler_params=SMALL,
        out_shape=struct((phi_devices, 4 * per, width), half),
        in_specs=in_vmem(4),
        out_specs=in_vmem(1)[0],
    )(mine, *partner, chosen)
    sent, radial_coef, theta_coef, phi_coef, field, other, weights = lax.optimization_barrier(
        (sent, radial_coef, theta_coef, phi_coef, start_field, other, phi_weight.T)
    )
    got = over_slabs(sent, leader(phi_devices))
    edge = struct((every * REACH + 2 * count // width, width), real)
    far_edge, near_edge, share = pl.pallas_call(
        edge_kernel,
        compiler_params=SMALL,
        out_shape=[edge, edge, struct((cells, count), half)],
        in_specs=in_vmem(4),
        out_specs=in_vmem(3),
    )(field, other, weights, picker)
    far_edge, near_edge = lax.ppermute(far_edge, "phi", outer), lax.ppermute(near_edge, "phi", inner)
    lines = struct((every, spread, width), real)
    diag, inv, lon, lat, faces = pl.pallas_call(
        coef_kernel,
        compiler_params=SMALL,
        out_shape=[
            lines,
            lines,
            struct((2, spread, width), real),
            struct((2, 8, width), real),
            struct((every + 1, width), real),
        ],
        in_specs=in_smem + in_vmem(2),
        out_specs=in_vmem(5),
    )(radial_coef, theta_coef.reshape(1, width), phi_coef.reshape(-1, width))
    got, far_edge, near_edge, diag, inv, lon, lat, faces = lax.optimization_barrier(
        (got, far_edge, near_edge, diag, inv, lon, lat, faces)
    )
    part = pl.pallas_call(
        boundary_kernel,
        compiler_params=SMALL,
        out_shape=struct((spread, width), real),
        in_specs=in_vmem(4),
        out_specs=in_vmem(1)[0],
    )(got, share, far_edge, near_edge)
    block = struct((layers, cells, width), real)
    totals, low, *vectors = pl.pallas_call(
        krylov_kernel,
        compiler_params=SMALL,
        out_shape=[struct((4, 8, width), real), struct((5, REACH, cells, width), real)]
        + [block] * 5,
        in_specs=in_vmem(9),
        out_specs=in_vmem(7),
    )(faces, field, other, far_edge, near_edge, diag, inv, lon, lat)
    sums, change = pl.pallas_call(
        boundary_effect_kernel,
        compiler_params=SMALL,
        out_shape=[struct((phi_devices, width), real), struct((5, REACH, cells, width), real)],
        in_specs=in_vmem(8),
        out_specs=in_vmem(2),
    )(faces, part, swap(part), inv, lon, lat, totals, low)
    sums = over_slabs(sums, leader(phi_devices) + 1)
    return pl.pallas_call(
        update_kernel,
        compiler_params=SMALL,
        out_shape=[block] * 2,
        in_specs=in_vmem(8),
        out_specs=in_vmem(2),
    )(sums, field, *vectors, change)


def body(*args):
    phi_weight, phi_coef, start_field = args[3], args[7], args[8]
    layers, cells, width = start_field.shape
    phi_devices = lax.axis_size("phi")
    fits = (
        lax.axis_size("row") == 2
        and phi_devices > 2
        and phi_devices % 4 == 0
        and phi_weight.shape[0] % (32 * phi_devices) == 0
        and layers >= REACH
        and cells % 8 == 0
        and cells >= 16
        and width % 128 == 0
        and phi_coef.shape[0] % width == 0
        and phi_weight.shape[0] % (2 * width) == 0
        and (2 * layers * REACH) % 8 == 0
    )
    return (paired_body if fits else general_body)(*args)


def solution(mesh):
    in_specs = (
        P("phi", "row"),
        P("phi"),
        P("phi"),
        P(None, "phi"),
        P("row", None),
        P(),
        P(),
        P(),
        P("row", "phi", None),
    )
    out_specs = (P("row", "phi", None), P("row", "phi", None))
    return jax.shard_map(body, mesh=mesh, in_specs=in_specs, out_specs=out_specs, check_vma=False)
```
